32 devices in a mesh: group: 1, ctx: 8 (over z, y), exp: 4 (over x, core).
Axes of the slice: x: 2, y: 2, z: 4, core: 2. Of those that a mesh axis runs over, the one named last changes fastest.
Arguments:
- hidden: bfloat16 [1536, 2048], P(('group', 'ctx', 'exp')), may hold values from -6 to 6
- queries: bfloat16 [1536, 512], P(('group', 'ctx'), 'exp'), may hold values from -6 to 6
- keys: bfloat16 [1536, 256], P(('group', 'ctx')), may hold values from -6 to 6
- values: bfloat16 [1536, 256], P(('group', 'ctx')), may hold values from -6 to 6
- positions: int32 [1536], P(('group', 'ctx')), may hold values from 0 to 191, as said below
- out_weight: bfloat16 [512, 2048], P('exp'), may hold values from -0.25 to 0.25
- ffn_gain: float32 [2048], replicated, may hold values from 0.1 to 1.9
- router_weight: bfloat16 [2048, 16], replicated, may hold values from -0.125 to 0.125
- routes: int32 [1536, 8], P(('group', 'ctx', 'exp')), may hold values from 0 to 15, all different within a row; in each aligned block of 48 rows (0 to 47, 48 to 95, ...) at most 36 rows name the same one
- expert_in: bfloat16 [8, 4, 2048, 384], P('ctx', 'exp'), may hold values from -0.125 to 0.125
- expert_out: bfloat16 [8, 4, 192, 2048], P('ctx', 'exp'), may hold values from -0.3125 to 0.3125
- rollout_logits: float32 [1536, 16], P(('group', 'ctx', 'exp')), may hold values from -12 to 12
Outputs:
- layer_out: bfloat16 [1536, 2048], P(('group', 'ctx', 'exp'))
- router_kl: float32 [1536], P(('group', 'ctx', 'exp'))
The draws below stay inside these ranges and needn't reach their ends.
Inputs may be any that keep to these rules, and one draw needn't show every extreme that they name: `positions`: documents are runs of consecutive tokens, each of at most 192 tokens; the offset is 0 at a document's first token and rises by one to its last; at least one document has exactly 192 tokens. `routes`: each row names 8 different experts. Within the rows of one device no expert is named by more than 36 rows, a bound that some block reaches.
All inputs are finite; a program needn't handle non-finite values.
Results may differ from the reference program's by a relative error of at most 0.013.
Values may be sent and summed in bfloat16 or wider, within the bound.
No kernel may reach another device: no remote copies, remote signals or barrier semaphores. Data moves between devices by JAX's collectives and lax.ppermute only.
A program may use at most 64 MiB of HBM per device.

```python
import math
import jax
import jax.numpy as jnp
import numpy as np
from jax import lax

D = 2048
HD = 128
TOP = 8
KVH = 2
EH = 384
TOK_MOE = 48
QHEADS = 4
EXPERTS = 16
EPC = 4
CAP = 36
TOK_CTX = 192
TOKENS = 1536
N_CTX = 8
N_EXP = 4


def draw_positions(key, part):
    key = jax.random.fold_in(key, 11)
    key_lengths, key_pick = jax.random.split(key)
    lengths = jax.random.randint(key_lengths, (TOKENS,), 1, TOK_CTX + 1)
    picked = jax.random.randint(key_pick, (), 0, 3)
    counter = jnp.arange(TOKENS, dtype=jnp.int32)
    lengths = jnp.where(counter == picked, TOK_CTX, lengths).astype(jnp.int32)
    starts = jnp.cumsum(lengths) - lengths
    marks = jnp.zeros((TOKENS,), jnp.int32).at[starts].set(1, mode='drop')
    opening = lax.cummax(jnp.where(marks == 1, counter, 0), axis=0)
    return (counter - opening).astype(jnp.int32)


def steps_of(own_key, extent, pieces, least, top_value):
    loudness = 1.0
    for position, shards_of in pieces:
        draws = jax.random.uniform(jax.random.fold_in(jax.random.fold_in(own_key, 6), position), (shards_of,), jnp.float32, least / len(pieces), top_value / len(pieces))
        loudness = loudness * jnp.repeat(jnp.exp(draws), extent[position] // shards_of).reshape((-1,) + (1,) * (len(extent) - 1 - position))
    return loudness


def deal_out(own_key, own, number, rows, number_of, top, bound, slope):
    ranking = jax.random.permutation(own_key, number_of)
    heavy_load, usual = load_shares(number_of, rows * top, bound, slope, True), load_shares(number_of, rows * top, bound, slope, False)
    places = jnp.arange(number_of)

    def named(tallies, turn):
        used = int((tallies > 0).sum())
        fixed = max(1, used // 4)
        moved = fixed + (places - fixed + turn * (used - fixed)) % max(1, number_of - fixed)
        return jnp.zeros((number_of,), jnp.int32).at[ranking[jnp.where(places < fixed, places, moved)]].set(jnp.asarray(tallies, jnp.int32))

    tallies = jnp.where(number % 4 == 0, named(heavy_load, number // 4), named(usual, number - number // 4 - 1))
    mixed = jax.random.permutation(jax.random.fold_in(own, 3), number_of)
    source_of, receiver = mixed[0:number_of // 2 * 2:2], mixed[1:number_of // 2 * 2:2]
    slack = jnp.minimum(tallies[source_of] - 1, bound - tallies[receiver]) // 2
    slack = jnp.where((source_of == ranking[0]) | (receiver == ranking[0]) | (tallies[receiver] == 0), 0, jnp.maximum(slack, 0))
    moved = jax.random.randint(jax.random.fold_in(own, 4), (number_of // 2,), 0, 1 << 20) % (slack + 1)
    tallies = tallies.at[source_of].add(-moved).at[receiver].add(moved)
    labels = jnp.searchsorted(jnp.cumsum(tallies), jnp.arange(rows * top), side="right").astype(jnp.int32)
    grid = labels.reshape(top, rows).T
    grid = grid[jax.random.permutation(jax.random.fold_in(own, 1), rows)]
    turn = jax.random.randint(jax.random.fold_in(own, 2), (rows, 1), 0, top)
    return jnp.take_along_axis(grid, (jnp.arange(top)[None, :] + turn) % top, axis=1)


def load_shares(amount, total, most, lean, full):
    portions = [(1 << 20) // math.isqrt(rank ** lean) + 1 for rank in range(1, amount + 1)]
    largest = most if full else min(most, max(-(-total // amount), total * portions[0] // sum(portions)))
    least = 1 if total - largest >= amount - 1 else 0
    given, surplus = [largest] + [least] * (amount - 1), total - largest - least * (amount - 1)
    while surplus > 0:
        candidates = [i for i in range(1, amount) if given[i] < largest] or [i for i in range(1, amount) if given[i] < most]
        mass, left = sum([portions[i] for i in candidates]), surplus
        for i in candidates:
            more = min(most - given[i], max(1, left * portions[i] // mass), surplus)
            given[i] = given[i] + more
            surplus = surplus - more
    return np.array(given)


def normal_values(stream_key, extent, deviation, limit, pieces=(), kind=jnp.bfloat16):
    drawn = jax.random.normal(stream_key, extent, jnp.float32) * deviation
    if len(pieces) > 0:
        drawn = steps_of(stream_key, extent, pieces, -0.22, 0.18) * drawn
    return jnp.clip(drawn, min=-limit, max=limit).astype(kind)


def setup_inputs(seed: int = 0, part: int = 0) -> dict:
    seeds = jax.random.split(jax.random.key(seed), 13)
    own_keys = jax.random.split(jax.random.fold_in(seeds[12], part), 13)
    hidden = normal_values(own_keys[0], (TOKENS, D), 1.0, 6.0, ((0, 32),))
    queries = normal_values(own_keys[1], (TOKENS, QHEADS * HD), 1.0, 6.0, ((0, 8), (1, 4)))
    keys = normal_values(own_keys[2], (TOKENS, KVH * HD), 1.0, 6.0, ((0, 8),))
    values = normal_values(own_keys[3], (TOKENS, KVH * HD), 1.0, 6.0, ((0, 8),))
    positions = draw_positions(jax.random.fold_in(jax.random.fold_in(seeds[12], part), 71), part)
    out_weight = normal_values(seeds[5], (QHEADS * HD, D), (QHEADS * HD) ** -0.5, 0.25, ((0, 4),))
    ffn_gain = jnp.clip(1.0 + 0.18 * jax.random.normal(seeds[6], (D,), jnp.float32), 0.1, 1.9)
    router_weight = normal_values(seeds[7], (D, EXPERTS), D ** -0.5, 0.125)
    routes_keys = jax.random.split(jax.random.fold_in(own_keys[8], 1), TOKENS // TOK_MOE)
    routes_turns = jax.random.permutation(jax.random.fold_in(own_keys[8], 3), TOKENS // TOK_MOE)
    routes = jax.vmap(lambda own, number: deal_out(jax.random.fold_in(own_keys[8], 2), own, number, TOK_MOE, EXPERTS, TOP, CAP, 2))(routes_keys, routes_turns).reshape((TOKENS, TOP))
    expert_in = normal_values(seeds[9], (2 * EPC, EXPERTS // EPC, D, EH), D ** -0.5, 0.125, ((0, 8), (1, 4)))
    expert_out = normal_values(seeds[10], (2 * EPC, EXPERTS // EPC, EH // 2, D), EH ** -0.5, 0.3125, ((0, 8), (1, 4)))
    rollout_logits = normal_values(own_keys[11], (TOKENS, EXPERTS), 2.0, 12.0, ((0, 32),), jnp.float32)
    return {"hidden": hidden, "queries": queries, "keys": keys, "values": values, "positions": positions, "out_weight": out_weight, "ffn_gain": ffn_gain, "router_weight": router_weight, "routes": routes, "expert_in": expert_in, "expert_out": expert_out, "rollout_logits": rollout_logits}


eps = 1e-06
theta = 1000000.0

def frequencies(head_dim):
    return theta ** (-jnp.arange(head_dim // 2, dtype=jnp.float32) * 2.0 / head_dim)

def head_norm(values_in):
    widened = values_in.astype(jnp.float32)
    return widened / jnp.sqrt(lax.optimization_barrier(jnp.mean(widened * widened, axis=-1, keepdims=True)) + eps)

def rotate(vectors, angle):
    middle = vectors.shape[-1] // 2
    cosine = jnp.cos(angle)
    sine_part = jnp.sin(angle)
    leading = vectors[..., :middle]
    trailing = vectors[..., middle:]
    return jnp.concatenate([leading * cosine - trailing * sine_part, trailing * cosine + leading * sine_part], axis=-1)

def reference(hidden, queries, keys, values, positions, out_weight, ffn_gain, router_weight, routes, expert_in, expert_out, rollout_logits):
    spectrum = frequencies(HD)
    angle = positions.astype(jnp.float32)[:, None, None] * spectrum[None, None, :]
    query_rot = rotate(head_norm(queries.reshape(TOKENS, QHEADS, HD)), angle).astype(jnp.bfloat16)
    key_rot = rotate(head_norm(keys.reshape(TOKENS, KVH, HD)), angle).astype(jnp.bfloat16)
    value_heads = values.reshape(TOKENS, KVH, HD)
    padding = jnp.zeros((TOK_CTX, KVH, HD), jnp.bfloat16)
    key_padded = jnp.concatenate([padding, key_rot], axis=0)
    value_padded = jnp.concatenate([padding, value_heads], axis=0)
    share = QHEADS // KVH

    def one_block(index):
        start = (index * TOK_CTX).astype(jnp.int32)
        query_block = lax.dynamic_slice_in_dim(query_rot, start, TOK_CTX, 0)
        key_block = jnp.repeat(lax.dynamic_slice_in_dim(key_padded, start, 2 * TOK_CTX, 0), share, axis=1)
        value_block = jnp.repeat(lax.dynamic_slice_in_dim(value_padded, start, 2 * TOK_CTX, 0), share, axis=1)
        scores = jnp.einsum('qhd,khd->hqk', query_block.astype(jnp.float32), key_block.astype(jnp.float32)) / jnp.sqrt(jnp.float32(HD))
        query_at = start + jnp.arange(TOK_CTX, dtype=jnp.int32)
        key_at = start - TOK_CTX + jnp.arange(2 * TOK_CTX, dtype=jnp.int32)
        offsets = lax.dynamic_slice_in_dim(positions, start, TOK_CTX, 0)
        allowed = (key_at[None, :] <= query_at[:, None]) & (key_at[None, :] >= (query_at - offsets)[:, None])
        raw = jnp.where(allowed[None, :, :], jnp.exp(scores), 0.0)
        weights = (raw / lax.optimization_barrier(jnp.sum(raw, axis=2, keepdims=True))).astype(jnp.bfloat16)
        mixed = jnp.einsum('hqk,khd->qhd', weights.astype(jnp.float32), value_block.astype(jnp.float32))
        return mixed.astype(jnp.bfloat16).reshape(TOK_CTX, QHEADS * HD)
    heads_out = lax.map(one_block, jnp.arange(N_CTX, dtype=jnp.int32)).reshape(TOKENS, QHEADS * HD)

    def add_head(head, total):
        rows_in = lax.dynamic_slice_in_dim(heads_out, head * HD, HD, 1)
        weight_rows = lax.dynamic_slice_in_dim(out_weight, head * HD, HD, 0)
        term = jnp.dot(rows_in, weight_rows, preferred_element_type=jnp.float32).astype(jnp.bfloat16)
        return total + lax.optimization_barrier(term).astype(jnp.float32)
    summed = lax.fori_loop(0, QHEADS, add_head, jnp.zeros((TOKENS, D), jnp.float32))
    attended = (hidden.astype(jnp.float32) + summed).astype(jnp.bfloat16)
    widened = attended.astype(jnp.float32)
    moe_in = (widened / jnp.sqrt(lax.optimization_barrier(jnp.mean(widened * widened, axis=1, keepdims=True)) + eps) * ffn_gain[None, :]).astype(jnp.bfloat16)
    router_logits = jnp.dot(moe_in, router_weight, preferred_element_type=jnp.float32)
    current_logprob = router_logits - jnp.log(lax.optimization_barrier(jnp.sum(jnp.exp(router_logits), axis=1, keepdims=True)))
    rollout_logprob = rollout_logits - jnp.log(lax.optimization_barrier(jnp.sum(jnp.exp(rollout_logits), axis=1, keepdims=True)))
    router_kl = lax.optimization_barrier(jnp.sum(jnp.exp(rollout_logprob) * (rollout_logprob - current_logprob), axis=1))
    chosen_logits = jnp.take_along_axis(router_logits, routes, axis=1)
    gate_raw = jnp.exp(chosen_logits)
    gates = (gate_raw / lax.optimization_barrier(jnp.sum(gate_raw, axis=1, keepdims=True))).astype(jnp.bfloat16)
    flat_routes = routes.reshape(-1)
    flat_gates = gates.reshape(-1)
    reach = N_CTX * N_EXP * CAP

    def add_expert(expert, total):
        member = flat_routes == expert
        chosen = jnp.nonzero(member, size=reach, fill_value=0)[0].astype(jnp.int32)
        count = jnp.sum(member.astype(jnp.int32))
        live = jnp.arange(reach, dtype=jnp.int32) < count
        token_rows = chosen // TOP
        inputs = moe_in[token_rows]
        column = expert // EPC
        within = expert % EPC
        output = jnp.zeros((reach, D), jnp.float32)
        for side in range(2):
            act = jnp.dot(inputs, expert_in[2 * within + side, column], preferred_element_type=jnp.float32)
            inner = (jax.nn.silu(act[:, :EH // 2]) * act[:, EH // 2:]).astype(jnp.bfloat16)
            part = jnp.dot(inner, expert_out[2 * within + side, column], preferred_element_type=jnp.float32).astype(jnp.bfloat16)
            output = output + part.astype(jnp.float32)
        output = lax.optimization_barrier(output.astype(jnp.bfloat16)).astype(jnp.float32)
        weight = jnp.where(live, flat_gates[chosen].astype(jnp.float32), 0.0)
        return total.at[token_rows].add(weight[:, None] * output)
    moe_out = lax.fori_loop(0, EXPERTS, add_expert, jnp.zeros((TOKENS, D), jnp.float32))
    layer_out = (attended.astype(jnp.float32) + moe_out).astype(jnp.bfloat16)
    return (layer_out, router_kl)
```

```python
import jax
import jax.numpy as jnp
from jax import lax
from jax.sharding import PartitionSpec as P

eps = 1e-06
theta = 1000000.0


def passed_along(value, axis, steps):
    count = lax.axis_size(axis)
    initial, last = (max(0, -steps), min(count, count - steps))
    return lax.ppermute(value, axis, [(source, source + steps) for source in range(initial, last)])


def frequencies(head_dim):
    return theta ** (-jnp.arange(head_dim // 2, dtype=jnp.float32) * 2.0 / head_dim)


def head_norm(values_in):
    widened = values_in.astype(jnp.float32)
    return widened / jnp.sqrt(jnp.mean(widened * widened, axis=-1, keepdims=True) + eps)


def rotate(vectors, angle):
    middle = vectors.shape[-1] // 2
    cosine = jnp.cos(angle)
    sine_part = jnp.sin(angle)
    leading = vectors[..., :middle]
    trailing = vectors[..., middle:]
    return jnp.concatenate(
        [leading * cosine - trailing * sine_part, trailing * cosine + leading * sine_part], axis=-1
    )


def activate(act):
    inner = act.shape[1] // 2
    return (jax.nn.silu(act[:, :inner]) * act[:, inner:]).astype(jnp.bfloat16)


def sparse_body(
    hidden,
    queries,
    keys,
    values,
    positions,
    out_weight,
    ffn_gain,
    router_weight,
    routes,
    expert_in,
    expert_out,
    rollout_logits,
):
    block_rows = queries.shape[0]
    head_dim = queries.shape[1]
    width = hidden.shape[1]
    token_rows = hidden.shape[0]
    top_count = routes.shape[1]
    experts_total = router_weight.shape[1]
    ctx_index = lax.axis_index("ctx")
    exp_index = lax.axis_index("exp")
    ctx_count = lax.axis_size("ctx")
    exp_count = lax.axis_size("exp")
    kv_heads = keys.shape[1] // head_dim
    kv_group = exp_index // (exp_count // kv_heads)
    angle = positions.astype(jnp.float32)[:, None] * frequencies(head_dim)[None, :]
    query_rot = rotate(head_norm(queries), angle).astype(jnp.bfloat16)
    key_own = rotate(
        head_norm(lax.dynamic_slice_in_dim(keys, kv_group * head_dim, head_dim, 1)), angle
    ).astype(jnp.bfloat16)
    value_own = lax.dynamic_slice_in_dim(values, kv_group * head_dim, head_dim, 1)
    key_before, value_before = passed_along((key_own, value_own), "ctx", 1)
    key_window = jnp.concatenate([key_before, key_own], axis=0)
    value_window = jnp.concatenate([value_before, value_own], axis=0)
    scores = lax.dot_general(
        query_rot, key_window, (((1,), (1,)), ((), ())), preferred_element_type=jnp.float32
    )
    scores = scores / jnp.sqrt(jnp.float32(head_dim))
    query_at = ctx_index * block_rows + jnp.arange(block_rows, dtype=jnp.int32)
    key_at = ctx_index * block_rows - block_rows + jnp.arange(2 * block_rows, dtype=jnp.int32)
    allowed = (key_at[None, :] <= query_at[:, None]) & (
        key_at[None, :] >= (query_at - positions)[:, None]
    )
    raw = jnp.where(allowed, jnp.exp(scores), 0.0)
    weights = (raw / jnp.sum(raw, axis=1, keepdims=True)).astype(jnp.bfloat16)
    head_out = jnp.dot(weights, value_window, preferred_element_type=jnp.float32).astype(
        jnp.bfloat16
    )
    term = jnp.dot(head_out, out_weight, preferred_element_type=jnp.float32).astype(jnp.bfloat16)
    summed = lax.psum_scatter(
        lax.optimization_barrier(term).astype(jnp.float32).astype(jnp.bfloat16),
        "exp",
        scatter_dimension=0,
        tiled=True,
    ).astype(jnp.float32)
    attended = (hidden.astype(jnp.float32) + summed).astype(jnp.bfloat16)
    widened = attended.astype(jnp.float32)
    moe_in = (
        widened
        / jnp.sqrt(jnp.mean(widened * widened, axis=1, keepdims=True) + eps)
        * ffn_gain[None, :]
    ).astype(jnp.bfloat16)
    router_logits = jnp.dot(moe_in, router_weight, preferred_element_type=jnp.float32)
    current_logprob = router_logits - jnp.log(
        jnp.sum(jnp.exp(router_logits), axis=1, keepdims=True)
    )
    rollout_logprob = rollout_logits - jnp.log(
        jnp.sum(jnp.exp(rollout_logits), axis=1, keepdims=True)
    )
    router_kl = jnp.sum(jnp.exp(rollout_logprob) * (rollout_logprob - current_logprob), axis=1)
    expert_ids = jnp.arange(experts_total, dtype=jnp.int32)
    picked = routes[:, :, None] == expert_ids[None, None, :]
    chosen_logits = jnp.sum(jnp.where(picked, router_logits[:, None, :], 0.0), axis=2)
    gate_raw = jnp.exp(chosen_logits)
    gates = (gate_raw / jnp.sum(gate_raw, axis=1, keepdims=True)).astype(jnp.bfloat16)
    capacity = min(token_rows, max(2, 3 * token_rows * top_count // (2 * experts_total)))
    per_column = experts_total // exp_count
    slots_total = experts_total * capacity
    flat_routes = routes.reshape(-1)
    member = (flat_routes[:, None] == expert_ids[None, :]).astype(jnp.int32)
    earlier = jnp.cumsum(member, axis=0) - member
    slot_rank = jnp.sum(earlier * member, axis=1)
    target = (
        flat_routes % per_column * exp_count + flat_routes // per_column
    ) * capacity + slot_rank
    target_grid = target.reshape(token_rows, top_count)
    slot_ids = jnp.arange(slots_total, dtype=jnp.int32)
    placing = jnp.any(target_grid[None, :, :] == slot_ids[:, None, None], axis=2).astype(
        jnp.bfloat16
    )
    gate_grid = jnp.where(
        target_grid[:, :, None] == slot_ids[None, None, :], gates[:, :, None], jnp.bfloat16(0)
    )
    combining = jnp.sum(gate_grid.astype(jnp.float32), axis=1).astype(jnp.bfloat16)
    weight_in = expert_in[0, 0]
    weight_out = expert_out[0, 0]
    packed = jnp.dot(placing, moe_in, preferred_element_type=jnp.float32).astype(jnp.bfloat16)
    packed = packed.reshape(per_column, 1, exp_count, capacity, width)
    doubled = jnp.broadcast_to(packed, (per_column, 2, exp_count, capacity, width)).reshape(
        ctx_count, exp_count, capacity, width
    )
    arrived = lax.all_to_all(
        lax.all_to_all(doubled, "ctx", split_axis=0, concat_axis=0, tiled=True),
        "exp",
        split_axis=1,
        concat_axis=1,
        tiled=True,
    )
    act = jnp.dot(arrived.reshape(-1, width), weight_in, preferred_element_type=jnp.float32)
    partial_value = jnp.dot(activate(act), weight_out, preferred_element_type=jnp.float32).astype(
        jnp.bfloat16
    )
    returned = lax.all_to_all(
        lax.all_to_all(
            partial_value.reshape(ctx_count, exp_count, capacity, width),
            "ctx",
            split_axis=0,
            concat_axis=0,
            tiled=True,
        ),
        "exp",
        split_axis=1,
        concat_axis=1,
        tiled=True,
    )
    paired = returned.reshape(per_column, 2, exp_count * capacity, width).astype(jnp.float32)
    expert_output = (paired[:, 0] + paired[:, 1]).astype(jnp.bfloat16).reshape(slots_total, width)
    moe_out = jnp.dot(combining, expert_output, preferred_element_type=jnp.float32)
    layer_out = (attended.astype(jnp.float32) + moe_out).astype(jnp.bfloat16)
    return (layer_out, router_kl)


def swapped(value, axis, mask):
    count = lax.axis_size(axis)
    return lax.ppermute(value, axis, [(source, source ^ mask) for source in range(count)])


def dense_body(
    hidden,
    queries,
    keys,
    values,
    positions,
    out_weight,
    ffn_gain,
    router_weight,
    routes,
    expert_in,
    expert_out,
    rollout_logits,
):
    block_rows = queries.shape[0]
    head_dim = queries.shape[1]
    width = hidden.shape[1]
    token_rows = hidden.shape[0]
    experts_total = router_weight.shape[1]
    ctx_index = lax.axis_index("ctx")
    exp_index = lax.axis_index("exp")
    exp_count = lax.axis_size("exp")
    kv_heads = keys.shape[1] // head_dim
    per_column = experts_total // exp_count
    share = exp_count // kv_heads
    bits = []
    step = exp_count // 2
    while step:
        bits.append(step)
        step //= 2

    weight_in = expert_in[0, 0]
    weight_out = expert_out[0, 0]
    kv_own = jnp.concatenate([keys, values], axis=1)
    kv_before = passed_along(kv_own, "ctx", 1)
    query_rows = lax.all_to_all(queries, "exp", split_axis=0, concat_axis=1, tiled=True)
    other_in = swapped(weight_in, "ctx", 1)
    other_out = swapped(weight_out, "ctx", 1)
    out_rows = out_weight
    for bit in bits:
        out_rows = jnp.concatenate([out_rows, swapped(out_rows, "exp", bit)], axis=0)
    head_order = [0]
    for bit in bits:
        head_order = head_order + [h ^ bit for h in head_order]

    row_start = exp_index * token_rows
    own_positions = lax.dynamic_slice_in_dim(positions, row_start, token_rows, 0)
    spectrum = frequencies(head_dim)
    key_positions = jnp.concatenate(
        [positions[0] - block_rows + jnp.arange(block_rows, dtype=jnp.int32), positions]
    )
    key_angle = key_positions.astype(jnp.float32)[:, None] * spectrum[None, :]
    query_angle = own_positions.astype(jnp.float32)[:, None] * spectrum[None, :]
    kv_window = jnp.concatenate([kv_before, kv_own], axis=0)
    query_at = row_start + jnp.arange(token_rows, dtype=jnp.int32)
    key_at = jnp.arange(2 * block_rows, dtype=jnp.int32) - block_rows
    allowed = (key_at[None, :] <= query_at[:, None]) & (
        key_at[None, :] >= (query_at - own_positions)[:, None]
    )
    heads = []
    key_rots = [
        rotate(head_norm(kv_window[:, g * head_dim : (g + 1) * head_dim]), key_angle).astype(jnp.bfloat16)
        for g in range(kv_heads)
    ]
    for h in range(exp_count):
        g = h // share
        query_rot = rotate(
            head_norm(query_rows[:, h * head_dim : (h + 1) * head_dim]), query_angle
        ).astype(jnp.bfloat16)
        scores = lax.dot_general(
            query_rot, key_rots[g], (((1,), (1,)), ((), ())), preferred_element_type=jnp.float32
        ) / jnp.sqrt(jnp.float32(head_dim))
        raw = jnp.where(allowed, jnp.exp(scores), 0.0)
        weights = (raw / jnp.sum(raw, axis=1, keepdims=True)).astype(jnp.bfloat16)
        value_cols = kv_window[:, (kv_heads + g) * head_dim : (kv_heads + g + 1) * head_dim]
        heads.append(
            jnp.dot(weights, value_cols, preferred_element_type=jnp.float32).astype(jnp.bfloat16)
        )
    stacked = jnp.stack(heads)
    head_out = jnp.concatenate(
        [lax.dynamic_index_in_dim(stacked, exp_index ^ h, 0, keepdims=False) for h in head_order], axis=1
    )
    summed = jnp.dot(head_out, out_rows, preferred_element_type=jnp.float32)
    attended = (hidden.astype(jnp.float32) + summed).astype(jnp.bfloat16)
    widened = attended.astype(jnp.float32)
    moe_in = (
        widened
        / jnp.sqrt(jnp.mean(widened * widened, axis=1, keepdims=True) + eps)
        * ffn_gain[None, :]
    ).astype(jnp.bfloat16)
    router_logits = jnp.dot(moe_in, router_weight, preferred_element_type=jnp.float32)
    current_logprob = router_logits - jnp.log(
        jnp.sum(jnp.exp(router_logits), axis=1, keepdims=True)
    )
    rollout_logprob = rollout_logits - jnp.log(
        jnp.sum(jnp.exp(rollout_logits), axis=1, keepdims=True)
    )
    router_kl = jnp.sum(jnp.exp(rollout_logprob) * (rollout_logprob - current_logprob), axis=1)
    expert_ids = jnp.arange(experts_total, dtype=jnp.int32)
    picked = jnp.any(routes[:, :, None] == expert_ids[None, None, :], axis=1)
    gate_raw = jnp.where(picked, jnp.exp(router_logits), 0.0)
    gates = (gate_raw / jnp.sum(gate_raw, axis=1, keepdims=True)).astype(jnp.bfloat16)
    lanes = -(-experts_total // 128) * 128
    payload = jnp.concatenate(
        [moe_in, jnp.pad(gates, ((0, 0), (0, lanes - experts_total)))], axis=1
    )

    gathered = jnp.stack([payload] + [swapped(payload, "ctx", 2 * k) for k in range(1, per_column)])
    for bit in bits:
        gathered = jnp.stack([gathered, swapped(gathered, "exp", bit)])
    flat = gathered.reshape(-1, width + lanes)
    tokens = flat[:, :width]
    gate = lax.dynamic_slice_in_dim(
        flat[:, width:], exp_index * per_column + ctx_index // 2, 1, 1
    ).astype(jnp.float32)
    inner = jnp.concatenate(
        [
            activate(jnp.dot(tokens, weight_in, preferred_element_type=jnp.float32)),
            activate(jnp.dot(tokens, other_in, preferred_element_type=jnp.float32)),
        ],
        axis=1,
    )
    partial = jnp.dot(
        inner, jnp.concatenate([weight_out, other_out], axis=0), preferred_element_type=jnp.float32
    )
    partial = (partial * gate).astype(jnp.bfloat16)
    for bit in reversed(bits):
        halves = partial.reshape(2, -1, width)
        partial = (
            halves[0].astype(jnp.float32) + swapped(halves[1], "exp", bit).astype(jnp.float32)
        ).astype(jnp.bfloat16)
    blocks = partial.reshape(per_column, token_rows, width)
    moe_out = blocks[0].astype(jnp.float32)
    for k in range(1, per_column):
        moe_out = moe_out + swapped(blocks[k], "ctx", 2 * k).astype(jnp.float32)
    layer_out = (attended.astype(jnp.float32) + moe_out).astype(jnp.bfloat16)
    return (layer_out, router_kl)


def powers_of_two(*counts):
    return all(count & (count - 1) == 0 for count in counts)


def body(*arrays):
    experts_total = arrays[7].shape[1]
    exp_count, ctx_count = lax.axis_size("exp"), lax.axis_size("ctx")
    dense = experts_total <= 2 * arrays[8].shape[1] and powers_of_two(exp_count, ctx_count)
    return (dense_body if dense else sparse_body)(*arrays)


def solution(mesh):
    return jax.shard_map(
        body,
        mesh=mesh,
        in_specs=(
            P(("group", "ctx", "exp"), None),
            P(("group", "ctx"), "exp"),
            P(("group", "ctx"), None),
            P(("group", "ctx"), None),
            P(("group", "ctx")),
            P("exp", None),
            P(),
            P(),
            P(("group", "ctx", "exp"), None),
            P("ctx", "exp", None, None),
            P("ctx", "exp", None, None),
            P(("group", "ctx", "exp"), None),
        ),
        out_specs=(P(("group", "ctx", "exp"), None), P(("group", "ctx", "exp"))),
        check_vma=False,
    )
```

```python
import functools

import jax
import jax.numpy as jnp
from jax import lax
from jax.experimental import pallas as pl
from jax.experimental.pallas import tpu as pltpu
from jax.sharding import PartitionSpec as P

eps = 1e-06
theta = 1000000.0


def passed_along(value, axis, steps):
    count = lax.axis_size(axis)
    initial, last = (max(0, -steps), min(count, count - steps))
    return lax.ppermute(value, axis, [(source, source + steps) for source in range(initial, last)])


def frequencies(head_dim):
    return theta ** (-jnp.arange(head_dim // 2, dtype=jnp.float32) * 2.0 / head_dim)


def head_norm(values_in):
    widened = values_in.astype(jnp.float32)
    return widened / jnp.sqrt(jnp.mean(widened * widened, axis=-1, keepdims=True) + eps)


def rotate(vectors, angle):
    middle = vectors.shape[-1] // 2
    cosine = jnp.cos(angle)
    sine_part = jnp.sin(angle)
    leading = vectors[..., :middle]
    trailing = vectors[..., middle:]
    return jnp.concatenate(
        [leading * cosine - trailing * sine_part, trailing * cosine + leading * sine_part], axis=-1
    )


def activate(act):
    inner = act.shape[1] // 2
    return (jax.nn.silu(act[:, :inner]) * act[:, inner:]).astype(jnp.bfloat16)


def sparse_body(
    hidden,
    queries,
    keys,
    values,
    positions,
    out_weight,
    ffn_gain,
    router_weight,
    routes,
    expert_in,
    expert_out,
    rollout_logits,
):
    block_rows = queries.shape[0]
    head_dim = queries.shape[1]
    width = hidden.shape[1]
    token_rows = hidden.shape[0]
    top_count = routes.shape[1]
    experts_total = router_weight.shape[1]
    ctx_index = lax.axis_index("ctx")
    exp_index = lax.axis_index("exp")
    ctx_count = lax.axis_size("ctx")
    exp_count = lax.axis_size("exp")
    kv_heads = keys.shape[1] // head_dim
    kv_group = exp_index // (exp_count // kv_heads)
    angle = positions.astype(jnp.float32)[:, None] * frequencies(head_dim)[None, :]
    query_rot = rotate(head_norm(queries), angle).astype(jnp.bfloat16)
    key_own = rotate(
        head_norm(lax.dynamic_slice_in_dim(keys, kv_group * head_dim, head_dim, 1)), angle
    ).astype(jnp.bfloat16)
    value_own = lax.dynamic_slice_in_dim(values, kv_group * head_dim, head_dim, 1)
    key_before, value_before = passed_along((key_own, value_own), "ctx", 1)
    key_window = jnp.concatenate([key_before, key_own], axis=0)
    value_window = jnp.concatenate([value_before, value_own], axis=0)
    scores = lax.dot_general(
        query_rot, key_window, (((1,), (1,)), ((), ())), preferred_element_type=jnp.float32
    )
    scores = scores / jnp.sqrt(jnp.float32(head_dim))
    query_at = ctx_index * block_rows + jnp.arange(block_rows, dtype=jnp.int32)
    key_at = ctx_index * block_rows - block_rows + jnp.arange(2 * block_rows, dtype=jnp.int32)
    allowed = (key_at[None, :] <= query_at[:, None]) & (
        key_at[None, :] >= (query_at - positions)[:, None]
    )
    raw = jnp.where(allowed, jnp.exp(scores), 0.0)
    weights = (raw / jnp.sum(raw, axis=1, keepdims=True)).astype(jnp.bfloat16)
    head_out = jnp.dot(weights, value_window, preferred_element_type=jnp.float32).astype(
        jnp.bfloat16
    )
    term = jnp.dot(head_out, out_weight, preferred_element_type=jnp.float32).astype(jnp.bfloat16)
    summed = lax.psum_scatter(
        lax.optimization_barrier(term).astype(jnp.float32).astype(jnp.bfloat16),
        "exp",
        scatter_dimension=0,
        tiled=True,
    ).astype(jnp.float32)
    attended = (hidden.astype(jnp.float32) + summed).astype(jnp.bfloat16)
    widened = attended.astype(jnp.float32)
    moe_in = (
        widened
        / jnp.sqrt(jnp.mean(widened * widened, axis=1, keepdims=True) + eps)
        * ffn_gain[None, :]
    ).astype(jnp.bfloat16)
    router_logits = jnp.dot(moe_in, router_weight, preferred_element_type=jnp.float32)
    current_logprob = router_logits - jnp.log(
        jnp.sum(jnp.exp(router_logits), axis=1, keepdims=True)
    )
    rollout_logprob = rollout_logits - jnp.log(
        jnp.sum(jnp.exp(rollout_logits), axis=1, keepdims=True)
    )
    router_kl = jnp.sum(jnp.exp(rollout_logprob) * (rollout_logprob - current_logprob), axis=1)
    expert_ids = jnp.arange(experts_total, dtype=jnp.int32)
    picked = routes[:, :, None] == expert_ids[None, None, :]
    chosen_logits = jnp.sum(jnp.where(picked, router_logits[:, None, :], 0.0), axis=2)
    gate_raw = jnp.exp(chosen_logits)
    gates = (gate_raw / jnp.sum(gate_raw, axis=1, keepdims=True)).astype(jnp.bfloat16)
    capacity = min(token_rows, max(2, 3 * token_rows * top_count // (2 * experts_total)))
    per_column = experts_total // exp_count
    slots_total = experts_total * capacity
    flat_routes = routes.reshape(-1)
    member = (flat_routes[:, None] == expert_ids[None, :]).astype(jnp.int32)
    earlier = jnp.cumsum(member, axis=0) - member
    slot_rank = jnp.sum(earlier * member, axis=1)
    target = (
        flat_routes % per_column * exp_count + flat_routes // per_column
    ) * capacity + slot_rank
    target_grid = target.reshape(token_rows, top_count)
    slot_ids = jnp.arange(slots_total, dtype=jnp.int32)
    placing = jnp.any(target_grid[None, :, :] == slot_ids[:, None, None], axis=2).astype(
        jnp.bfloat16
    )
    gate_grid = jnp.where(
        target_grid[:, :, None] == slot_ids[None, None, :], gates[:, :, None], jnp.bfloat16(0)
    )
    combining = jnp.sum(gate_grid.astype(jnp.float32), axis=1).astype(jnp.bfloat16)
    weight_in = expert_in[0, 0]
    weight_out = expert_out[0, 0]
    packed = jnp.dot(placing, moe_in, preferred_element_type=jnp.float32).astype(jnp.bfloat16)
    packed = packed.reshape(per_column, 1, exp_count, capacity, width)
    doubled = jnp.broadcast_to(packed, (per_column, 2, exp_count, capacity, width)).reshape(
        ctx_count, exp_count, capacity, width
    )
    arrived = lax.all_to_all(
        lax.all_to_all(doubled, "ctx", split_axis=0, concat_axis=0, tiled=True),
        "exp",
        split_axis=1,
        concat_axis=1,
        tiled=True,
    )
    act = jnp.dot(arrived.reshape(-1, width), weight_in, preferred_element_type=jnp.float32)
    partial_value = jnp.dot(activate(act), weight_out, preferred_element_type=jnp.float32).astype(
        jnp.bfloat16
    )
    returned = lax.all_to_all(
        lax.all_to_all(
            partial_value.reshape(ctx_count, exp_count, capacity, width),
            "ctx",
            split_axis=0,
            concat_axis=0,
            tiled=True,
        ),
        "exp",
        split_axis=1,
        concat_axis=1,
        tiled=True,
    )
    paired = returned.reshape(per_column, 2, exp_count * capacity, width).astype(jnp.float32)
    expert_output = (paired[:, 0] + paired[:, 1]).astype(jnp.bfloat16).reshape(slots_total, width)
    moe_out = jnp.dot(combining, expert_output, preferred_element_type=jnp.float32)
    layer_out = (attended.astype(jnp.float32) + moe_out).astype(jnp.bfloat16)
    return (layer_out, router_kl)


def swapped(value, axis, mask):
    count = lax.axis_size(axis)
    return lax.ppermute(value, axis, [(source, source ^ mask) for source in range(count)])


def expert_kernel(parts, width, index_ref, *refs):
    token_refs, refs = refs[:parts], refs[parts:]
    own_in, first, second, own_out, other_out, keep_ref, send_ref, tokens, gates = refs
    rows = token_refs[0].shape[0]
    lanes = token_refs[0].shape[1] - width
    for p, ref in enumerate(token_refs):
        tokens[p * rows : (p + 1) * rows, :] = ref[:, :width]
        picked = lax.broadcasted_iota(jnp.int32, (rows, lanes), 1) == index_ref[0]
        gates[p * rows : (p + 1) * rows, :] = jnp.sum(
            jnp.where(picked, ref[:, width:].astype(jnp.float32), 0.0), axis=1, keepdims=True
        )
    depth = width // 2
    own = jnp.dot(tokens[...], own_in[...], preferred_element_type=jnp.float32)
    other = jnp.dot(tokens[:, :depth], first[...], preferred_element_type=jnp.float32) + jnp.dot(
        tokens[:, depth:], second[...], preferred_element_type=jnp.float32
    )
    out = jnp.dot(activate(own), own_out[...], preferred_element_type=jnp.float32) + jnp.dot(
        activate(other), other_out[...], preferred_element_type=jnp.float32
    )
    out = (out * gates[...]).astype(jnp.bfloat16)
    half = keep_ref.shape[0]
    keep_ref[...] = out[:half]
    send_ref[...] = out[half:]


def expert_block(index, tokens, own_in, own_out, other_in, other_out, width):
    parts = len(tokens)
    rows = parts * tokens[0].shape[0]
    half = jax.ShapeDtypeStruct((rows // 2, width), jnp.bfloat16)
    vmem = pl.BlockSpec(memory_space=pltpu.VMEM)
    return pl.pallas_call(
        functools.partial(expert_kernel, parts, width),
        out_shape=(half, half),
        in_specs=[pl.BlockSpec(memory_space=pltpu.SMEM)] + [vmem] * (parts + 5),
        out_specs=(vmem, vmem),
        scratch_shapes=[
            pltpu.VMEM((rows, width), jnp.bfloat16),
            pltpu.VMEM((rows, 1), jnp.float32),
        ],
        compiler_params=pltpu.CompilerParams(vmem_limit_bytes=40 * 1024 * 1024),
        cost_estimate=pl.CostEstimate(
            flops=2 * rows * 3 * width * own_in.shape[1], bytes_accessed=8 << 20, transcendentals=0
        ),
    )(index, *tokens, own_in, other_in[0], other_in[1], own_out, other_out)


def dense_body(
    hidden,
    queries,
    keys,
    values,
    positions,
    out_weight,
    ffn_gain,
    router_weight,
    routes,
    expert_in,
    expert_out,
    rollout_logits,
):
    block_rows = queries.shape[0]
    head_dim = queries.shape[1]
    width = hidden.shape[1]
    token_rows = hidden.shape[0]
    experts_total = router_weight.shape[1]
    ctx_index = lax.axis_index("ctx")
    exp_index = lax.axis_index("exp")
    exp_count = lax.axis_size("exp")
    kv_heads = keys.shape[1] // head_dim
    per_column = experts_total // exp_count
    share = exp_count // kv_heads
    bits = []
    step = exp_count // 2
    while step:
        bits.append(step)
        step //= 2

    weight_in = expert_in[0, 0]
    weight_out = expert_out[0, 0]
    kv_own = jnp.concatenate([keys, values], axis=1)
    kv_before = passed_along(kv_own, "ctx", 1)
    query_rows = lax.all_to_all(queries, "exp", split_axis=0, concat_axis=1, tiled=True)
    out_rows = out_weight
    for bit in bits:
        out_rows = jnp.concatenate([out_rows, swapped(out_rows, "exp", bit)], axis=0)
    head_order = [0]
    for bit in bits:
        head_order = head_order + [h ^ bit for h in head_order]

    row_start = exp_index * token_rows
    own_positions = lax.dynamic_slice_in_dim(positions, row_start, token_rows, 0)
    spectrum = frequencies(head_dim)
    key_positions = jnp.concatenate(
        [positions[0] - block_rows + jnp.arange(block_rows, dtype=jnp.int32), positions]
    )
    key_angle = key_positions.astype(jnp.float32)[:, None] * spectrum[None, :]
    query_angle = own_positions.astype(jnp.float32)[:, None] * spectrum[None, :]
    kv_window = jnp.concatenate([kv_before, kv_own], axis=0)
    query_at = row_start + jnp.arange(token_rows, dtype=jnp.int32)
    key_at = jnp.arange(2 * block_rows, dtype=jnp.int32) - block_rows
    allowed = (key_at[None, :] <= query_at[:, None]) & (
        key_at[None, :] >= (query_at - own_positions)[:, None]
    )
    heads = []
    key_rots = [
        rotate(head_norm(kv_window[:, g * head_dim : (g + 1) * head_dim]), key_angle).astype(jnp.bfloat16)
        for g in range(kv_heads)
    ]
    for h in range(exp_count):
        g = h // share
        query_rot = rotate(
            head_norm(query_rows[:, h * head_dim : (h + 1) * head_dim]), query_angle
        ).astype(jnp.bfloat16)
        scores = lax.dot_general(
            query_rot, key_rots[g], (((1,), (1,)), ((), ())), preferred_element_type=jnp.float32
        ) / jnp.sqrt(jnp.float32(head_dim))
        raw = jnp.where(allowed, jnp.exp(scores), 0.0)
        weights = (raw / jnp.sum(raw, axis=1, keepdims=True)).astype(jnp.bfloat16)
        value_cols = kv_window[:, (kv_heads + g) * head_dim : (kv_heads + g + 1) * head_dim]
        heads.append(
            jnp.dot(weights, value_cols, preferred_element_type=jnp.float32).astype(jnp.bfloat16)
        )
    stacked = jnp.stack(heads)
    head_out = jnp.concatenate(
        [lax.dynamic_index_in_dim(stacked, exp_index ^ h, 0, keepdims=False) for h in head_order], axis=1
    )
    summed = jnp.dot(head_out, out_rows, preferred_element_type=jnp.float32)
    attended = (hidden.astype(jnp.float32) + summed).astype(jnp.bfloat16)
    widened = attended.astype(jnp.float32)
    moe_in = (
        widened
        / jnp.sqrt(jnp.mean(widened * widened, axis=1, keepdims=True) + eps)
        * ffn_gain[None, :]
    ).astype(jnp.bfloat16)
    router_logits = jnp.dot(moe_in, router_weight, preferred_element_type=jnp.float32)
    current_logprob = router_logits - jnp.log(
        jnp.sum(jnp.exp(router_logits), axis=1, keepdims=True)
    )
    rollout_logprob = rollout_logits - jnp.log(
        jnp.sum(jnp.exp(rollout_logits), axis=1, keepdims=True)
    )
    router_kl = jnp.sum(jnp.exp(rollout_logprob) * (rollout_logprob - current_logprob), axis=1)
    expert_ids = jnp.arange(experts_total, dtype=jnp.int32)
    picked = jnp.any(routes[:, :, None] == expert_ids[None, None, :], axis=1)
    gate_raw = jnp.where(picked, jnp.exp(router_logits), 0.0)
    gates = (gate_raw / jnp.sum(gate_raw, axis=1, keepdims=True)).astype(jnp.bfloat16)
    lanes = -(-experts_total // 128) * 128
    payload = jnp.concatenate(
        [moe_in, jnp.pad(gates, ((0, 0), (0, lanes - experts_total)))], axis=1
    )

    first, second = weight_in[: width // 2], weight_in[width // 2 :]
    other_first = swapped(first, "ctx", 1)
    payload, other_first, second = lax.optimization_barrier((payload, other_first, second))
    other_second = swapped(second, "ctx", 1)
    blocks = [payload] + [swapped(payload, "ctx", 2 * k) for k in range(1, per_column)]
    gathered = []
    for k, block in enumerate(blocks):
        parts = [block]
        for bit in bits:
            parts = parts + [swapped(part, "exp", bit) for part in parts]
        gathered.append(parts)
    expert_index = (exp_index * per_column + ctx_index // 2).reshape(1).astype(jnp.int32)
    other_second, weight_out_late = lax.optimization_barrier((other_second, weight_out))
    other_out = swapped(weight_out_late, "ctx", 1)
    returned = {}
    for k in sorted(range(per_column), key=lambda k: -min(k, 2.5)):
        keep, send = expert_block(
            expert_index, gathered[k], weight_in, weight_out, (other_first, other_second), other_out, width
        )
        for bit in reversed(bits):
            total = keep.astype(jnp.float32) + swapped(send, "exp", bit).astype(jnp.float32)
            total = total.astype(jnp.bfloat16)
            half = total.shape[0] // 2
            keep, send = total[:half], total[half:]
        returned[k] = total if k == 0 else swapped(total, "ctx", 2 * k)
    moe_out = sum(returned[k].astype(jnp.float32) for k in range(per_column))
    layer_out = (attended.astype(jnp.float32) + moe_out).astype(jnp.bfloat16)
    return (layer_out, router_kl)


def powers_of_two(*counts):
    return all(count & (count - 1) == 0 for count in counts)


def body(*arrays):
    experts_total = arrays[7].shape[1]
    exp_count, ctx_count = lax.axis_size("exp"), lax.axis_size("ctx")
    dense = experts_total <= 2 * arrays[8].shape[1] and powers_of_two(exp_count, ctx_count)
    return (dense_body if dense else sparse_body)(*arrays)


def solution(mesh):
    return jax.shard_map(
        body,
        mesh=mesh,
        in_specs=(
            P(("group", "ctx", "exp"), None),
            P(("group", "ctx"), "exp"),
            P(("group", "ctx"), None),
            P(("group", "ctx"), None),
            P(("group", "ctx")),
            P("exp", None),
            P(),
            P(),
            P(("group", "ctx", "exp"), None),
            P("ctx", "exp", None, None),
            P("ctx", "exp", None, None),
            P(("group", "ctx", "exp"), None),
        ),
        out_specs=(P(("group", "ctx", "exp"), None), P(("group", "ctx", "exp"))),
        check_vma=False,
    )
```

```python
import functools
import math

import jax
import jax.numpy as jnp
import numpy as np
from jax import lax
from jax.experimental import pallas as pl
from jax.experimental.pallas import tpu as pltpu
from jax.sharding import PartitionSpec as P

eps = 1e-06
theta = 1000000.0


def passed_along(value, axis, steps):
    count = lax.axis_size(axis)
    initial, last = (max(0, -steps), min(count, count - steps))
    return lax.ppermute(value, axis, [(source, source + steps) for source in range(initial, last)])


def frequencies(head_dim):
    return theta ** (-jnp.arange(head_dim // 2, dtype=jnp.float32) * 2.0 / head_dim)


def head_norm(values_in):
    widened = values_in.astype(jnp.float32)
    return widened / jnp.sqrt(jnp.mean(widened * widened, axis=-1, keepdims=True) + eps)


def rotate(vectors, angle):
    middle = vectors.shape[-1] // 2
    cosine = jnp.cos(angle)
    sine_part = jnp.sin(angle)
    leading = vectors[..., :middle]
    trailing = vectors[..., middle:]
    return jnp.concatenate(
        [leading * cosine - trailing * sine_part, trailing * cosine + leading * sine_part], axis=-1
    )


def activate(act):
    inner = act.shape[1] // 2
    return (jax.nn.silu(act[:, :inner]) * act[:, inner:]).astype(jnp.bfloat16)


def sparse_body(
    hidden,
    queries,
    keys,
    values,
    positions,
    out_weight,
    ffn_gain,
    router_weight,
    routes,
    expert_in,
    expert_out,
    rollout_logits,
):
    block_rows = queries.shape[0]
    head_dim = queries.shape[1]
    width = hidden.shape[1]
    token_rows = hidden.shape[0]
    top_count = routes.shape[1]
    experts_total = router_weight.shape[1]
    ctx_index = lax.axis_index("ctx")
    exp_index = lax.axis_index("exp")
    ctx_count = lax.axis_size("ctx")
    exp_count = lax.axis_size("exp")
    kv_heads = keys.shape[1] // head_dim
    kv_group = exp_index // (exp_count // kv_heads)
    angle = positions.astype(jnp.float32)[:, None] * frequencies(head_dim)[None, :]
    query_rot = rotate(head_norm(queries), angle).astype(jnp.bfloat16)
    key_own = rotate(
        head_norm(lax.dynamic_slice_in_dim(keys, kv_group * head_dim, head_dim, 1)), angle
    ).astype(jnp.bfloat16)
    value_own = lax.dynamic_slice_in_dim(values, kv_group * head_dim, head_dim, 1)
    key_before, value_before = passed_along((key_own, value_own), "ctx", 1)
    key_window = jnp.concatenate([key_before, key_own], axis=0)
    value_window = jnp.concatenate([value_before, value_own], axis=0)
    scores = lax.dot_general(
        query_rot, key_window, (((1,), (1,)), ((), ())), preferred_element_type=jnp.float32
    )
    scores = scores / jnp.sqrt(jnp.float32(head_dim))
    query_at = ctx_index * block_rows + jnp.arange(block_rows, dtype=jnp.int32)
    key_at = ctx_index * block_rows - block_rows + jnp.arange(2 * block_rows, dtype=jnp.int32)
    allowed = (key_at[None, :] <= query_at[:, None]) & (
        key_at[None, :] >= (query_at - positions)[:, None]
    )
    raw = jnp.where(allowed, jnp.exp(scores), 0.0)
    weights = (raw / jnp.sum(raw, axis=1, keepdims=True)).astype(jnp.bfloat16)
    head_out = jnp.dot(weights, value_window, preferred_element_type=jnp.float32).astype(
        jnp.bfloat16
    )
    term = jnp.dot(head_out, out_weight, preferred_element_type=jnp.float32).astype(jnp.bfloat16)
    summed = lax.psum_scatter(
        lax.optimization_barrier(term).astype(jnp.float32).astype(jnp.bfloat16),
        "exp",
        scatter_dimension=0,
        tiled=True,
    ).astype(jnp.float32)
    attended = (hidden.astype(jnp.float32) + summed).astype(jnp.bfloat16)
    widened = attended.astype(jnp.float32)
    moe_in = (
        widened
        / jnp.sqrt(jnp.mean(widened * widened, axis=1, keepdims=True) + eps)
        * ffn_gain[None, :]
    ).astype(jnp.bfloat16)
    router_logits = jnp.dot(moe_in, router_weight, preferred_element_type=jnp.float32)
    current_logprob = router_logits - jnp.log(
        jnp.sum(jnp.exp(router_logits), axis=1, keepdims=True)
    )
    rollout_logprob = rollout_logits - jnp.log(
        jnp.sum(jnp.exp(rollout_logits), axis=1, keepdims=True)
    )
    router_kl = jnp.sum(jnp.exp(rollout_logprob) * (rollout_logprob - current_logprob), axis=1)
    expert_ids = jnp.arange(experts_total, dtype=jnp.int32)
    picked = routes[:, :, None] == expert_ids[None, None, :]
    chosen_logits = jnp.sum(jnp.where(picked, router_logits[:, None, :], 0.0), axis=2)
    gate_raw = jnp.exp(chosen_logits)
    gates = (gate_raw / jnp.sum(gate_raw, axis=1, keepdims=True)).astype(jnp.bfloat16)
    capacity = min(token_rows, max(2, 3 * token_rows * top_count // (2 * experts_total)))
    per_column = experts_total // exp_count
    slots_total = experts_total * capacity
    flat_routes = routes.reshape(-1)
    member = (flat_routes[:, None] == expert_ids[None, :]).astype(jnp.int32)
    earlier = jnp.cumsum(member, axis=0) - member
    slot_rank = jnp.sum(earlier * member, axis=1)
    target = (
        flat_routes % per_column * exp_count + flat_routes // per_column
    ) * capacity + slot_rank
    target_grid = target.reshape(token_rows, top_count)
    slot_ids = jnp.arange(slots_total, dtype=jnp.int32)
    placing = jnp.any(target_grid[None, :, :] == slot_ids[:, None, None], axis=2).astype(
        jnp.bfloat16
    )
    gate_grid = jnp.where(
        target_grid[:, :, None] == slot_ids[None, None, :], gates[:, :, None], jnp.bfloat16(0)
    )
    combining = jnp.sum(gate_grid.astype(jnp.float32), axis=1).astype(jnp.bfloat16)
    weight_in = expert_in[0, 0]
    weight_out = expert_out[0, 0]
    packed = jnp.dot(placing, moe_in, preferred_element_type=jnp.float32).astype(jnp.bfloat16)
    packed = packed.reshape(per_column, 1, exp_count, capacity, width)
    doubled = jnp.broadcast_to(packed, (per_column, 2, exp_count, capacity, width)).reshape(
        ctx_count, exp_count, capacity, width
    )
    arrived = lax.all_to_all(
        lax.all_to_all(doubled, "ctx", split_axis=0, concat_axis=0, tiled=True),
        "exp",
        split_axis=1,
        concat_axis=1,
        tiled=True,
    )
    act = jnp.dot(arrived.reshape(-1, width), weight_in, preferred_element_type=jnp.float32)
    partial_value = jnp.dot(activate(act), weight_out, preferred_element_type=jnp.float32).astype(
        jnp.bfloat16
    )
    returned = lax.all_to_all(
        lax.all_to_all(
            partial_value.reshape(ctx_count, exp_count, capacity, width),
            "ctx",
            split_axis=0,
            concat_axis=0,
            tiled=True,
        ),
        "exp",
        split_axis=1,
        concat_axis=1,
        tiled=True,
    )
    paired = returned.reshape(per_column, 2, exp_count * capacity, width).astype(jnp.float32)
    expert_output = (paired[:, 0] + paired[:, 1]).astype(jnp.bfloat16).reshape(slots_total, width)
    moe_out = jnp.dot(combining, expert_output, preferred_element_type=jnp.float32)
    layer_out = (attended.astype(jnp.float32) + moe_out).astype(jnp.bfloat16)
    return (layer_out, router_kl)


def swapped(value, axis, mask):
    count = lax.axis_size(axis)
    return lax.ppermute(value, axis, [(source, source ^ mask) for source in range(count)])


def attention_kernel(share, index_ref, spectrum_ref, pos_ref, q_ref, *refs):
    before_ref, own_k, own_v, out_ref, cos_ref, sin_ref, pos_col = refs
    heads, rows, size = out_ref.shape
    block = own_k.shape[0]
    start = pl.multiple_of(index_ref[0] * rows, 16)
    pos_row = pos_ref[...].astype(jnp.float32)
    along = lax.broadcasted_iota(jnp.int32, (block, block), 0)
    across = lax.broadcasted_iota(jnp.int32, (block, block), 1)
    pos_col[...] = jnp.sum(jnp.where(along == across, pos_row, 0.0), axis=1, keepdims=True)
    opening = jnp.sum(jnp.where(across[:1] == 0, pos_row, 0.0), axis=1, keepdims=True)
    earlier = opening - block + along[:, :1].astype(jnp.float32)
    lane = lax.broadcasted_iota(jnp.int32, (1, size), 1)
    lower = lane < size // 2
    phase = jnp.where(lower, 0.0, math.pi / 2)
    for half, at in enumerate((earlier, pos_col[...])):
        turn = jnp.cos(at * spectrum_ref[...] - phase)
        swap = pltpu.roll(turn, size // 2, 1)
        cos_ref[half * block : (half + 1) * block, :] = jnp.where(lower, turn, swap)
        sin_ref[half * block : (half + 1) * block, :] = jnp.where(lower, -swap, turn)

    def turned(vectors, cosine, sine):
        wide = vectors.astype(jnp.float32)
        wide = wide * lax.rsqrt(jnp.mean(wide * wide, axis=1, keepdims=True) + eps)
        return (wide * cosine + pltpu.roll(wide, size // 2, 1) * sine).astype(jnp.bfloat16)

    own = pl.ds(block + start, rows)
    query_at = start + lax.broadcasted_iota(jnp.int32, (rows, 2 * block), 0)
    key_at = lax.broadcasted_iota(jnp.int32, (rows, 2 * block), 1) - block
    reach = pos_col[pl.ds(start, rows), :].astype(jnp.int32)
    allowed = (key_at <= query_at) & (key_at >= query_at - reach)
    for group in range(heads // share):
        columns = slice(group * size, (group + 1) * size)
        keys = jnp.concatenate(
            [
                turned(before_ref[:, columns], cos_ref[:block, :], sin_ref[:block, :]),
                turned(own_k[:, columns], cos_ref[block:, :], sin_ref[block:, :]),
            ],
            axis=0,
        )
        values = jnp.concatenate([before_ref[:, own_k.shape[1] + group * size :][:, :size], own_v[:, columns]], axis=0)
        for h in range(group * share, (group + 1) * share):
            query = turned(q_ref[:, h * size : (h + 1) * size], cos_ref[own, :], sin_ref[own, :])
            scores = lax.dot_general(
                query, keys, (((1,), (1,)), ((), ())), preferred_element_type=jnp.float32
            ) * (1.0 / math.sqrt(size))
            raw = jnp.where(allowed, jnp.exp(scores), 0.0)
            weights = (raw / jnp.sum(raw, axis=1, keepdims=True)).astype(jnp.bfloat16)
            out_ref[h] = jnp.dot(weights, values, preferred_element_type=jnp.float32).astype(
                jnp.bfloat16
            )


def router_kernel(order, index_ref, heads_ref, *refs):
    parts, refs = refs[: len(order)], refs[len(order) :]
    hidden_ref, gain_ref, router_ref, routes_ref, rollout_ref, attended_ref, payload_ref, kl_ref = refs
    width = hidden_ref.shape[1]
    experts, rows = rollout_ref.shape
    total = hidden_ref[...].astype(jnp.float32)
    for part, h in zip(parts, order):
        total = total + jnp.dot(
            heads_ref[index_ref[0] ^ h], part[...], preferred_element_type=jnp.float32
        )
    attended = total.astype(jnp.bfloat16)
    attended_ref[...] = attended
    wide = attended.astype(jnp.float32)
    moe_in = (
        wide * lax.rsqrt(jnp.mean(wide * wide, axis=1, keepdims=True) + eps) * gain_ref[...]
    ).astype(jnp.bfloat16)
    payload_ref[:, :width] = moe_in
    logits = lax.dot_general(
        router_ref[...], moe_in, (((1,), (1,)), ((), ())), preferred_element_type=jnp.float32
    )
    raised = jnp.exp(logits)
    rollout = rollout_ref[...]
    current_log = logits - jnp.log(jnp.sum(raised, axis=0, keepdims=True))
    rollout_log = rollout - jnp.log(jnp.sum(jnp.exp(rollout), axis=0, keepdims=True))
    kl_ref[...] = jnp.sum(jnp.exp(rollout_log) * (rollout_log - current_log), axis=0, keepdims=True)
    ids = lax.broadcasted_iota(jnp.int32, (experts, rows), 0)
    picked = jnp.zeros((experts, rows), jnp.float32)
    for k in range(routes_ref.shape[0]):
        picked = picked + jnp.where(routes_ref[k : k + 1, :] == ids, 1.0, 0.0)
    chosen = jnp.where(picked > 0.0, raised, 0.0)
    gates = (chosen / jnp.sum(chosen, axis=0, keepdims=True)).astype(jnp.bfloat16)
    lanes = payload_ref.shape[1] - width
    spread = (
        lax.broadcasted_iota(jnp.int32, (experts, lanes), 0)
        == lax.broadcasted_iota(jnp.int32, (experts, lanes), 1)
    ).astype(jnp.float32).astype(jnp.bfloat16)
    payload_ref[:, width:] = lax.dot_general(
        gates, spread, (((0,), (0,)), ((), ())), preferred_element_type=jnp.float32
    ).astype(jnp.bfloat16)


VMEM = pl.BlockSpec(memory_space=pltpu.VMEM)
SMEM = pl.BlockSpec(memory_space=pltpu.SMEM)


HBM = pl.BlockSpec(memory_space=pltpu.HBM)


def fetching(kernel, count, stored, index_ref, *refs):
    inputs, refs = refs[:count], refs[count:]
    outputs, refs = refs[: len(stored)], refs[len(stored) :]
    held, refs = refs[:count], refs[count:]
    sent, refs = refs[: sum(stored)], refs[sum(stored) :]
    arrived, left, scratch = refs[0], refs[1], refs[2:]
    copies = [
        pltpu.make_async_copy(source, target, arrived.at[i])
        for i, (source, target) in enumerate(zip(inputs, held))
    ]
    for copy in copies:
        copy.start()
    for copy in copies:
        copy.wait()
    sent = iter(sent)
    built, copies = [], []
    for output, far in zip(outputs, stored):
        built.append(next(sent) if far else output)
        if far:
            copies.append(pltpu.make_async_copy(built[-1], output, left.at[len(copies)]))
    kernel(index_ref, *held, *built, *scratch)
    for copy in copies:
        copy.start()
    for copy in copies:
        copy.wait()


def small_kernel(kernel, out_shape, inputs, stored, scratch=(), flops=0):
    held = [pltpu.VMEM(array.shape, array.dtype) for array in inputs[1:]]
    sent = [pltpu.VMEM(leaf.shape, leaf.dtype) for leaf, far in zip(out_shape, stored) if far]
    return pl.pallas_call(
        functools.partial(fetching, kernel, len(held), stored),
        out_shape=out_shape,
        in_specs=[SMEM] + [HBM] * len(held),
        out_specs=tuple(HBM if far else VMEM for far in stored),
        scratch_shapes=[
            *held,
            *sent,
            pltpu.SemaphoreType.DMA((len(held),)),
            pltpu.SemaphoreType.DMA((max(1, len(sent)),)),
            *scratch,
        ],
        compiler_params=pltpu.CompilerParams(vmem_limit_bytes=16 * 1024 * 1024),
        cost_estimate=pl.CostEstimate(flops=flops, bytes_accessed=1 << 20, transcendentals=0),
    )(*inputs)


def expert_kernel(parts, width, index_ref, *refs):
    token_refs, refs = refs[:parts], refs[parts:]
    own_in, other_in, own_out, other_out, keep_ref, send_ref, tokens, arrived = refs
    rows = token_refs[0].shape[0]
    lanes = token_refs[0].shape[1] - width
    copies = [
        pltpu.make_async_copy(ref, tokens.at[pl.ds(p * rows, rows), :], arrived.at[p])
        for p, ref in enumerate(token_refs)
    ]
    for copy in copies:
        copy.start()
    for copy in copies:
        copy.wait()
    picked = lax.broadcasted_iota(jnp.int32, (parts * rows, lanes), 1) == index_ref[0]
    gate = jnp.sum(
        jnp.where(picked, tokens[:, width:].astype(jnp.float32), 0.0), axis=1, keepdims=True
    )
    own = jnp.dot(tokens[:, :width], own_in[...], preferred_element_type=jnp.float32)
    other = jnp.dot(tokens[:, :width], other_in[...], preferred_element_type=jnp.float32)
    out = jnp.dot(activate(own), own_out[...], preferred_element_type=jnp.float32) + jnp.dot(
        activate(other), other_out[...], preferred_element_type=jnp.float32
    )
    out = (out * gate).astype(jnp.bfloat16)
    half = keep_ref.shape[0]
    keep_ref[...] = out[:half]
    send_ref[...] = out[half:]


def expert_block(index, tokens, own_in, own_out, other_in, other_out, width):
    parts = len(tokens)
    rows = parts * tokens[0].shape[0]
    half = jax.ShapeDtypeStruct((rows // 2, width), jnp.bfloat16)
    return pl.pallas_call(
        functools.partial(expert_kernel, parts, width),
        out_shape=(half, half),
        in_specs=[SMEM] + [HBM] * parts + [VMEM] * 4,
        out_specs=(VMEM, VMEM),
        scratch_shapes=[
            pltpu.VMEM((rows, tokens[0].shape[1]), jnp.bfloat16),
            pltpu.SemaphoreType.DMA((parts,)),
        ],
        compiler_params=pltpu.CompilerParams(vmem_limit_bytes=16 * 1024 * 1024),
        cost_estimate=pl.CostEstimate(
            flops=2 * rows * 3 * width * own_in.shape[1], bytes_accessed=8 << 20, transcendentals=0
        ),
    )(index, *tokens, own_in, other_in, own_out, other_out)


def dense_body(
    hidden,
    queries,
    keys,
    values,
    positions,
    out_weight,
    ffn_gain,
    router_weight,
    routes,
    expert_in,
    expert_out,
    rollout_logits,
):
    block_rows = queries.shape[0]
    head_dim = queries.shape[1]
    width = hidden.shape[1]
    token_rows = hidden.shape[0]
    experts_total = router_weight.shape[1]
    ctx_index = lax.axis_index("ctx")
    exp_index = lax.axis_index("exp")
    exp_count = lax.axis_size("exp")
    kv_heads = keys.shape[1] // head_dim
    per_column = experts_total // exp_count
    share = exp_count // kv_heads
    bits = []
    step = exp_count // 2
    while step:
        bits.append(step)
        step //= 2

    weight_in = expert_in[0, 0]
    weight_out = expert_out[0, 0]
    before = passed_along(jnp.concatenate([keys, values], axis=1), "ctx", 1)
    query_rows = lax.all_to_all(queries, "exp", split_axis=0, concat_axis=1, tiled=True)
    before, weight_in, weight_out = lax.optimization_barrier((before, weight_in, weight_out))
    other_out = swapped(weight_out, "ctx", 1)
    other_in = swapped(weight_in, "ctx", 1)

    index = exp_index.reshape(1).astype(jnp.int32)
    spectrum = np.float32(theta) ** (-np.arange(head_dim // 2, dtype=np.float32) * 2.0 / head_dim)
    spectrum = jnp.asarray(np.concatenate([spectrum, spectrum])[None, :].astype(np.float32))
    table = pltpu.VMEM((2 * block_rows, head_dim), jnp.float32)
    (head_out,) = small_kernel(
        functools.partial(attention_kernel, exp_count // kv_heads),
        (jax.ShapeDtypeStruct((exp_count, token_rows, head_dim), jnp.bfloat16),),
        (index, spectrum, positions[None, :], query_rows, before, keys, values),
        (True,),
        (table, table, pltpu.VMEM((block_rows, 1), jnp.float32)),
        8 * block_rows * token_rows * queries.shape[1],
    )
    out_parts, head_order = [out_weight], [0]
    for bit in bits[:-1]:
        out_parts = out_parts + [swapped(part, "exp", bit) for part in out_parts]
        head_order = head_order + [h ^ bit for h in head_order]
    head_out, *late = lax.optimization_barrier((head_out, *out_parts[1:]))
    out_parts = out_parts[:1] + late
    out_parts = out_parts + [swapped(part, "exp", bits[-1]) for part in out_parts]
    head_order = head_order + [h ^ bits[-1] for h in head_order]
    lanes = -(-experts_total // 128) * 128
    attended, payload, router_kl = small_kernel(
        functools.partial(router_kernel, tuple(head_order)),
        (
            jax.ShapeDtypeStruct((token_rows, width), jnp.bfloat16),
            jax.ShapeDtypeStruct((token_rows, width + lanes), jnp.bfloat16),
            jax.ShapeDtypeStruct((1, token_rows), jnp.float32),
        ),
        (index, head_out, *out_parts, hidden, ffn_gain[None, :], router_weight.T, routes.T, rollout_logits.T),
        (False, True, False),
        (),
        2 * token_rows * width * out_weight.shape[0] * exp_count,
    )
    router_kl = router_kl[0]
    blocks = [payload] + [swapped(payload, "ctx", 2 * k) for k in range(1, per_column)]
    gathered, passed = [], None
    for block in blocks:
        parts = [block]
        for bit in bits:
            if passed is not None and bit != bits[-1]:
                passed, *parts = lax.optimization_barrier((passed, *parts))
                gathered[-1][1] = passed
            parts = parts + [swapped(part, "exp", bit) for part in parts]
            if bit == bits[0]:
                passed = parts[-1]
        gathered.append(parts)
    expert_index = (exp_index * per_column + ctx_index // 2).reshape(1).astype(jnp.int32)
    returned, passed = {}, None
    for k in sorted(range(per_column), key=lambda k: -min(k, 2.5)):
        keep, send = expert_block(
            expert_index, gathered[k], weight_in, weight_out, other_in, other_out, width
        )
        for bit in reversed(bits):
            if passed is not None and bit == bits[0]:
                passed, send = lax.optimization_barrier((passed, send))
            received = swapped(send, "exp", bit)
            if bit == bits[0]:
                passed = received
            total = keep.astype(jnp.float32) + received.astype(jnp.float32)
            total = total.astype(jnp.bfloat16)
            half = total.shape[0] // 2
            keep, send = total[:half], total[half:]
        returned[k] = total if k == 0 else swapped(total, "ctx", 2 * k)
    moe_out = sum(returned[k].astype(jnp.float32) for k in range(per_column))
    layer_out = (attended.astype(jnp.float32) + moe_out).astype(jnp.bfloat16)
    return (layer_out, router_kl)


def powers_of_two(*counts):
    return all(count & (count - 1) == 0 for count in counts)


def body(*arrays):
    experts_total = arrays[7].shape[1]
    exp_count, ctx_count = lax.axis_size("exp"), lax.axis_size("ctx")
    dense = experts_total <= 2 * arrays[8].shape[1] and powers_of_two(exp_count, ctx_count)
    return (dense_body if dense else sparse_body)(*arrays)


def solution(mesh):
    return jax.shard_map(
        body,
        mesh=mesh,
        in_specs=(
            P(("group", "ctx", "exp"), None),
            P(("group", "ctx"), "exp"),
            P(("group", "ctx"), None),
            P(("group", "ctx"), None),
            P(("group", "ctx")),
            P("exp", None),
            P(),
            P(),
            P(("group", "ctx", "exp"), None),
            P("ctx", "exp", None, None),
            P("ctx", "exp", None, None),
            P(("group", "ctx", "exp"), None),
        ),
        out_specs=(P(("group", "ctx", "exp"), None), P(("group", "ctx", "exp"))),
        check_vma=False,
    )
```

```python
import functools
import math

import jax
import jax.numpy as jnp
import numpy as np
from jax import lax
from jax.experimental import pallas as pl
from jax.experimental.pallas import tpu as pltpu
from jax.sharding import PartitionSpec as P

eps = 1e-06
theta = 1000000.0


def passed_along(value, axis, steps):
    count = lax.axis_size(axis)
    initial, last = (max(0, -steps), min(count, count - steps))
    return lax.ppermute(value, axis, [(source, source + steps) for source in range(initial, last)])


def frequencies(head_dim):
    return theta ** (-jnp.arange(head_dim // 2, dtype=jnp.float32) * 2.0 / head_dim)


def head_norm(values_in):
    widened = values_in.astype(jnp.float32)
    return widened / jnp.sqrt(jnp.mean(widened * widened, axis=-1, keepdims=True) + eps)


def rotate(vectors, angle):
    middle = vectors.shape[-1] // 2
    cosine = jnp.cos(angle)
    sine_part = jnp.sin(angle)
    leading = vectors[..., :middle]
    trailing = vectors[..., middle:]
    return jnp.concatenate(
        [leading * cosine - trailing * sine_part, trailing * cosine + leading * sine_part], axis=-1
    )


def activate(act):
    inner = act.shape[1] // 2
    return (jax.nn.silu(act[:, :inner]) * act[:, inner:]).astype(jnp.bfloat16)


def sparse_body(
    hidden,
    queries,
    keys,
    values,
    positions,
    out_weight,
    ffn_gain,
    router_weight,
    routes,
    expert_in,
    expert_out,
    rollout_logits,
):
    block_rows = queries.shape[0]
    head_dim = queries.shape[1]
    width = hidden.shape[1]
    token_rows = hidden.shape[0]
    top_count = routes.shape[1]
    experts_total = router_weight.shape[1]
    ctx_index = lax.axis_index("ctx")
    exp_index = lax.axis_index("exp")
    ctx_count = lax.axis_size("ctx")
    exp_count = lax.axis_size("exp")
    kv_heads = keys.shape[1] // head_dim
    kv_group = exp_index // (exp_count // kv_heads)
    angle = positions.astype(jnp.float32)[:, None] * frequencies(head_dim)[None, :]
    query_rot = rotate(head_norm(queries), angle).astype(jnp.bfloat16)
    key_own = rotate(
        head_norm(lax.dynamic_slice_in_dim(keys, kv_group * head_dim, head_dim, 1)), angle
    ).astype(jnp.bfloat16)
    value_own = lax.dynamic_slice_in_dim(values, kv_group * head_dim, head_dim, 1)
    key_before, value_before = passed_along((key_own, value_own), "ctx", 1)
    key_window = jnp.concatenate([key_before, key_own], axis=0)
    value_window = jnp.concatenate([value_before, value_own], axis=0)
    scores = lax.dot_general(
        query_rot, key_window, (((1,), (1,)), ((), ())), preferred_element_type=jnp.float32
    )
    scores = scores / jnp.sqrt(jnp.float32(head_dim))
    query_at = ctx_index * block_rows + jnp.arange(block_rows, dtype=jnp.int32)
    key_at = ctx_index * block_rows - block_rows + jnp.arange(2 * block_rows, dtype=jnp.int32)
    allowed = (key_at[None, :] <= query_at[:, None]) & (
        key_at[None, :] >= (query_at - positions)[:, None]
    )
    raw = jnp.where(allowed, jnp.exp(scores), 0.0)
    weights = (raw / jnp.sum(raw, axis=1, keepdims=True)).astype(jnp.bfloat16)
    head_out = jnp.dot(weights, value_window, preferred_element_type=jnp.float32).astype(
        jnp.bfloat16
    )
    term = jnp.dot(head_out, out_weight, preferred_element_type=jnp.float32).astype(jnp.bfloat16)
    summed = lax.psum_scatter(
        lax.optimization_barrier(term).astype(jnp.float32).astype(jnp.bfloat16),
        "exp",
        scatter_dimension=0,
        tiled=True,
    ).astype(jnp.float32)
    attended = (hidden.astype(jnp.float32) + summed).astype(jnp.bfloat16)
    widened = attended.astype(jnp.float32)
    moe_in = (
        widened
        / jnp.sqrt(jnp.mean(widened * widened, axis=1, keepdims=True) + eps)
        * ffn_gain[None, :]
    ).astype(jnp.bfloat16)
    router_logits = jnp.dot(moe_in, router_weight, preferred_element_type=jnp.float32)
    current_logprob = router_logits - jnp.log(
        jnp.sum(jnp.exp(router_logits), axis=1, keepdims=True)
    )
    rollout_logprob = rollout_logits - jnp.log(
        jnp.sum(jnp.exp(rollout_logits), axis=1, keepdims=True)
    )
    router_kl = jnp.sum(jnp.exp(rollout_logprob) * (rollout_logprob - current_logprob), axis=1)
    expert_ids = jnp.arange(experts_total, dtype=jnp.int32)
    picked = routes[:, :, None] == expert_ids[None, None, :]
    chosen_logits = jnp.sum(jnp.where(picked, router_logits[:, None, :], 0.0), axis=2)
    gate_raw = jnp.exp(chosen_logits)
    gates = (gate_raw / jnp.sum(gate_raw, axis=1, keepdims=True)).astype(jnp.bfloat16)
    capacity = min(token_rows, max(2, 3 * token_rows * top_count // (2 * experts_total)))
    per_column = experts_total // exp_count
    slots_total = experts_total * capacity
    flat_routes = routes.reshape(-1)
    member = (flat_routes[:, None] == expert_ids[None, :]).astype(jnp.int32)
    earlier = jnp.cumsum(member, axis=0) - member
    slot_rank = jnp.sum(earlier * member, axis=1)
    target = (
        flat_routes % per_column * exp_count + flat_routes // per_column
    ) * capacity + slot_rank
    target_grid = target.reshape(token_rows, top_count)
    slot_ids = jnp.arange(slots_total, dtype=jnp.int32)
    placing = jnp.any(target_grid[None, :, :] == slot_ids[:, None, None], axis=2).astype(
        jnp.bfloat16
    )
    gate_grid = jnp.where(
        target_grid[:, :, None] == slot_ids[None, None, :], gates[:, :, None], jnp.bfloat16(0)
    )
    combining = jnp.sum(gate_grid.astype(jnp.float32), axis=1).astype(jnp.bfloat16)
    weight_in = expert_in[0, 0]
    weight_out = expert_out[0, 0]
    packed = jnp.dot(placing, moe_in, preferred_element_type=jnp.float32).astype(jnp.bfloat16)
    packed = packed.reshape(per_column, 1, exp_count, capacity, width)
    doubled = jnp.broadcast_to(packed, (per_column, 2, exp_count, capacity, width)).reshape(
        ctx_count, exp_count, capacity, width
    )
    arrived = lax.all_to_all(
        lax.all_to_all(doubled, "ctx", split_axis=0, concat_axis=0, tiled=True),
        "exp",
        split_axis=1,
        concat_axis=1,
        tiled=True,
    )
    act = jnp.dot(arrived.reshape(-1, width), weight_in, preferred_element_type=jnp.float32)
    partial_value = jnp.dot(activate(act), weight_out, preferred_element_type=jnp.float32).astype(
        jnp.bfloat16
    )
    returned = lax.all_to_all(
        lax.all_to_all(
            partial_value.reshape(ctx_count, exp_count, capacity, width),
            "ctx",
            split_axis=0,
            concat_axis=0,
            tiled=True,
        ),
        "exp",
        split_axis=1,
        concat_axis=1,
        tiled=True,
    )
    paired = returned.reshape(per_column, 2, exp_count * capacity, width).astype(jnp.float32)
    expert_output = (paired[:, 0] + paired[:, 1]).astype(jnp.bfloat16).reshape(slots_total, width)
    moe_out = jnp.dot(combining, expert_output, preferred_element_type=jnp.float32)
    layer_out = (attended.astype(jnp.float32) + moe_out).astype(jnp.bfloat16)
    return (layer_out, router_kl)


def swapped(value, axis, mask):
    count = lax.axis_size(axis)
    return lax.ppermute(value, axis, [(source, source ^ mask) for source in range(count)])


def attention_kernel(order, index_ref, pos_ref, q_ref, before_ref, own_ref, weight_ref, *refs):
    outputs, (cos_ref, sin_ref, mixed) = refs[:-3], refs[-3:]
    block, size = q_ref.shape
    rows = block // len(order)
    pos_row = pos_ref[...].astype(jnp.float32)
    along = lax.broadcasted_iota(jnp.int32, (block, block), 0)
    across = lax.broadcasted_iota(jnp.int32, (block, block), 1)
    pos_col = jnp.sum(jnp.where(along == across, pos_row, 0.0), axis=1, keepdims=True)
    opening = jnp.sum(jnp.where(across[:1] == 0, pos_row, 0.0), axis=1, keepdims=True)
    earlier = opening - block + along[:, :1].astype(jnp.float32)
    lane = lax.broadcasted_iota(jnp.int32, (1, size), 1)
    lower = lane < size // 2
    phase = jnp.where(lower, 0.0, math.pi / 2)
    turn_of = jnp.where(lower, lane, lane - size // 2).astype(jnp.float32)
    spectrum = jnp.exp(turn_of * (-2.0 * math.log(theta) / size))
    for half, at in enumerate((earlier, pos_col)):
        turn = jnp.cos(at * spectrum - phase)
        swap = pltpu.roll(turn, size // 2, 1)
        cos_ref[half * block : (half + 1) * block, :] = jnp.where(lower, turn, swap)
        sin_ref[half * block : (half + 1) * block, :] = jnp.where(lower, -swap, turn)

    def turned(vectors, start):
        wide = vectors.astype(jnp.float32)
        wide = wide * lax.rsqrt(jnp.mean(wide * wide, axis=1, keepdims=True) + eps)
        cosine, sine = cos_ref[start : start + block, :], sin_ref[start : start + block, :]
        return (wide * cosine + pltpu.roll(wide, size // 2, 1) * sine).astype(jnp.bfloat16)

    query_at = lax.broadcasted_iota(jnp.int32, (block, 2 * block), 0)
    key_at = lax.broadcasted_iota(jnp.int32, (block, 2 * block), 1) - block
    allowed = (key_at <= query_at) & (key_at >= query_at - pos_col.astype(jnp.int32))
    keys = jnp.concatenate([turned(before_ref[:, :size], 0), turned(own_ref[:, :size], block)], axis=0)
    values = jnp.concatenate([before_ref[:, size:], own_ref[:, size:]], axis=0)
    query = turned(q_ref[...], block)
    scores = lax.dot_general(
        query, keys, (((1,), (1,)), ((), ())), preferred_element_type=jnp.float32
    ) * (1.0 / math.sqrt(size))
    raw = jnp.where(allowed, jnp.exp(scores), 0.0)
    weights = (raw / jnp.sum(raw, axis=1, keepdims=True)).astype(jnp.bfloat16)
    mixed[...] = jnp.dot(weights, values, preferred_element_type=jnp.float32).astype(jnp.bfloat16)
    picked = [
        mixed[pl.ds(pl.multiple_of((index_ref[0] ^ owner) * rows, 16), rows), :] for owner in order
    ]
    term = jnp.dot(
        jnp.concatenate(picked, axis=0), weight_ref[...], preferred_element_type=jnp.float32
    ).astype(jnp.bfloat16)
    for i, output in enumerate(outputs):
        output[...] = term[i * rows : (i + 1) * rows]


def router_kernel(heads, index_ref, *refs):
    terms, refs = refs[:heads], refs[heads:]
    hidden_ref, gain_ref, router_ref, routes_ref, rollout_ref = refs[:5]
    attended_ref, payload_ref, kl_ref = refs[5:]
    width = hidden_ref.shape[1]
    experts, rows = rollout_ref.shape
    total = sum(term[...].astype(jnp.float32) for term in terms) + hidden_ref[...].astype(jnp.float32)
    attended = total.astype(jnp.bfloat16)
    attended_ref[...] = attended
    wide = attended.astype(jnp.float32)
    moe_in = (
        wide * lax.rsqrt(jnp.mean(wide * wide, axis=1, keepdims=True) + eps) * gain_ref[...]
    ).astype(jnp.bfloat16)
    payload_ref[:, :width] = moe_in
    logits = lax.dot_general(
        router_ref[...], moe_in, (((1,), (1,)), ((), ())), preferred_element_type=jnp.float32
    )
    raised = jnp.exp(logits)
    rollout = rollout_ref[...]
    current_log = logits - jnp.log(jnp.sum(raised, axis=0, keepdims=True))
    rollout_log = rollout - jnp.log(jnp.sum(jnp.exp(rollout), axis=0, keepdims=True))
    kl_ref[...] = jnp.sum(jnp.exp(rollout_log) * (rollout_log - current_log), axis=0, keepdims=True)
    ids = lax.broadcasted_iota(jnp.int32, (experts, rows), 0)
    picked = jnp.zeros((experts, rows), jnp.float32)
    for k in range(routes_ref.shape[0]):
        picked = picked + jnp.where(routes_ref[k : k + 1, :] == ids, 1.0, 0.0)
    chosen = jnp.where(picked > 0.0, raised, 0.0)
    gates = (chosen / jnp.sum(chosen, axis=0, keepdims=True)).astype(jnp.bfloat16)
    lanes = payload_ref.shape[1] - width
    spread = (
        lax.broadcasted_iota(jnp.int32, (experts, lanes), 0)
        == lax.broadcasted_iota(jnp.int32, (experts, lanes), 1)
    ).astype(jnp.float32).astype(jnp.bfloat16)
    payload_ref[:, width:] = lax.dot_general(
        gates, spread, (((0,), (0,)), ((), ())), preferred_element_type=jnp.float32
    ).astype(jnp.bfloat16)


VMEM = pl.BlockSpec(memory_space=pltpu.VMEM)
SMEM = pl.BlockSpec(memory_space=pltpu.SMEM)


HBM = pl.BlockSpec(memory_space=pltpu.HBM)
GRANT = 60 * 1024 * 1024


def fetching(kernel, count, stored, index_ref, *refs):
    inputs, refs = refs[:count], refs[count:]
    outputs, refs = refs[: len(stored)], refs[len(stored) :]
    held, refs = refs[:count], refs[count:]
    sent, refs = refs[: sum(stored)], refs[sum(stored) :]
    arrived, left, scratch = refs[0], refs[1], refs[2:]
    copies = [
        pltpu.make_async_copy(source, target, arrived.at[i])
        for i, (source, target) in enumerate(zip(inputs, held))
    ]
    for copy in copies:
        copy.start()
    for copy in copies:
        copy.wait()
    sent = iter(sent)
    built, copies = [], []
    for output, far in zip(outputs, stored):
        built.append(next(sent) if far else output)
        if far:
            copies.append(pltpu.make_async_copy(built[-1], output, left.at[len(copies)]))
    kernel(index_ref, *held, *built, *scratch)
    for copy in copies:
        copy.start()
    for copy in copies:
        copy.wait()


def small_kernel(kernel, out_shape, inputs, stored, scratch=(), flops=0):
    held = [pltpu.VMEM(array.shape, array.dtype) for array in inputs[1:]]
    sent = [pltpu.VMEM(leaf.shape, leaf.dtype) for leaf, far in zip(out_shape, stored) if far]
    return pl.pallas_call(
        functools.partial(fetching, kernel, len(held), stored),
        out_shape=out_shape,
        in_specs=[SMEM] + [HBM] * len(held),
        out_specs=tuple(HBM if far else VMEM for far in stored),
        scratch_shapes=[
            *held,
            *sent,
            pltpu.SemaphoreType.DMA((len(held),)),
            pltpu.SemaphoreType.DMA((max(1, len(sent)),)),
            *scratch,
        ],
        compiler_params=pltpu.CompilerParams(vmem_limit_bytes=GRANT),
        cost_estimate=pl.CostEstimate(flops=0, bytes_accessed=0, transcendentals=0),
    )(*inputs)


def fetched(sources, targets, arrived):
    copies = [
        pltpu.make_async_copy(source, target, arrived.at[i])
        for i, (source, target) in enumerate(zip(sources, targets))
    ]
    for copy in copies:
        copy.start()
    return copies


def hidden_kernel(width, *refs):
    parts = len(refs) - 8
    sources, refs = refs[: parts + 2], refs[parts + 2 :]
    inner_ref, spare_ref, own, other, tokens, arrived = refs
    rows = sources[2].shape[0]
    targets = [own, other] + [tokens.at[pl.ds(p * rows, rows), :] for p in range(parts)]
    copies = fetched(sources, targets, arrived)
    for copy in copies[:1] + copies[2:]:
        copy.wait()
    half = own.shape[1] // 2
    inner_ref[:, :half] = activate(
        jnp.dot(tokens[:, :width], own[...], preferred_element_type=jnp.float32)
    )
    spare_ref[...] = tokens[:, width:]
    copies[1].wait()
    inner_ref[:, half:] = activate(
        jnp.dot(tokens[:, :width], other[...], preferred_element_type=jnp.float32)
    )


def hidden_blocks(tokens, own_in, other_in):
    width, inner = own_in.shape
    rows, total = tokens[0].shape
    parts = len(tokens)
    return pl.pallas_call(
        functools.partial(hidden_kernel, width),
        out_shape=(
            jax.ShapeDtypeStruct((parts * rows, inner), jnp.bfloat16),
            jax.ShapeDtypeStruct((parts * rows, total - width), jnp.bfloat16),
        ),
        in_specs=[HBM] * (parts + 2),
        out_specs=(VMEM, VMEM),
        scratch_shapes=[
            pltpu.VMEM(own_in.shape, own_in.dtype),
            pltpu.VMEM(own_in.shape, own_in.dtype),
            pltpu.VMEM((parts * rows, total), jnp.bfloat16),
            pltpu.SemaphoreType.DMA((parts + 2,)),
        ],
        compiler_params=pltpu.CompilerParams(vmem_limit_bytes=GRANT),
        cost_estimate=pl.CostEstimate(flops=0, bytes_accessed=9 << 20, transcendentals=0),
    )(own_in, other_in, *tokens)


def output_kernel(index_ref, inner_ref, spare_ref, own_ref, other_ref, *refs):
    outputs, (inner, spare, weight, ready, arrived, left) = refs[:-6], refs[-6:]
    depth = own_ref.shape[0]
    targets = [weight.at[pl.ds(0, depth), :], weight.at[pl.ds(depth, depth), :], inner, spare]
    for copy in fetched([own_ref, other_ref, inner_ref, spare_ref], targets, arrived):
        copy.wait()
    part = outputs[0].shape[0]
    step = 4 * part
    copies = []
    for start in reversed(range(0, inner.shape[0], step)):
        block = slice(start, start + step)
        chosen = spare[block, :].astype(jnp.float32)
        picked = lax.broadcasted_iota(jnp.int32, chosen.shape, 1) == index_ref[0]
        gate = jnp.sum(jnp.where(picked, chosen, 0.0), axis=1, keepdims=True)
        out = jnp.dot(inner[block, :], weight[...], preferred_element_type=jnp.float32)
        ready[block, :] = (out * gate).astype(jnp.bfloat16)
        for i in reversed(range(start // part, (start + step) // part)):
            source = ready.at[pl.ds(i * part, part), :]
            copies.append(pltpu.make_async_copy(source, outputs[i], left.at[i]))
            copies[-1].start()
    for copy in copies:
        copy.wait()


def output_blocks(count, index, inner, spare, own_out, other_out):
    width = own_out.shape[1]
    rows = inner.shape[0]
    half = jax.ShapeDtypeStruct((rows // count // 2, width), jnp.bfloat16)
    flat = pl.pallas_call(
        output_kernel,
        out_shape=(half,) * (2 * count),
        in_specs=[SMEM] + [HBM] * 4,
        out_specs=(HBM,) * (2 * count),
        scratch_shapes=[
            pltpu.VMEM(inner.shape, inner.dtype),
            pltpu.VMEM(spare.shape, spare.dtype),
            pltpu.VMEM((inner.shape[1], width), jnp.bfloat16),
            pltpu.VMEM((rows, width), jnp.bfloat16),
            pltpu.SemaphoreType.DMA((4,)),
            pltpu.SemaphoreType.DMA((2 * count,)),
        ],
        compiler_params=pltpu.CompilerParams(vmem_limit_bytes=GRANT),
        cost_estimate=pl.CostEstimate(flops=0, bytes_accessed=0, transcendentals=0),
    )(index, inner, spare, own_out, other_out)
    return [flat[2 * k : 2 * k + 2] for k in range(count)]


def dense_body(
    hidden,
    queries,
    keys,
    values,
    positions,
    out_weight,
    ffn_gain,
    router_weight,
    routes,
    expert_in,
    expert_out,
    rollout_logits,
):
    block_rows = queries.shape[0]
    head_dim = queries.shape[1]
    width = hidden.shape[1]
    token_rows = hidden.shape[0]
    experts_total = router_weight.shape[1]
    ctx_index = lax.axis_index("ctx")
    exp_index = lax.axis_index("exp")
    exp_count = lax.axis_size("exp")
    kv_heads = keys.shape[1] // head_dim
    per_column = experts_total // exp_count
    share = exp_count // kv_heads
    bits = []
    step = exp_count // 2
    while step:
        bits.append(step)
        step //= 2

    weight_in = expert_in[0, 0]
    weight_out = expert_out[0, 0]
    kv_group = exp_index // share
    kv_own = jnp.concatenate(
        [lax.dynamic_slice_in_dim(array, kv_group * head_dim, head_dim, 1) for array in (keys, values)],
        axis=1,
    )
    before = passed_along(kv_own, "ctx", 1)
    before, weight_in_sent, weight_out_sent = lax.optimization_barrier((before, weight_in, weight_out))
    other_out = swapped(weight_out_sent, "ctx", 1)
    other_in = swapped(weight_in_sent, "ctx", 1)

    index = exp_index.reshape(1).astype(jnp.int32)
    owners = [0]
    for bit in bits:
        owners = owners + [owner ^ bit for owner in owners]
    table = pltpu.VMEM((2 * block_rows, head_dim), jnp.float32)
    term = jax.ShapeDtypeStruct((token_rows, width), jnp.bfloat16)
    terms = small_kernel(
        functools.partial(attention_kernel, tuple(owners)),
        (term,) * exp_count,
        (index, positions[None, :], queries, before, kv_own, out_weight),
        (True,) * exp_count,
        (table, table, pltpu.VMEM((block_rows, head_dim), jnp.bfloat16)),
        0,
    )
    terms = [terms[0]] + [swapped(term, "exp", owner) for term, owner in zip(terms[1:], owners[1:])]
    lanes = -(-experts_total // 128) * 128
    attended, payload, router_kl = small_kernel(
        functools.partial(router_kernel, exp_count),
        (
            jax.ShapeDtypeStruct((token_rows, width), jnp.bfloat16),
            jax.ShapeDtypeStruct((token_rows, width + lanes), jnp.bfloat16),
            jax.ShapeDtypeStruct((1, token_rows), jnp.float32),
        ),
        (
            index,
            *terms,
            hidden,
            ffn_gain[None, :],
            router_weight.T,
            routes.T,
            rollout_logits.T,
        ),
        (False, True, False),
        (),
        2 * token_rows * width * experts_total,
    )
    router_kl = router_kl[0]
    blocks, sent = [payload], payload
    for k in range(1, per_column):
        if k > 2:
            blocks[-1], sent = lax.optimization_barrier((blocks[-1], payload))
        blocks.append(swapped(sent, "ctx", 2 * k))
    crossed = []
    for turn, block in enumerate(blocks):
        parts = [block]
        for bit in bits[:-1]:
            if turn > 0:
                crossed[turn - 1][-1], *parts = lax.optimization_barrier((crossed[turn - 1][-1], *parts))
            parts = parts + [swapped(part, "exp", bit) for part in parts]
        crossed.append(parts)
    expert_index = (exp_index * per_column + ctx_index // 2).reshape(1).astype(jnp.int32)
    groups, pairs, tokens = 1, [], []
    for turn, parts in enumerate(crossed):
        stack = jnp.concatenate(parts, axis=0)
        tokens = tokens + [stack, swapped(stack, "exp", bits[-1])]
        if (turn + 1) % (per_column // groups) == 0:
            pairs.append(hidden_blocks(tokens, weight_in, other_in))
            tokens = []
    inner, spare = pairs[0]
    inner, other_out = lax.optimization_barrier((inner, other_out))
    partials = output_blocks(per_column, expert_index, inner, spare, weight_out, other_out)
    returned = {}
    for k in reversed(range(per_column)):
        keep, send = partials[k]
        for bit in reversed(bits):
            if bit == bits[0] and k == 0:
                send, returned[2] = lax.optimization_barrier((send, returned[2]))
            received = swapped(send, "exp", bit)
            total = keep.astype(jnp.float32) + received.astype(jnp.float32)
            total = total.astype(jnp.bfloat16)
            middle = total.shape[0] // 2
            keep, send = total[:middle], total[middle:]
        returned[k] = total
    returned = {k: total if k == 0 else swapped(total, "ctx", 2 * k) for k, total in returned.items()}
    moe_out = sum(returned[k].astype(jnp.float32) for k in range(per_column))
    layer_out = (attended.astype(jnp.float32) + moe_out).astype(jnp.bfloat16)
    return (layer_out, router_kl)


def powers_of_two(*counts):
    return all(count & (count - 1) == 0 for count in counts)


def body(*arrays):
    experts_total = arrays[7].shape[1]
    exp_count, ctx_count = lax.axis_size("exp"), lax.axis_size("ctx")
    dense = experts_total <= 2 * arrays[8].shape[1] and powers_of_two(exp_count, ctx_count)
    return (dense_body if dense else sparse_body)(*arrays)


def solution(mesh):
    return jax.shard_map(
        body,
        mesh=mesh,
        in_specs=(
            P(("group", "ctx", "exp"), None),
            P(("group", "ctx"), "exp"),
            P(("group", "ctx"), None),
            P(("group", "ctx"), None),
            P(("group", "ctx")),
            P("exp", None),
            P(),
            P(),
            P(("group", "ctx", "exp"), None),
            P("ctx", "exp", None, None),
            P("ctx", "exp", None, None),
            P(("group", "ctx", "exp"), None),
        ),
        out_specs=(P(("group", "ctx", "exp"), None), P(("group", "ctx", "exp"))),
        check_vma=False,
    )
```

```python
import functools
import math

import jax
import jax.numpy as jnp
import numpy as np
from jax import lax
from jax.experimental import pallas as pl
from jax.experimental.pallas import tpu as pltpu
from jax.sharding import PartitionSpec as P

eps = 1e-06
theta = 1000000.0


def passed_along(value, axis, steps):
    count = lax.axis_size(axis)
    initial, last = (max(0, -steps), min(count, count - steps))
    return lax.ppermute(value, axis, [(source, source + steps) for source in range(initial, last)])


def frequencies(head_dim):
    return theta ** (-jnp.arange(head_dim // 2, dtype=jnp.float32) * 2.0 / head_dim)


def head_norm(values_in):
    widened = values_in.astype(jnp.float32)
    return widened / jnp.sqrt(jnp.mean(widened * widened, axis=-1, keepdims=True) + eps)


def rotate(vectors, angle):
    middle = vectors.shape[-1] // 2
    cosine = jnp.cos(angle)
    sine_part = jnp.sin(angle)
    leading = vectors[..., :middle]
    trailing = vectors[..., middle:]
    return jnp.concatenate(
        [leading * cosine - trailing * sine_part, trailing * cosine + leading * sine_part], axis=-1
    )


def activate(act):
    inner = act.shape[1] // 2
    return (jax.nn.silu(act[:, :inner]) * act[:, inner:]).astype(jnp.bfloat16)


def sparse_body(
    hidden,
    queries,
    keys,
    values,
    positions,
    out_weight,
    ffn_gain,
    router_weight,
    routes,
    expert_in,
    expert_out,
    rollout_logits,
):
    block_rows = queries.shape[0]
    head_dim = queries.shape[1]
    width = hidden.shape[1]
    token_rows = hidden.shape[0]
    top_count = routes.shape[1]
    experts_total = router_weight.shape[1]
    ctx_index = lax.axis_index("ctx")
    exp_index = lax.axis_index("exp")
    ctx_count = lax.axis_size("ctx")
    exp_count = lax.axis_size("exp")
    kv_heads = keys.shape[1] // head_dim
    kv_group = exp_index // (exp_count // kv_heads)
    angle = positions.astype(jnp.float32)[:, None] * frequencies(head_dim)[None, :]
    query_rot = rotate(head_norm(queries), angle).astype(jnp.bfloat16)
    key_own = rotate(
        head_norm(lax.dynamic_slice_in_dim(keys, kv_group * head_dim, head_dim, 1)), angle
    ).astype(jnp.bfloat16)
    value_own = lax.dynamic_slice_in_dim(values, kv_group * head_dim, head_dim, 1)
    key_before, value_before = passed_along((key_own, value_own), "ctx", 1)
    key_window = jnp.concatenate([key_before, key_own], axis=0)
    value_window = jnp.concatenate([value_before, value_own], axis=0)
    scores = lax.dot_general(
        query_rot, key_window, (((1,), (1,)), ((), ())), preferred_element_type=jnp.float32
    )
    scores = scores / jnp.sqrt(jnp.float32(head_dim))
    query_at = ctx_index * block_rows + jnp.arange(block_rows, dtype=jnp.int32)
    key_at = ctx_index * block_rows - block_rows + jnp.arange(2 * block_rows, dtype=jnp.int32)
    allowed = (key_at[None, :] <= query_at[:, None]) & (
        key_at[None, :] >= (query_at - positions)[:, None]
    )
    raw = jnp.where(allowed, jnp.exp(scores), 0.0)
    weights = (raw / jnp.sum(raw, axis=1, keepdims=True)).astype(jnp.bfloat16)
    head_out = jnp.dot(weights, value_window, preferred_element_type=jnp.float32).astype(
        jnp.bfloat16
    )
    term = jnp.dot(head_out, out_weight, preferred_element_type=jnp.float32).astype(jnp.bfloat16)
    summed = lax.psum_scatter(
        lax.optimization_barrier(term).astype(jnp.float32).astype(jnp.bfloat16),
        "exp",
        scatter_dimension=0,
        tiled=True,
    ).astype(jnp.float32)
    attended = (hidden.astype(jnp.float32) + summed).astype(jnp.bfloat16)
    widened = attended.astype(jnp.float32)
    moe_in = (
        widened
        / jnp.sqrt(jnp.mean(widened * widened, axis=1, keepdims=True) + eps)
        * ffn_gain[None, :]
    ).astype(jnp.bfloat16)
    router_logits = jnp.dot(moe_in, router_weight, preferred_element_type=jnp.float32)
    current_logprob = router_logits - jnp.log(
        jnp.sum(jnp.exp(router_logits), axis=1, keepdims=True)
    )
    rollout_logprob = rollout_logits - jnp.log(
        jnp.sum(jnp.exp(rollout_logits), axis=1, keepdims=True)
    )
    router_kl = jnp.sum(jnp.exp(rollout_logprob) * (rollout_logprob - current_logprob), axis=1)
    expert_ids = jnp.arange(experts_total, dtype=jnp.int32)
    picked = routes[:, :, None] == expert_ids[None, None, :]
    chosen_logits = jnp.sum(jnp.where(picked, router_logits[:, None, :], 0.0), axis=2)
    gate_raw = jnp.exp(chosen_logits)
    gates = (gate_raw / jnp.sum(gate_raw, axis=1, keepdims=True)).astype(jnp.bfloat16)
    capacity = min(token_rows, max(2, 3 * token_rows * top_count // (2 * experts_total)))
    per_column = experts_total // exp_count
    slots_total = experts_total * capacity
    flat_routes = routes.reshape(-1)
    member = (flat_routes[:, None] == expert_ids[None, :]).astype(jnp.int32)
    earlier = jnp.cumsum(member, axis=0) - member
    slot_rank = jnp.sum(earlier * member, axis=1)
    target = (
        flat_routes % per_column * exp_count + flat_routes // per_column
    ) * capacity + slot_rank
    target_grid = target.reshape(token_rows, top_count)
    slot_ids = jnp.arange(slots_total, dtype=jnp.int32)
    placing = jnp.any(target_grid[None, :, :] == slot_ids[:, None, None], axis=2).astype(
        jnp.bfloat16
    )
    gate_grid = jnp.where(
        target_grid[:, :, None] == slot_ids[None, None, :], gates[:, :, None], jnp.bfloat16(0)
    )
    combining = jnp.sum(gate_grid.astype(jnp.float32), axis=1).astype(jnp.bfloat16)
    weight_in = expert_in[0, 0]
    weight_out = expert_out[0, 0]
    packed = jnp.dot(placing, moe_in, preferred_element_type=jnp.float32).astype(jnp.bfloat16)
    packed = packed.reshape(per_column, 1, exp_count, capacity, width)
    doubled = jnp.broadcast_to(packed, (per_column, 2, exp_count, capacity, width)).reshape(
        ctx_count, exp_count, capacity, width
    )
    arrived = lax.all_to_all(
        lax.all_to_all(doubled, "ctx", split_axis=0, concat_axis=0, tiled=True),
        "exp",
        split_axis=1,
        concat_axis=1,
        tiled=True,
    )
    act = jnp.dot(arrived.reshape(-1, width), weight_in, preferred_element_type=jnp.float32)
    partial_value = jnp.dot(activate(act), weight_out, preferred_element_type=jnp.float32).astype(
        jnp.bfloat16
    )
    returned = lax.all_to_all(
        lax.all_to_all(
            partial_value.reshape(ctx_count, exp_count, capacity, width),
            "ctx",
            split_axis=0,
            concat_axis=0,
            tiled=True,
        ),
        "exp",
        split_axis=1,
        concat_axis=1,
        tiled=True,
    )
    paired = returned.reshape(per_column, 2, exp_count * capacity, width).astype(jnp.float32)
    expert_output = (paired[:, 0] + paired[:, 1]).astype(jnp.bfloat16).reshape(slots_total, width)
    moe_out = jnp.dot(combining, expert_output, preferred_element_type=jnp.float32)
    layer_out = (attended.astype(jnp.float32) + moe_out).astype(jnp.bfloat16)
    return (layer_out, router_kl)


def swapped(value, axis, mask):
    count = lax.axis_size(axis)
    return lax.ppermute(value, axis, [(source, source ^ mask) for source in range(count)])


def attention_kernel(order, index_ref, pos_ref, q_ref, before_ref, own_ref, weight_ref, *refs):
    outputs, (cos_ref, sin_ref, mixed) = refs[:-3], refs[-3:]
    block, size = q_ref.shape
    rows = block // len(order)
    pos_row = pos_ref[...].astype(jnp.float32)
    along = lax.broadcasted_iota(jnp.int32, (block, block), 0)
    across = lax.broadcasted_iota(jnp.int32, (block, block), 1)
    pos_col = jnp.sum(jnp.where(along == across, pos_row, 0.0), axis=1, keepdims=True)
    opening = jnp.sum(jnp.where(across[:1] == 0, pos_row, 0.0), axis=1, keepdims=True)
    earlier = opening - block + along[:, :1].astype(jnp.float32)
    lane = lax.broadcasted_iota(jnp.int32, (1, size), 1)
    lower = lane < size // 2
    phase = jnp.where(lower, 0.0, math.pi / 2)
    turn_of = jnp.where(lower, lane, lane - size // 2).astype(jnp.float32)
    spectrum = jnp.exp(turn_of * (-2.0 * math.log(theta) / size))
    for half, at in enumerate((earlier, pos_col)):
        turn = jnp.cos(at * spectrum - phase)
        swap = pltpu.roll(turn, size // 2, 1)
        cos_ref[half * block : (half + 1) * block, :] = jnp.where(lower, turn, swap)
        sin_ref[half * block : (half + 1) * block, :] = jnp.where(lower, -swap, turn)

    def turned(vectors, start):
        wide = vectors.astype(jnp.float32)
        wide = wide * lax.rsqrt(jnp.mean(wide * wide, axis=1, keepdims=True) + eps)
        cosine, sine = cos_ref[start : start + block, :], sin_ref[start : start + block, :]
        return (wide * cosine + pltpu.roll(wide, size // 2, 1) * sine).astype(jnp.bfloat16)

    query_at = lax.broadcasted_iota(jnp.int32, (block, 2 * block), 0)
    key_at = lax.broadcasted_iota(jnp.int32, (block, 2 * block), 1) - block
    allowed = (key_at <= query_at) & (key_at >= query_at - pos_col.astype(jnp.int32))
    keys = jnp.concatenate([turned(before_ref[:, :size], 0), turned(own_ref[:, :size], block)], axis=0)
    values = jnp.concatenate([before_ref[:, size:], own_ref[:, size:]], axis=0)
    query = turned(q_ref[...], block)
    scores = lax.dot_general(
        query, keys, (((1,), (1,)), ((), ())), preferred_element_type=jnp.float32
    ) * (1.0 / math.sqrt(size))
    raw = jnp.where(allowed, jnp.exp(scores), 0.0)
    weights = (raw / jnp.sum(raw, axis=1, keepdims=True)).astype(jnp.bfloat16)
    mixed[...] = jnp.dot(weights, values, preferred_element_type=jnp.float32).astype(jnp.bfloat16)
    picked = [
        mixed[pl.ds(pl.multiple_of((index_ref[0] ^ owner) * rows, 16), rows), :] for owner in order
    ]
    term = jnp.dot(
        jnp.concatenate(picked, axis=0), weight_ref[...], preferred_element_type=jnp.float32
    ).astype(jnp.bfloat16)
    for i, output in enumerate(outputs):
        output[...] = term[i * rows : (i + 1) * rows]


def router_kernel(heads, index_ref, *refs):
    terms, refs = refs[:heads], refs[heads:]
    hidden_ref, gain_ref, router_ref, routes_ref, rollout_ref = refs[:5]
    attended_ref, payload_ref, kl_ref = refs[5:]
    width = hidden_ref.shape[1]
    experts, rows = rollout_ref.shape
    total = sum(term[...].astype(jnp.float32) for term in terms) + hidden_ref[...].astype(jnp.float32)
    attended = total.astype(jnp.bfloat16)
    attended_ref[...] = attended
    wide = attended.astype(jnp.float32)
    moe_in = (
        wide * lax.rsqrt(jnp.mean(wide * wide, axis=1, keepdims=True) + eps) * gain_ref[...]
    ).astype(jnp.bfloat16)
    payload_ref[:, :width] = moe_in
    logits = lax.dot_general(
        router_ref[...], moe_in, (((1,), (1,)), ((), ())), preferred_element_type=jnp.float32
    )
    raised = jnp.exp(logits)
    rollout = rollout_ref[...]
    current_log = logits - jnp.log(jnp.sum(raised, axis=0, keepdims=True))
    rollout_log = rollout - jnp.log(jnp.sum(jnp.exp(rollout), axis=0, keepdims=True))
    kl_ref[...] = jnp.sum(jnp.exp(rollout_log) * (rollout_log - current_log), axis=0, keepdims=True)
    ids = lax.broadcasted_iota(jnp.int32, (experts, rows), 0)
    picked = jnp.zeros((experts, rows), jnp.float32)
    for k in range(routes_ref.shape[0]):
        picked = picked + jnp.where(routes_ref[k : k + 1, :] == ids, 1.0, 0.0)
    chosen = jnp.where(picked > 0.0, raised, 0.0)
    gates = (chosen / jnp.sum(chosen, axis=0, keepdims=True)).astype(jnp.bfloat16)
    lanes = payload_ref.shape[1] - width
    spread = (
        lax.broadcasted_iota(jnp.int32, (experts, lanes), 0)
        == lax.broadcasted_iota(jnp.int32, (experts, lanes), 1)
    ).astype(jnp.float32).astype(jnp.bfloat16)
    payload_ref[:, width:] = lax.dot_general(
        gates, spread, (((0,), (0,)), ((), ())), preferred_element_type=jnp.float32
    ).astype(jnp.bfloat16)


VMEM = pl.BlockSpec(memory_space=pltpu.VMEM)
SMEM = pl.BlockSpec(memory_space=pltpu.SMEM)


HBM = pl.BlockSpec(memory_space=pltpu.HBM)
GRANT = 60 * 1024 * 1024


def fetching(kernel, count, stored, index_ref, *refs):
    inputs, refs = refs[:count], refs[count:]
    outputs, refs = refs[: len(stored)], refs[len(stored) :]
    held, refs = refs[:count], refs[count:]
    sent, refs = refs[: sum(stored)], refs[sum(stored) :]
    arrived, left, scratch = refs[0], refs[1], refs[2:]
    copies = [
        pltpu.make_async_copy(source, target, arrived.at[i])
        for i, (source, target) in enumerate(zip(inputs, held))
    ]
    for copy in copies:
        copy.start()
    for copy in copies:
        copy.wait()
    sent = iter(sent)
    built, copies = [], []
    for output, far in zip(outputs, stored):
        built.append(next(sent) if far else output)
        if far:
            copies.append(pltpu.make_async_copy(built[-1], output, left.at[len(copies)]))
    kernel(index_ref, *held, *built, *scratch)
    for copy in copies:
        copy.start()
    for copy in copies:
        copy.wait()


def small_kernel(kernel, out_shape, inputs, stored, scratch=(), flops=0):
    held = [pltpu.VMEM(array.shape, array.dtype) for array in inputs[1:]]
    sent = [pltpu.VMEM(leaf.shape, leaf.dtype) for leaf, far in zip(out_shape, stored) if far]
    return pl.pallas_call(
        functools.partial(fetching, kernel, len(held), stored),
        out_shape=out_shape,
        in_specs=[SMEM] + [HBM] * len(held),
        out_specs=tuple(HBM if far else VMEM for far in stored),
        scratch_shapes=[
            *held,
            *sent,
            pltpu.SemaphoreType.DMA((len(held),)),
            pltpu.SemaphoreType.DMA((max(1, len(sent)),)),
            *scratch,
        ],
        compiler_params=pltpu.CompilerParams(vmem_limit_bytes=GRANT),
        cost_estimate=pl.CostEstimate(flops=0, bytes_accessed=0, transcendentals=0),
    )(*inputs)


def fetched(sources, targets, arrived):
    copies = [
        pltpu.make_async_copy(source, target, arrived.at[i])
        for i, (source, target) in enumerate(zip(sources, targets))
    ]
    for copy in copies:
        copy.start()
    return copies


def hidden_kernel(width, *refs):
    parts = len(refs) - 8
    sources, refs = refs[: parts + 2], refs[parts + 2 :]
    inner_ref, spare_ref, own, other, tokens, arrived = refs
    rows = sources[2].shape[0]
    targets = [own, other] + [tokens.at[pl.ds(p * rows, rows), :] for p in range(parts)]
    copies = fetched(sources, targets, arrived)
    for copy in copies[:1] + copies[2:]:
        copy.wait()
    half = own.shape[1] // 2
    inner_ref[:, :half] = activate(
        jnp.dot(tokens[:, :width], own[...], preferred_element_type=jnp.float32)
    )
    spare_ref[...] = tokens[:, width:]
    copies[1].wait()
    inner_ref[:, half:] = activate(
        jnp.dot(tokens[:, :width], other[...], preferred_element_type=jnp.float32)
    )


def hidden_blocks(tokens, own_in, other_in):
    width, inner = own_in.shape
    rows, total = tokens[0].shape
    parts = len(tokens)
    return pl.pallas_call(
        functools.partial(hidden_kernel, width),
        out_shape=(
            jax.ShapeDtypeStruct((parts * rows, inner), jnp.bfloat16),
            jax.ShapeDtypeStruct((parts * rows, total - width), jnp.bfloat16),
        ),
        in_specs=[HBM] * (parts + 2),
        out_specs=(VMEM, VMEM),
        scratch_shapes=[
            pltpu.VMEM(own_in.shape, own_in.dtype),
            pltpu.VMEM(own_in.shape, own_in.dtype),
            pltpu.VMEM((parts * rows, total), jnp.bfloat16),
            pltpu.SemaphoreType.DMA((parts + 2,)),
        ],
        compiler_params=pltpu.CompilerParams(vmem_limit_bytes=GRANT),
        cost_estimate=pl.CostEstimate(flops=0, bytes_accessed=9 << 20, transcendentals=0),
    )(own_in, other_in, *tokens)


def output_kernel(index_ref, inner_ref, spare_ref, own_ref, other_ref, *refs):
    outputs, (inner, spare, weight, ready, arrived, left) = refs[:-6], refs[-6:]
    depth = own_ref.shape[0]
    targets = [weight.at[pl.ds(0, depth), :], weight.at[pl.ds(depth, depth), :], inner, spare]
    for copy in fetched([own_ref, other_ref, inner_ref, spare_ref], targets, arrived):
        copy.wait()
    part = outputs[0].shape[0]
    step = 4 * part
    copies = []
    for start in reversed(range(0, inner.shape[0], step)):
        block = slice(start, start + step)
        chosen = spare[block, :].astype(jnp.float32)
        picked = lax.broadcasted_iota(jnp.int32, chosen.shape, 1) == index_ref[0]
        gate = jnp.sum(jnp.where(picked, chosen, 0.0), axis=1, keepdims=True)
        out = jnp.dot(inner[block, :], weight[...], preferred_element_type=jnp.float32)
        ready[block, :] = (out * gate).astype(jnp.bfloat16)
        for i in reversed(range(start // part, (start + step) // part)):
            source = ready.at[pl.ds(i * part, part), :]
            copies.append(pltpu.make_async_copy(source, outputs[i], left.at[i]))
            copies[-1].start()
    for copy in copies:
        copy.wait()


def output_blocks(count, index, inner, spare, own_out, other_out):
    width = own_out.shape[1]
    rows = inner.shape[0]
    half = jax.ShapeDtypeStruct((rows // count // 2, width), jnp.bfloat16)
    flat = pl.pallas_call(
        output_kernel,
        out_shape=(half,) * (2 * count),
        in_specs=[SMEM] + [HBM] * 4,
        out_specs=(HBM,) * (2 * count),
        scratch_shapes=[
            pltpu.VMEM(inner.shape, inner.dtype),
            pltpu.VMEM(spare.shape, spare.dtype),
            pltpu.VMEM((inner.shape[1], width), jnp.bfloat16),
            pltpu.VMEM((rows, width), jnp.bfloat16),
            pltpu.SemaphoreType.DMA((4,)),
            pltpu.SemaphoreType.DMA((2 * count,)),
        ],
        compiler_params=pltpu.CompilerParams(vmem_limit_bytes=GRANT),
        cost_estimate=pl.CostEstimate(flops=0, bytes_accessed=0, transcendentals=0),
    )(index, inner, spare, own_out, other_out)
    return [flat[2 * k : 2 * k + 2] for k in range(count)]


def dense_body(
    hidden,
    queries,
    keys,
    values,
    positions,
    out_weight,
    ffn_gain,
    router_weight,
    routes,
    expert_in,
    expert_out,
    rollout_logits,
):
    block_rows = queries.shape[0]
    head_dim = queries.shape[1]
    width = hidden.shape[1]
    token_rows = hidden.shape[0]
    experts_total = router_weight.shape[1]
    ctx_index = lax.axis_index("ctx")
    exp_index = lax.axis_index("exp")
    exp_count = lax.axis_size("exp")
    kv_heads = keys.shape[1] // head_dim
    per_column = experts_total // exp_count
    share = exp_count // kv_heads
    bits = []
    step = exp_count // 2
    while step:
        bits.append(step)
        step //= 2

    weight_in = expert_in[0, 0]
    weight_out = expert_out[0, 0]
    kv_group = exp_index // share
    kv_own = jnp.concatenate(
        [lax.dynamic_slice_in_dim(array, kv_group * head_dim, head_dim, 1) for array in (keys, values)],
        axis=1,
    )
    before = passed_along(kv_own, "ctx", 1)
    before, weight_in_sent, weight_out_sent = lax.optimization_barrier((before, weight_in, weight_out))
    other_out = swapped(weight_out_sent, "ctx", 1)
    other_in = swapped(weight_in_sent, "ctx", 1)

    index = exp_index.reshape(1).astype(jnp.int32)
    owners = [0]
    for bit in bits:
        owners = owners + [owner ^ bit for owner in owners]
    table = pltpu.VMEM((2 * block_rows, head_dim), jnp.float32)
    term = jax.ShapeDtypeStruct((token_rows, width), jnp.bfloat16)
    terms = small_kernel(
        functools.partial(attention_kernel, tuple(owners)),
        (term,) * exp_count,
        (index, positions[None, :], queries, before, kv_own, out_weight),
        (True,) * exp_count,
        (table, table, pltpu.VMEM((block_rows, head_dim), jnp.bfloat16)),
        0,
    )
    terms = [terms[0]] + [swapped(term, "exp", owner) for term, owner in zip(terms[1:], owners[1:])]
    lanes = -(-experts_total // 128) * 128
    attended, payload, router_kl = small_kernel(
        functools.partial(router_kernel, exp_count),
        (
            jax.ShapeDtypeStruct((token_rows, width), jnp.bfloat16),
            jax.ShapeDtypeStruct((token_rows, width + lanes), jnp.bfloat16),
            jax.ShapeDtypeStruct((1, token_rows), jnp.float32),
        ),
        (
            index,
            *terms,
            hidden,
            ffn_gain[None, :],
            router_weight.T,
            routes.T,
            rollout_logits.T,
        ),
        (False, True, False),
        (),
        2 * token_rows * width * experts_total,
    )
    router_kl = router_kl[0]
    crossed, passed = {}, None
    for k in sorted(range(per_column), key=lambda k: (k.bit_count(), -k)):
        low = k & -k
        if k != low:
            crossed[k] = [swapped(part, "ctx", 2 * low) for part in crossed[k ^ low]]
            continue
        parts = [payload if k == 0 else swapped(payload, "ctx", 2 * k)]
        for bit in bits[:-1]:
            if k > 0:
                passed, *parts = lax.optimization_barrier((passed, *parts))
            parts = parts + [swapped(part, "exp", bit) for part in parts]
        passed = parts[-1]
        crossed[k] = parts
    crossed = [crossed[k] for k in range(per_column)]
    expert_index = (exp_index * per_column + ctx_index // 2).reshape(1).astype(jnp.int32)
    groups, pairs, tokens = 1, [], []
    for turn, parts in enumerate(crossed):
        stack = jnp.concatenate(parts, axis=0)
        if turn == per_column // 2:
            stack, other_in = lax.optimization_barrier((stack, other_in))
        tokens = tokens + [stack, swapped(stack, "exp", bits[-1])]
        if (turn + 1) % (per_column // groups) == 0:
            pairs.append(hidden_blocks(tokens, weight_in, other_in))
            tokens = []
    inner, spare = pairs[0]
    inner, other_out = lax.optimization_barrier((inner, other_out))
    partials = output_blocks(per_column, expert_index, inner, spare, weight_out, other_out)
    returned = {}
    for k in reversed(range(per_column)):
        keep, send = partials[k]
        for bit in reversed(bits):
            if bit == bits[0] and k == 0 and per_column > 2:
                send, returned[2] = lax.optimization_barrier((send, returned[2]))
            received = swapped(send, "exp", bit)
            total = keep.astype(jnp.float32) + received.astype(jnp.float32)
            total = total.astype(jnp.bfloat16)
            middle = total.shape[0] // 2
            keep, send = total[:middle], total[middle:]
        returned[k] = total
    returned = {k: total if k == 0 else swapped(total, "ctx", 2 * k) for k, total in returned.items()}
    moe_out = sum(returned[k].astype(jnp.float32) for k in range(per_column))
    layer_out = (attended.astype(jnp.float32) + moe_out).astype(jnp.bfloat16)
    return (layer_out, router_kl)


def powers_of_two(*counts):
    return all(count & (count - 1) == 0 for count in counts)


def body(*arrays):
    experts_total = arrays[7].shape[1]
    exp_count, ctx_count = lax.axis_size("exp"), lax.axis_size("ctx")
    dense = experts_total <= 2 * arrays[8].shape[1] and powers_of_two(exp_count, ctx_count)
    return (dense_body if dense else sparse_body)(*arrays)


def solution(mesh):
    return jax.shard_map(
        body,
        mesh=mesh,
        in_specs=(
            P(("group", "ctx", "exp"), None),
            P(("group", "ctx"), "exp"),
            P(("group", "ctx"), None),
            P(("group", "ctx"), None),
            P(("group", "ctx")),
            P("exp", None),
            P(),
            P(),
            P(("group", "ctx", "exp"), None),
            P("ctx", "exp", None, None),
            P("ctx", "exp", None, None),
            P(("group", "ctx", "exp"), None),
        ),
        out_specs=(P(("group", "ctx", "exp"), None), P(("group", "ctx", "exp"))),
        check_vma=False,
    )
```

```python
import functools
import math

import jax
import jax.numpy as jnp
import numpy as np
from jax import lax
from jax.experimental import pallas as pl
from jax.experimental.pallas import tpu as pltpu
from jax.sharding import PartitionSpec as P

eps = 1e-06
theta = 1000000.0


def passed_along(value, axis, steps):
    count = lax.axis_size(axis)
    initial, last = (max(0, -steps), min(count, count - steps))
    return lax.ppermute(value, axis, [(source, source + steps) for source in range(initial, last)])


def frequencies(head_dim):
    return theta ** (-jnp.arange(head_dim // 2, dtype=jnp.float32) * 2.0 / head_dim)


def head_norm(values_in):
    widened = values_in.astype(jnp.float32)
    return widened / jnp.sqrt(jnp.mean(widened * widened, axis=-1, keepdims=True) + eps)


def rotate(vectors, angle):
    middle = vectors.shape[-1] // 2
    cosine = jnp.cos(angle)
    sine_part = jnp.sin(angle)
    leading = vectors[..., :middle]
    trailing = vectors[..., middle:]
    return jnp.concatenate(
        [leading * cosine - trailing * sine_part, trailing * cosine + leading * sine_part], axis=-1
    )


def activate(act):
    inner = act.shape[1] // 2
    return (jax.nn.silu(act[:, :inner]) * act[:, inner:]).astype(jnp.bfloat16)


def sparse_body(
    hidden,
    queries,
    keys,
    values,
    positions,
    out_weight,
    ffn_gain,
    router_weight,
    routes,
    expert_in,
    expert_out,
    rollout_logits,
):
    block_rows = queries.shape[0]
    head_dim = queries.shape[1]
    width = hidden.shape[1]
    token_rows = hidden.shape[0]
    top_count = routes.shape[1]
    experts_total = router_weight.shape[1]
    ctx_index = lax.axis_index("ctx")
    exp_index = lax.axis_index("exp")
    ctx_count = lax.axis_size("ctx")
    exp_count = lax.axis_size("exp")
    kv_heads = keys.shape[1] // head_dim
    kv_group = exp_index // (exp_count // kv_heads)
    angle = positions.astype(jnp.float32)[:, None] * frequencies(head_dim)[None, :]
    query_rot = rotate(head_norm(queries), angle).astype(jnp.bfloat16)
    key_own = rotate(
        head_norm(lax.dynamic_slice_in_dim(keys, kv_group * head_dim, head_dim, 1)), angle
    ).astype(jnp.bfloat16)
    value_own = lax.dynamic_slice_in_dim(values, kv_group * head_dim, head_dim, 1)
    key_before, value_before = passed_along((key_own, value_own), "ctx", 1)
    key_window = jnp.concatenate([key_before, key_own], axis=0)
    value_window = jnp.concatenate([value_before, value_own], axis=0)
    scores = lax.dot_general(
        query_rot, key_window, (((1,), (1,)), ((), ())), preferred_element_type=jnp.float32
    )
    scores = scores / jnp.sqrt(jnp.float32(head_dim))
    query_at = ctx_index * block_rows + jnp.arange(block_rows, dtype=jnp.int32)
    key_at = ctx_index * block_rows - block_rows + jnp.arange(2 * block_rows, dtype=jnp.int32)
    allowed = (key_at[None, :] <= query_at[:, None]) & (
        key_at[None, :] >= (query_at - positions)[:, None]
    )
    raw = jnp.where(allowed, jnp.exp(scores), 0.0)
    weights = (raw / jnp.sum(raw, axis=1, keepdims=True)).astype(jnp.bfloat16)
    head_out = jnp.dot(weights, value_window, preferred_element_type=jnp.float32).astype(
        jnp.bfloat16
    )
    term = jnp.dot(head_out, out_weight, preferred_element_type=jnp.float32).astype(jnp.bfloat16)
    summed = lax.psum_scatter(
        lax.optimization_barrier(term).astype(jnp.float32).astype(jnp.bfloat16),
        "exp",
        scatter_dimension=0,
        tiled=True,
    ).astype(jnp.float32)
    attended = (hidden.astype(jnp.float32) + summed).astype(jnp.bfloat16)
    widened = attended.astype(jnp.float32)
    moe_in = (
        widened
        / jnp.sqrt(jnp.mean(widened * widened, axis=1, keepdims=True) + eps)
        * ffn_gain[None, :]
    ).astype(jnp.bfloat16)
    router_logits = jnp.dot(moe_in, router_weight, preferred_element_type=jnp.float32)
    current_logprob = router_logits - jnp.log(
        jnp.sum(jnp.exp(router_logits), axis=1, keepdims=True)
    )
    rollout_logprob = rollout_logits - jnp.log(
        jnp.sum(jnp.exp(rollout_logits), axis=1, keepdims=True)
    )
    router_kl = jnp.sum(jnp.exp(rollout_logprob) * (rollout_logprob - current_logprob), axis=1)
    expert_ids = jnp.arange(experts_total, dtype=jnp.int32)
    picked = routes[:, :, None] == expert_ids[None, None, :]
    chosen_logits = jnp.sum(jnp.where(picked, router_logits[:, None, :], 0.0), axis=2)
    gate_raw = jnp.exp(chosen_logits)
    gates = (gate_raw / jnp.sum(gate_raw, axis=1, keepdims=True)).astype(jnp.bfloat16)
    capacity = min(token_rows, max(2, 3 * token_rows * top_count // (2 * experts_total)))
    per_column = experts_total // exp_count
    slots_total = experts_total * capacity
    flat_routes = routes.reshape(-1)
    member = (flat_routes[:, None] == expert_ids[None, :]).astype(jnp.int32)
    earlier = jnp.cumsum(member, axis=0) - member
    slot_rank = jnp.sum(earlier * member, axis=1)
    target = (
        flat_routes % per_column * exp_count + flat_routes // per_column
    ) * capacity + slot_rank
    target_grid = target.reshape(token_rows, top_count)
    slot_ids = jnp.arange(slots_total, dtype=jnp.int32)
    placing = jnp.any(target_grid[None, :, :] == slot_ids[:, None, None], axis=2).astype(
        jnp.bfloat16
    )
    gate_grid = jnp.where(
        target_grid[:, :, None] == slot_ids[None, None, :], gates[:, :, None], jnp.bfloat16(0)
    )
    combining = jnp.sum(gate_grid.astype(jnp.float32), axis=1).astype(jnp.bfloat16)
    weight_in = expert_in[0, 0]
    weight_out = expert_out[0, 0]
    packed = jnp.dot(placing, moe_in, preferred_element_type=jnp.float32).astype(jnp.bfloat16)
    packed = packed.reshape(per_column, 1, exp_count, capacity, width)
    doubled = jnp.broadcast_to(packed, (per_column, 2, exp_count, capacity, width)).reshape(
        ctx_count, exp_count, capacity, width
    )
    arrived = lax.all_to_all(
        lax.all_to_all(doubled, "ctx", split_axis=0, concat_axis=0, tiled=True),
        "exp",
        split_axis=1,
        concat_axis=1,
        tiled=True,
    )
    act = jnp.dot(arrived.reshape(-1, width), weight_in, preferred_element_type=jnp.float32)
    partial_value = jnp.dot(activate(act), weight_out, preferred_element_type=jnp.float32).astype(
        jnp.bfloat16
    )
    returned = lax.all_to_all(
        lax.all_to_all(
            partial_value.reshape(ctx_count, exp_count, capacity, width),
            "ctx",
            split_axis=0,
            concat_axis=0,
            tiled=True,
        ),
        "exp",
        split_axis=1,
        concat_axis=1,
        tiled=True,
    )
    paired = returned.reshape(per_column, 2, exp_count * capacity, width).astype(jnp.float32)
    expert_output = (paired[:, 0] + paired[:, 1]).astype(jnp.bfloat16).reshape(slots_total, width)
    moe_out = jnp.dot(combining, expert_output, preferred_element_type=jnp.float32)
    layer_out = (attended.astype(jnp.float32) + moe_out).astype(jnp.bfloat16)
    return (layer_out, router_kl)


def swapped(value, axis, mask):
    count = lax.axis_size(axis)
    return lax.ppermute(value, axis, [(source, source ^ mask) for source in range(count)])


def column_of(row):
    count = row.shape[1]
    along = lax.broadcasted_iota(jnp.int32, (count, count), 0)
    across = lax.broadcasted_iota(jnp.int32, (count, count), 1)
    return jnp.sum(jnp.where(along == across, row, 0.0), axis=1, keepdims=True)


def turned(vectors, cosine, sine):
    wide = vectors.astype(jnp.float32)
    wide = wide * lax.rsqrt(jnp.mean(wide * wide, axis=1, keepdims=True) + eps)
    return (wide * cosine + pltpu.roll(wide, wide.shape[1] // 2, 1) * sine).astype(jnp.bfloat16)


def rotation_kernel(index_ref, pos_ref, q_ref, own_ref, query_ref, key_ref, cos_ref, sin_ref):
    block, size = q_ref.shape
    pos_row = pos_ref[...].astype(jnp.float32)
    pos_col = column_of(pos_row)
    first = lax.broadcasted_iota(jnp.int32, (1, block), 1) == 0
    opening = jnp.sum(jnp.where(first, pos_row, 0.0), axis=1, keepdims=True)
    earlier = opening - block + lax.broadcasted_iota(jnp.int32, (block, 1), 0).astype(jnp.float32)
    lane = lax.broadcasted_iota(jnp.int32, (1, size), 1)
    lower = lane < size // 2
    phase = jnp.where(lower, 0.0, math.pi / 2)
    turn_of = jnp.where(lower, lane, lane - size // 2).astype(jnp.float32)
    spectrum = jnp.exp(turn_of * (-2.0 * math.log(theta) / size))

    def table(at):
        turn = jnp.cos(at * spectrum - phase)
        swap = pltpu.roll(turn, size // 2, 1)
        return jnp.where(lower, turn, swap), jnp.where(lower, -swap, turn)

    cosine, sine = table(pos_col)
    query_ref[...] = turned(q_ref[...], cosine, sine)
    key_ref[...] = turned(own_ref[:, :size], cosine, sine)
    cos_ref[...], sin_ref[...] = table(earlier)


def attention_kernel(order, index_ref, pos_ref, query_ref, key_ref, cos_ref, sin_ref, before_ref, own_ref, *refs):
    weight_ref, outputs, mixed = refs[0], refs[1:-1], refs[-1]
    block, size = query_ref.shape
    rows = block // len(order)
    pos_col = column_of(pos_ref[...].astype(jnp.float32))
    query_at = lax.broadcasted_iota(jnp.int32, (block, 2 * block), 0)
    key_at = lax.broadcasted_iota(jnp.int32, (block, 2 * block), 1) - block
    allowed = (key_at <= query_at) & (key_at >= query_at - pos_col.astype(jnp.int32))
    keys = jnp.concatenate(
        [turned(before_ref[:, :size], cos_ref[...], sin_ref[...]), key_ref[...]], axis=0
    )
    values = jnp.concatenate([before_ref[:, size:], own_ref[:, size:]], axis=0)
    scores = lax.dot_general(
        query_ref[...], keys, (((1,), (1,)), ((), ())), preferred_element_type=jnp.float32
    ) * (1.0 / math.sqrt(size))
    raw = jnp.where(allowed, jnp.exp(scores), 0.0)
    weights = (raw / jnp.sum(raw, axis=1, keepdims=True)).astype(jnp.bfloat16)
    mixed[...] = jnp.dot(weights, values, preferred_element_type=jnp.float32).astype(jnp.bfloat16)
    picked = [
        mixed[pl.ds(pl.multiple_of((index_ref[0] ^ owner) * rows, 16), rows), :] for owner in order
    ]
    term = jnp.dot(
        jnp.concatenate(picked, axis=0), weight_ref[...], preferred_element_type=jnp.float32
    ).astype(jnp.bfloat16)
    for i, output in enumerate(outputs):
        output[...] = term[i * rows : (i + 1) * rows]


def router_kernel(heads, index_ref, *refs):
    terms, refs = refs[:heads], refs[heads:]
    hidden_ref, gain_ref, router_ref, routes_ref, rollout_ref = refs[:5]
    attended_ref, payload_ref, kl_ref = refs[5:]
    width = hidden_ref.shape[1]
    experts, rows = rollout_ref.shape
    total = sum(term[...].astype(jnp.float32) for term in terms) + hidden_ref[...].astype(jnp.float32)
    attended = total.astype(jnp.bfloat16)
    attended_ref[...] = attended
    wide = attended.astype(jnp.float32)
    moe_in = (
        wide * lax.rsqrt(jnp.mean(wide * wide, axis=1, keepdims=True) + eps) * gain_ref[...]
    ).astype(jnp.bfloat16)
    payload_ref[:, :width] = moe_in
    logits = lax.dot_general(
        router_ref[...], moe_in, (((1,), (1,)), ((), ())), preferred_element_type=jnp.float32
    )
    raised = jnp.exp(logits)
    rollout = rollout_ref[...]
    current_log = logits - jnp.log(jnp.sum(raised, axis=0, keepdims=True))
    rollout_log = rollout - jnp.log(jnp.sum(jnp.exp(rollout), axis=0, keepdims=True))
    kl_ref[...] = jnp.sum(jnp.exp(rollout_log) * (rollout_log - current_log), axis=0, keepdims=True)
    ids = lax.broadcasted_iota(jnp.int32, (experts, rows), 0)
    picked = jnp.zeros((experts, rows), jnp.float32)
    for k in range(routes_ref.shape[0]):
        picked = picked + jnp.where(routes_ref[k : k + 1, :] == ids, 1.0, 0.0)
    chosen = jnp.where(picked > 0.0, raised, 0.0)
    gates = (chosen / jnp.sum(chosen, axis=0, keepdims=True)).astype(jnp.bfloat16)
    lanes = payload_ref.shape[1] - width
    spread = (
        lax.broadcasted_iota(jnp.int32, (experts, lanes), 0)
        == lax.broadcasted_iota(jnp.int32, (experts, lanes), 1)
    ).astype(jnp.float32).astype(jnp.bfloat16)
    payload_ref[:, width:] = lax.dot_general(
        gates, spread, (((0,), (0,)), ((), ())), preferred_element_type=jnp.float32
    ).astype(jnp.bfloat16)


VMEM = pl.BlockSpec(memory_space=pltpu.VMEM)
SMEM = pl.BlockSpec(memory_space=pltpu.SMEM)


HBM = pl.BlockSpec(memory_space=pltpu.HBM)
GRANT = 60 * 1024 * 1024
LEAN_GRANT = 24 * 1024 * 1024


def fetching(kernel, count, stored, index_ref, *refs):
    inputs, refs = refs[:count], refs[count:]
    outputs, refs = refs[: len(stored)], refs[len(stored) :]
    held, refs = refs[:count], refs[count:]
    sent, refs = refs[: sum(stored)], refs[sum(stored) :]
    arrived, left, scratch = refs[0], refs[1], refs[2:]
    copies = [
        pltpu.make_async_copy(source, target, arrived.at[i])
        for i, (source, target) in enumerate(zip(inputs, held))
    ]
    for copy in copies:
        copy.start()
    for copy in copies:
        copy.wait()
    sent = iter(sent)
    built, copies = [], []
    for output, far in zip(outputs, stored):
        built.append(next(sent) if far else output)
        if far:
            copies.append(pltpu.make_async_copy(built[-1], output, left.at[len(copies)]))
    kernel(index_ref, *held, *built, *scratch)
    for copy in copies:
        copy.start()
    for copy in copies:
        copy.wait()


def small_kernel(kernel, out_shape, inputs, stored, scratch=(), moved=0):
    held = [pltpu.VMEM(array.shape, array.dtype) for array in inputs[1:]]
    sent = [pltpu.VMEM(leaf.shape, leaf.dtype) for leaf, far in zip(out_shape, stored) if far]
    return pl.pallas_call(
        functools.partial(fetching, kernel, len(held), stored),
        out_shape=out_shape,
        in_specs=[SMEM] + [HBM] * len(held),
        out_specs=tuple(HBM if far else VMEM for far in stored),
        scratch_shapes=[
            *held,
            *sent,
            pltpu.SemaphoreType.DMA((len(held),)),
            pltpu.SemaphoreType.DMA((max(1, len(sent)),)),
            *scratch,
        ],
        compiler_params=pltpu.CompilerParams(vmem_limit_bytes=GRANT),
        cost_estimate=pl.CostEstimate(flops=0, bytes_accessed=moved, transcendentals=0),
    )(*inputs)


def fetched(sources, targets, arrived):
    copies = [
        pltpu.make_async_copy(source, target, arrived.at[i])
        for i, (source, target) in enumerate(zip(sources, targets))
    ]
    for copy in copies:
        copy.start()
    return copies


def hidden_kernel(width, *refs):
    parts = len(refs) - 8
    sources, refs = refs[: parts + 2], refs[parts + 2 :]
    inner_ref, spare_ref, own, other, tokens, arrived = refs
    rows = sources[2].shape[0]
    targets = [own, other] + [tokens.at[pl.ds(p * rows, rows), :] for p in range(parts)]
    copies = fetched(sources, targets, arrived)
    for copy in copies[:1] + copies[2:]:
        copy.wait()
    half = own.shape[1] // 2
    inner_ref[:, :half] = activate(
        jnp.dot(tokens[:, :width], own[...], preferred_element_type=jnp.float32)
    )
    spare_ref[...] = tokens[:, width:]
    copies[1].wait()
    inner_ref[:, half:] = activate(
        jnp.dot(tokens[:, :width], other[...], preferred_element_type=jnp.float32)
    )


def hidden_blocks(tokens, own_in, other_in):
    width, inner = own_in.shape
    rows, total = tokens[0].shape
    parts = len(tokens)
    return pl.pallas_call(
        functools.partial(hidden_kernel, width),
        out_shape=(
            jax.ShapeDtypeStruct((parts * rows, inner), jnp.bfloat16),
            jax.ShapeDtypeStruct((parts * rows, total - width), jnp.bfloat16),
        ),
        in_specs=[pl.BlockSpec(memory_space=pl.ANY)] * (parts + 2),
        out_specs=(VMEM, VMEM),
        scratch_shapes=[
            pltpu.VMEM(own_in.shape, own_in.dtype),
            pltpu.VMEM(own_in.shape, own_in.dtype),
            pltpu.VMEM((parts * rows, total), jnp.bfloat16),
            pltpu.SemaphoreType.DMA((parts + 2,)),
        ],
        compiler_params=pltpu.CompilerParams(vmem_limit_bytes=LEAN_GRANT),
        cost_estimate=pl.CostEstimate(flops=0, bytes_accessed=9 << 20, transcendentals=0),
    )(own_in, other_in, *tokens)


def output_kernel(index_ref, inner_ref, spare_ref, own_ref, other_ref, *refs):
    outputs, (inner, spare, weight, arrived) = refs[:-4], refs[-4:]
    depth = own_ref.shape[0]
    targets = [weight.at[pl.ds(0, depth), :], weight.at[pl.ds(depth, depth), :], inner, spare]
    for copy in fetched([own_ref, other_ref, inner_ref, spare_ref], targets, arrived):
        copy.wait()
    part = outputs[0].shape[0]
    step = 4 * part
    for start in reversed(range(0, inner.shape[0], step)):
        block = slice(start, start + step)
        chosen = spare[block, :].astype(jnp.float32)
        picked = lax.broadcasted_iota(jnp.int32, chosen.shape, 1) == index_ref[0]
        gate = jnp.sum(jnp.where(picked, chosen, 0.0), axis=1, keepdims=True)
        out = jnp.dot(inner[block, :], weight[...], preferred_element_type=jnp.float32)
        out = (out * gate).astype(jnp.bfloat16)
        for i in range(start // part, (start + step) // part):
            outputs[i][...] = out[i * part - start : (i + 1) * part - start]


def output_blocks(count, index, inner, spare, own_out, other_out):
    width = own_out.shape[1]
    rows = inner.shape[0]
    half = jax.ShapeDtypeStruct((rows // count // 2, width), jnp.bfloat16)
    flat = pl.pallas_call(
        output_kernel,
        out_shape=(half,) * (2 * count),
        in_specs=[SMEM] + [pl.BlockSpec(memory_space=pl.ANY)] * 4,
        out_specs=(VMEM,) * (2 * count),
        scratch_shapes=[
            pltpu.VMEM(inner.shape, inner.dtype),
            pltpu.VMEM(spare.shape, spare.dtype),
            pltpu.VMEM((inner.shape[1], width), jnp.bfloat16),
            pltpu.SemaphoreType.DMA((4,)),
        ],
        compiler_params=pltpu.CompilerParams(vmem_limit_bytes=LEAN_GRANT),
        cost_estimate=pl.CostEstimate(flops=0, bytes_accessed=0, transcendentals=0),
    )(index, inner, spare, own_out, other_out)
    return [flat[2 * k : 2 * k + 2] for k in range(count)]


def dense_body(
    hidden,
    queries,
    keys,
    values,
    positions,
    out_weight,
    ffn_gain,
    router_weight,
    routes,
    expert_in,
    expert_out,
    rollout_logits,
):
    block_rows = queries.shape[0]
    head_dim = queries.shape[1]
    width = hidden.shape[1]
    token_rows = hidden.shape[0]
    experts_total = router_weight.shape[1]
    ctx_index = lax.axis_index("ctx")
    exp_index = lax.axis_index("exp")
    exp_count = lax.axis_size("exp")
    kv_heads = keys.shape[1] // head_dim
    per_column = experts_total // exp_count
    share = exp_count // kv_heads
    bits = []
    step = exp_count // 2
    while step:
        bits.append(step)
        step //= 2

    weight_in = expert_in[0, 0]
    weight_out = expert_out[0, 0]
    kv_group = exp_index // share
    kv_own = jnp.concatenate(
        [lax.dynamic_slice_in_dim(array, kv_group * head_dim, head_dim, 1) for array in (keys, values)],
        axis=1,
    )
    before = passed_along(kv_own, "ctx", 1)
    before, weight_in_sent, weight_out_sent = lax.optimization_barrier((before, weight_in, weight_out))
    other_out = swapped(weight_out_sent, "ctx", 1)
    other_in = swapped(weight_in_sent, "ctx", 1)

    index = exp_index.reshape(1).astype(jnp.int32)
    owners = [0]
    for bit in bits:
        owners = owners + [owner ^ bit for owner in owners]
    turned_head = jax.ShapeDtypeStruct((block_rows, head_dim), jnp.bfloat16)
    table = jax.ShapeDtypeStruct((block_rows, head_dim), jnp.float32)
    rotated = small_kernel(
        rotation_kernel,
        (turned_head, turned_head, table, table),
        (index, positions[None, :], queries, kv_own),
        (True,) * 4,
        moved=20 << 20,
    )
    term = jax.ShapeDtypeStruct((token_rows, width), jnp.bfloat16)
    terms = small_kernel(
        functools.partial(attention_kernel, tuple(owners)),
        (term,) * exp_count,
        (index, positions[None, :], *rotated, before, kv_own, out_weight),
        (True,) * exp_count,
        (pltpu.VMEM((block_rows, head_dim), jnp.bfloat16),),
    )
    terms = [terms[0]] + [swapped(term, "exp", owner) for term, owner in zip(terms[1:], owners[1:])]
    lanes = -(-experts_total // 128) * 128
    attended, payload, router_kl = small_kernel(
        functools.partial(router_kernel, exp_count),
        (
            jax.ShapeDtypeStruct((token_rows, width), jnp.bfloat16),
            jax.ShapeDtypeStruct((token_rows, width + lanes), jnp.bfloat16),
            jax.ShapeDtypeStruct((1, token_rows), jnp.float32),
        ),
        (
            index,
            *terms,
            hidden,
            ffn_gain[None, :],
            router_weight.T,
            routes.T,
            rollout_logits.T,
        ),
        (False, True, False),
    )
    router_kl = router_kl[0]
    crossed, passed = {}, None
    for k in sorted(range(per_column), key=lambda k: (k.bit_count(), -k)):
        low = k & -k
        if k != low:
            crossed[k] = [swapped(part, "ctx", 2 * low) for part in crossed[k ^ low]]
            continue
        parts = [payload if k == 0 else swapped(payload, "ctx", 2 * k)]
        for bit in bits[:-1]:
            if k > 0:
                passed, *parts = lax.optimization_barrier((passed, *parts))
            parts = parts + [swapped(part, "exp", bit) for part in parts]
        passed = parts[-1]
        crossed[k] = parts
    crossed = [crossed[k] for k in range(per_column)]
    expert_index = (exp_index * per_column + ctx_index // 2).reshape(1).astype(jnp.int32)
    groups, pairs, tokens = 1, [], []
    for turn, parts in enumerate(crossed):
        stack = jnp.concatenate(parts, axis=0)
        if turn == per_column // 2:
            stack, other_in = lax.optimization_barrier((stack, other_in))
        tokens = tokens + [stack, swapped(stack, "exp", bits[-1])]
        if (turn + 1) % (per_column // groups) == 0:
            pairs.append(hidden_blocks(tokens, weight_in, other_in))
            tokens = []
    inner, spare = pairs[0]
    inner, other_out = lax.optimization_barrier((inner, other_out))
    partials = output_blocks(per_column, expert_index, inner, spare, weight_out, other_out)
    returned = {}
    for k in reversed(range(per_column)):
        keep, send = partials[k]
        for bit in reversed(bits):
            if bit == bits[0] and k == 0 and per_column > 2:
                send, returned[2] = lax.optimization_barrier((send, returned[2]))
            received = swapped(send, "exp", bit)
            total = keep.astype(jnp.float32) + received.astype(jnp.float32)
            total = total.astype(jnp.bfloat16)
            middle = total.shape[0] // 2
            keep, send = total[:middle], total[middle:]
        returned[k] = total
    returned = {k: total if k == 0 else swapped(total, "ctx", 2 * k) for k, total in returned.items()}
    moe_out = sum(returned[k].astype(jnp.float32) for k in range(per_column))
    layer_out = (attended.astype(jnp.float32) + moe_out).astype(jnp.bfloat16)
    return (layer_out, router_kl)


def powers_of_two(*counts):
    return all(count & (count - 1) == 0 for count in counts)


def body(*arrays):
    experts_total = arrays[7].shape[1]
    exp_count, ctx_count = lax.axis_size("exp"), lax.axis_size("ctx")
    dense = experts_total <= 2 * arrays[8].shape[1] and powers_of_two(exp_count, ctx_count)
    return (dense_body if dense else sparse_body)(*arrays)


def solution(mesh):
    return jax.shard_map(
        body,
        mesh=mesh,
        in_specs=(
            P(("group", "ctx", "exp"), None),
            P(("group", "ctx"), "exp"),
            P(("group", "ctx"), None),
            P(("group", "ctx"), None),
            P(("group", "ctx")),
            P("exp", None),
            P(),
            P(),
            P(("group", "ctx", "exp"), None),
            P("ctx", "exp", None, None),
            P("ctx", "exp", None, None),
            P(("group", "ctx", "exp"), None),
        ),
        out_specs=(P(("group", "ctx", "exp"), None), P(("group", "ctx", "exp"))),
        check_vma=False,
    )
```

```python
import functools
import math

import jax
import jax.numpy as jnp
import numpy as np
from jax import lax
from jax.experimental import pallas as pl
from jax.experimental.pallas import tpu as pltpu
from jax.sharding import PartitionSpec as P

eps = 1e-06
theta = 1000000.0


def passed_along(value, axis, steps):
    count = lax.axis_size(axis)
    initial, last = (max(0, -steps), min(count, count - steps))
    return lax.ppermute(value, axis, [(source, source + steps) for source in range(initial, last)])


def frequencies(head_dim):
    return theta ** (-jnp.arange(head_dim // 2, dtype=jnp.float32) * 2.0 / head_dim)


def head_norm(values_in):
    widened = values_in.astype(jnp.float32)
    return widened / jnp.sqrt(jnp.mean(widened * widened, axis=-1, keepdims=True) + eps)


def rotate(vectors, angle):
    middle = vectors.shape[-1] // 2
    cosine = jnp.cos(angle)
    sine_part = jnp.sin(angle)
    leading = vectors[..., :middle]
    trailing = vectors[..., middle:]
    return jnp.concatenate(
        [leading * cosine - trailing * sine_part, trailing * cosine + leading * sine_part], axis=-1
    )


def activate(act):
    inner = act.shape[1] // 2
    return (jax.nn.silu(act[:, :inner]) * act[:, inner:]).astype(jnp.bfloat16)


def sparse_body(
    hidden,
    queries,
    keys,
    values,
    positions,
    out_weight,
    ffn_gain,
    router_weight,
    routes,
    expert_in,
    expert_out,
    rollout_logits,
):
    block_rows = queries.shape[0]
    head_dim = queries.shape[1]
    width = hidden.shape[1]
    token_rows = hidden.shape[0]
    top_count = routes.shape[1]
    experts_total = router_weight.shape[1]
    ctx_index = lax.axis_index("ctx")
    exp_index = lax.axis_index("exp")
    ctx_count = lax.axis_size("ctx")
    exp_count = lax.axis_size("exp")
    kv_heads = keys.shape[1] // head_dim
    kv_group = exp_index // (exp_count // kv_heads)
    angle = positions.astype(jnp.float32)[:, None] * frequencies(head_dim)[None, :]
    query_rot = rotate(head_norm(queries), angle).astype(jnp.bfloat16)
    key_own = rotate(
        head_norm(lax.dynamic_slice_in_dim(keys, kv_group * head_dim, head_dim, 1)), angle
    ).astype(jnp.bfloat16)
    value_own = lax.dynamic_slice_in_dim(values, kv_group * head_dim, head_dim, 1)
    key_before, value_before = passed_along((key_own, value_own), "ctx", 1)
    key_window = jnp.concatenate([key_before, key_own], axis=0)
    value_window = jnp.concatenate([value_before, value_own], axis=0)
    scores = lax.dot_general(
        query_rot, key_window, (((1,), (1,)), ((), ())), preferred_element_type=jnp.float32
    )
    scores = scores / jnp.sqrt(jnp.float32(head_dim))
    query_at = ctx_index * block_rows + jnp.arange(block_rows, dtype=jnp.int32)
    key_at = ctx_index * block_rows - block_rows + jnp.arange(2 * block_rows, dtype=jnp.int32)
    allowed = (key_at[None, :] <= query_at[:, None]) & (
        key_at[None, :] >= (query_at - positions)[:, None]
    )
    raw = jnp.where(allowed, jnp.exp(scores), 0.0)
    weights = (raw / jnp.sum(raw, axis=1, keepdims=True)).astype(jnp.bfloat16)
    head_out = jnp.dot(weights, value_window, preferred_element_type=jnp.float32).astype(
        jnp.bfloat16
    )
    term = jnp.dot(head_out, out_weight, preferred_element_type=jnp.float32).astype(jnp.bfloat16)
    summed = lax.psum_scatter(
        lax.optimization_barrier(term).astype(jnp.float32).astype(jnp.bfloat16),
        "exp",
        scatter_dimension=0,
        tiled=True,
    ).astype(jnp.float32)
    attended = (hidden.astype(jnp.float32) + summed).astype(jnp.bfloat16)
    widened = attended.astype(jnp.float32)
    moe_in = (
        widened
        / jnp.sqrt(jnp.mean(widened * widened, axis=1, keepdims=True) + eps)
        * ffn_gain[None, :]
    ).astype(jnp.bfloat16)
    router_logits = jnp.dot(moe_in, router_weight, preferred_element_type=jnp.float32)
    current_logprob = router_logits - jnp.log(
        jnp.sum(jnp.exp(router_logits), axis=1, keepdims=True)
    )
    rollout_logprob = rollout_logits - jnp.log(
        jnp.sum(jnp.exp(rollout_logits), axis=1, keepdims=True)
    )
    router_kl = jnp.sum(jnp.exp(rollout_logprob) * (rollout_logprob - current_logprob), axis=1)
    expert_ids = jnp.arange(experts_total, dtype=jnp.int32)
    picked = routes[:, :, None] == expert_ids[None, None, :]
    chosen_logits = jnp.sum(jnp.where(picked, router_logits[:, None, :], 0.0), axis=2)
    gate_raw = jnp.exp(chosen_logits)
    gates = (gate_raw / jnp.sum(gate_raw, axis=1, keepdims=True)).astype(jnp.bfloat16)
    capacity = min(token_rows, max(2, 3 * token_rows * top_count // (2 * experts_total)))
    per_column = experts_total // exp_count
    slots_total = experts_total * capacity
    flat_routes = routes.reshape(-1)
    member = (flat_routes[:, None] == expert_ids[None, :]).astype(jnp.int32)
    earlier = jnp.cumsum(member, axis=0) - member
    slot_rank = jnp.sum(earlier * member, axis=1)
    target = (
        flat_routes % per_column * exp_count + flat_routes // per_column
    ) * capacity + slot_rank
    target_grid = target.reshape(token_rows, top_count)
    slot_ids = jnp.arange(slots_total, dtype=jnp.int32)
    placing = jnp.any(target_grid[None, :, :] == slot_ids[:, None, None], axis=2).astype(
        jnp.bfloat16
    )
    gate_grid = jnp.where(
        target_grid[:, :, None] == slot_ids[None, None, :], gates[:, :, None], jnp.bfloat16(0)
    )
    combining = jnp.sum(gate_grid.astype(jnp.float32), axis=1).astype(jnp.bfloat16)
    weight_in = expert_in[0, 0]
    weight_out = expert_out[0, 0]
    packed = jnp.dot(placing, moe_in, preferred_element_type=jnp.float32).astype(jnp.bfloat16)
    packed = packed.reshape(per_column, 1, exp_count, capacity, width)
    doubled = jnp.broadcast_to(packed, (per_column, 2, exp_count, capacity, width)).reshape(
        ctx_count, exp_count, capacity, width
    )
    arrived = lax.all_to_all(
        lax.all_to_all(doubled, "ctx", split_axis=0, concat_axis=0, tiled=True),
        "exp",
        split_axis=1,
        concat_axis=1,
        tiled=True,
    )
    act = jnp.dot(arrived.reshape(-1, width), weight_in, preferred_element_type=jnp.float32)
    partial_value = jnp.dot(activate(act), weight_out, preferred_element_type=jnp.float32).astype(
        jnp.bfloat16
    )
    returned = lax.all_to_all(
        lax.all_to_all(
            partial_value.reshape(ctx_count, exp_count, capacity, width),
            "ctx",
            split_axis=0,
            concat_axis=0,
            tiled=True,
        ),
        "exp",
        split_axis=1,
        concat_axis=1,
        tiled=True,
    )
    paired = returned.reshape(per_column, 2, exp_count * capacity, width).astype(jnp.float32)
    expert_output = (paired[:, 0] + paired[:, 1]).astype(jnp.bfloat16).reshape(slots_total, width)
    moe_out = jnp.dot(combining, expert_output, preferred_element_type=jnp.float32)
    layer_out = (attended.astype(jnp.float32) + moe_out).astype(jnp.bfloat16)
    return (layer_out, router_kl)


def swapped(value, axis, mask):
    count = lax.axis_size(axis)
    return lax.ppermute(value, axis, [(source, source ^ mask) for source in range(count)])


def column_of(row):
    count = row.shape[1]
    along = lax.broadcasted_iota(jnp.int32, (count, count), 0)
    across = lax.broadcasted_iota(jnp.int32, (count, count), 1)
    return jnp.sum(jnp.where(along == across, row, 0.0), axis=1, keepdims=True)


def turned(vectors, cosine, sine):
    wide = vectors.astype(jnp.float32)
    wide = wide * lax.rsqrt(jnp.mean(wide * wide, axis=1, keepdims=True) + eps)
    return (wide * cosine + pltpu.roll(wide, wide.shape[1] // 2, 1) * sine).astype(jnp.bfloat16)


def rotation_kernel(index_ref, pos_ref, q_ref, own_ref, query_ref, key_ref, cos_ref, sin_ref):
    block, size = q_ref.shape
    pos_row = pos_ref[...].astype(jnp.float32)
    pos_col = column_of(pos_row)
    first = lax.broadcasted_iota(jnp.int32, (1, block), 1) == 0
    opening = jnp.sum(jnp.where(first, pos_row, 0.0), axis=1, keepdims=True)
    earlier = opening - block + lax.broadcasted_iota(jnp.int32, (block, 1), 0).astype(jnp.float32)
    lane = lax.broadcasted_iota(jnp.int32, (1, size), 1)
    lower = lane < size // 2
    phase = jnp.where(lower, 0.0, math.pi / 2)
    turn_of = jnp.where(lower, lane, lane - size // 2).astype(jnp.float32)
    spectrum = jnp.exp(turn_of * (-2.0 * math.log(theta) / size))

    def table(at):
        turn = jnp.cos(at * spectrum - phase)
        swap = pltpu.roll(turn, size // 2, 1)
        return jnp.where(lower, turn, swap), jnp.where(lower, -swap, turn)

    cosine, sine = table(pos_col)
    query_ref[...] = turned(q_ref[...], cosine, sine)
    key_ref[...] = turned(own_ref[:, :size], cosine, sine)
    cos_ref[...], sin_ref[...] = table(earlier)


def attention_kernel(order, index_ref, pos_ref, query_ref, key_ref, cos_ref, sin_ref, before_ref, own_ref, *refs):
    weight_ref, outputs, mixed = refs[0], refs[1:-1], refs[-1]
    block, size = query_ref.shape
    rows = block // len(order)
    pos_col = column_of(pos_ref[...].astype(jnp.float32))
    query_at = lax.broadcasted_iota(jnp.int32, (block, 2 * block), 0)
    key_at = lax.broadcasted_iota(jnp.int32, (block, 2 * block), 1) - block
    allowed = (key_at <= query_at) & (key_at >= query_at - pos_col.astype(jnp.int32))
    keys = jnp.concatenate(
        [turned(before_ref[:, :size], cos_ref[...], sin_ref[...]), key_ref[...]], axis=0
    )
    values = jnp.concatenate([before_ref[:, size:], own_ref[:, size:]], axis=0)
    scores = lax.dot_general(
        query_ref[...], keys, (((1,), (1,)), ((), ())), preferred_element_type=jnp.float32
    ) * (1.0 / math.sqrt(size))
    raw = jnp.where(allowed, jnp.exp(scores), 0.0)
    weights = (raw / jnp.sum(raw, axis=1, keepdims=True)).astype(jnp.bfloat16)
    mixed[...] = jnp.dot(weights, values, preferred_element_type=jnp.float32).astype(jnp.bfloat16)
    picked = [
        mixed[pl.ds(pl.multiple_of((index_ref[0] ^ owner) * rows, 16), rows), :] for owner in order
    ]
    term = jnp.dot(
        jnp.concatenate(picked, axis=0), weight_ref[...], preferred_element_type=jnp.float32
    ).astype(jnp.bfloat16)
    for i, output in enumerate(outputs):
        output[...] = term[i * rows : (i + 1) * rows]


def router_kernel(heads, index_ref, *refs):
    terms, refs = refs[:heads], refs[heads:]
    hidden_ref, gain_ref, router_ref, routes_ref, rollout_ref = refs[:5]
    attended_ref, payload_ref, kl_ref = refs[5:]
    width = hidden_ref.shape[1]
    experts, rows = rollout_ref.shape
    total = sum(term[...].astype(jnp.float32) for term in terms) + hidden_ref[...].astype(jnp.float32)
    attended = total.astype(jnp.bfloat16)
    attended_ref[...] = attended
    wide = attended.astype(jnp.float32)
    moe_in = (
        wide * lax.rsqrt(jnp.mean(wide * wide, axis=1, keepdims=True) + eps) * gain_ref[...]
    ).astype(jnp.bfloat16)
    payload_ref[:, :width] = moe_in
    logits = lax.dot_general(
        router_ref[...], moe_in, (((1,), (1,)), ((), ())), preferred_element_type=jnp.float32
    )
    raised = jnp.exp(logits)
    rollout = rollout_ref[...]
    current_log = logits - jnp.log(jnp.sum(raised, axis=0, keepdims=True))
    rollout_log = rollout - jnp.log(jnp.sum(jnp.exp(rollout), axis=0, keepdims=True))
    kl_ref[...] = jnp.sum(jnp.exp(rollout_log) * (rollout_log - current_log), axis=0, keepdims=True)
    ids = lax.broadcasted_iota(jnp.int32, (experts, rows), 0)
    picked = jnp.zeros((experts, rows), jnp.float32)
    for k in range(routes_ref.shape[0]):
        picked = picked + jnp.where(routes_ref[k : k + 1, :] == ids, 1.0, 0.0)
    chosen = jnp.where(picked > 0.0, raised, 0.0)
    gates = (chosen / jnp.sum(chosen, axis=0, keepdims=True)).astype(jnp.bfloat16)
    lanes = payload_ref.shape[1] - width
    spread = (
        lax.broadcasted_iota(jnp.int32, (experts, lanes), 0)
        == lax.broadcasted_iota(jnp.int32, (experts, lanes), 1)
    ).astype(jnp.float32).astype(jnp.bfloat16)
    payload_ref[:, width:] = lax.dot_general(
        gates, spread, (((0,), (0,)), ((), ())), preferred_element_type=jnp.float32
    ).astype(jnp.bfloat16)


VMEM = pl.BlockSpec(memory_space=pltpu.VMEM)
SMEM = pl.BlockSpec(memory_space=pltpu.SMEM)


HBM = pl.BlockSpec(memory_space=pltpu.HBM)
GRANT = 60 * 1024 * 1024
LEAN_GRANT = 24 * 1024 * 1024


def fetching(kernel, count, stored, index_ref, *refs):
    inputs, refs = refs[:count], refs[count:]
    outputs, refs = refs[: len(stored)], refs[len(stored) :]
    held, refs = refs[:count], refs[count:]
    sent, refs = refs[: sum(stored)], refs[sum(stored) :]
    arrived, left, scratch = refs[0], refs[1], refs[2:]
    copies = [
        pltpu.make_async_copy(source, target, arrived.at[i])
        for i, (source, target) in enumerate(zip(inputs, held))
    ]
    for copy in copies:
        copy.start()
    for copy in copies:
        copy.wait()
    sent = iter(sent)
    built, copies = [], []
    for output, far in zip(outputs, stored):
        built.append(next(sent) if far else output)
        if far:
            copies.append(pltpu.make_async_copy(built[-1], output, left.at[len(copies)]))
    kernel(index_ref, *held, *built, *scratch)
    for copy in copies:
        copy.start()
    for copy in copies:
        copy.wait()


def small_kernel(kernel, out_shape, inputs, stored, scratch=(), moved=0):
    held = [pltpu.VMEM(array.shape, array.dtype) for array in inputs[1:]]
    sent = [pltpu.VMEM(leaf.shape, leaf.dtype) for leaf, far in zip(out_shape, stored) if far]
    return pl.pallas_call(
        functools.partial(fetching, kernel, len(held), stored),
        out_shape=out_shape,
        in_specs=[SMEM] + [HBM] * len(held),
        out_specs=tuple(HBM if far else VMEM for far in stored),
        scratch_shapes=[
            *held,
            *sent,
            pltpu.SemaphoreType.DMA((len(held),)),
            pltpu.SemaphoreType.DMA((max(1, len(sent)),)),
            *scratch,
        ],
        compiler_params=pltpu.CompilerParams(vmem_limit_bytes=GRANT),
        cost_estimate=pl.CostEstimate(flops=0, bytes_accessed=moved, transcendentals=0),
    )(*inputs)


def fetched(sources, targets, arrived):
    copies = [
        pltpu.make_async_copy(source, target, arrived.at[i])
        for i, (source, target) in enumerate(zip(sources, targets))
    ]
    for copy in copies:
        copy.start()
    return copies


def hidden_kernel(width, *refs):
    parts = len(refs) - 8
    sources, refs = refs[: parts + 2], refs[parts + 2 :]
    inner_ref, spare_ref, own, other, tokens, arrived = refs
    rows = sources[2].shape[0]
    targets = [own, other] + [tokens.at[pl.ds(p * rows, rows), :] for p in range(parts)]
    copies = fetched(sources, targets, arrived)
    for copy in copies[:1] + copies[2:]:
        copy.wait()
    half = own.shape[1] // 2
    inner_ref[:, :half] = activate(
        jnp.dot(tokens[:, :width], own[...], preferred_element_type=jnp.float32)
    )
    spare_ref[...] = tokens[:, width:]
    copies[1].wait()
    inner_ref[:, half:] = activate(
        jnp.dot(tokens[:, :width], other[...], preferred_element_type=jnp.float32)
    )


def hidden_blocks(tokens, own_in, other_in):
    width, inner = own_in.shape
    rows, total = tokens[0].shape
    parts = len(tokens)
    return pl.pallas_call(
        functools.partial(hidden_kernel, width),
        out_shape=(
            jax.ShapeDtypeStruct((parts * rows, inner), jnp.bfloat16),
            jax.ShapeDtypeStruct((parts * rows, total - width), jnp.bfloat16),
        ),
        in_specs=[pl.BlockSpec(memory_space=pl.ANY)] * (parts + 2),
        out_specs=(VMEM, VMEM),
        scratch_shapes=[
            pltpu.VMEM(own_in.shape, own_in.dtype),
            pltpu.VMEM(own_in.shape, own_in.dtype),
            pltpu.VMEM((parts * rows, total), jnp.bfloat16),
            pltpu.SemaphoreType.DMA((parts + 2,)),
        ],
        compiler_params=pltpu.CompilerParams(vmem_limit_bytes=LEAN_GRANT),
        cost_estimate=pl.CostEstimate(flops=0, bytes_accessed=9 << 20, transcendentals=0),
    )(own_in, other_in, *tokens)


def output_kernel(index_ref, inner_ref, spare_ref, own_ref, other_ref, *refs):
    outputs, (inner, spare, weight, arrived) = refs[:-4], refs[-4:]
    depth = own_ref.shape[0]
    targets = [weight.at[pl.ds(0, depth), :], weight.at[pl.ds(depth, depth), :], inner, spare]
    for copy in fetched([own_ref, other_ref, inner_ref, spare_ref], targets, arrived):
        copy.wait()
    part = outputs[0].shape[0]
    step = 4 * part
    for start in reversed(range(0, inner.shape[0], step)):
        block = slice(start, start + step)
        chosen = spare[block, :].astype(jnp.float32)
        picked = lax.broadcasted_iota(jnp.int32, chosen.shape, 1) == index_ref[0]
        gate = jnp.sum(jnp.where(picked, chosen, 0.0), axis=1, keepdims=True)
        out = jnp.dot(inner[block, :], weight[...], preferred_element_type=jnp.float32)
        out = (out * gate).astype(jnp.bfloat16)
        for i in range(start // part, (start + step) // part):
            outputs[i][...] = out[i * part - start : (i + 1) * part - start]


def output_blocks(count, index, inner, spare, own_out, other_out):
    width = own_out.shape[1]
    rows = inner.shape[0]
    half = jax.ShapeDtypeStruct((rows // count // 2, width), jnp.bfloat16)
    flat = pl.pallas_call(
        output_kernel,
        out_shape=(half,) * (2 * count),
        in_specs=[SMEM] + [pl.BlockSpec(memory_space=pl.ANY)] * 4,
        out_specs=(VMEM,) * (2 * count),
        scratch_shapes=[
            pltpu.VMEM(inner.shape, inner.dtype),
            pltpu.VMEM(spare.shape, spare.dtype),
            pltpu.VMEM((inner.shape[1], width), jnp.bfloat16),
            pltpu.SemaphoreType.DMA((4,)),
        ],
        compiler_params=pltpu.CompilerParams(vmem_limit_bytes=LEAN_GRANT),
        cost_estimate=pl.CostEstimate(flops=0, bytes_accessed=0, transcendentals=0),
    )(index, inner, spare, own_out, other_out)
    return [flat[2 * k : 2 * k + 2] for k in range(count)]


def dense_body(
    hidden,
    queries,
    keys,
    values,
    positions,
    out_weight,
    ffn_gain,
    router_weight,
    routes,
    expert_in,
    expert_out,
    rollout_logits,
):
    block_rows = queries.shape[0]
    head_dim = queries.shape[1]
    width = hidden.shape[1]
    token_rows = hidden.shape[0]
    experts_total = router_weight.shape[1]
    ctx_index = lax.axis_index("ctx")
    exp_index = lax.axis_index("exp")
    exp_count = lax.axis_size("exp")
    kv_heads = keys.shape[1] // head_dim
    per_column = experts_total // exp_count
    share = exp_count // kv_heads
    bits = []
    step = exp_count // 2
    while step:
        bits.append(step)
        step //= 2

    weight_in = expert_in[0, 0]
    weight_out = expert_out[0, 0]
    kv_group = exp_index // share
    kv_own = jnp.concatenate(
        [lax.dynamic_slice_in_dim(array, kv_group * head_dim, head_dim, 1) for array in (keys, values)],
        axis=1,
    )
    before = passed_along(kv_own, "ctx", 1)
    before, weight_in_sent, weight_out_sent = lax.optimization_barrier((before, weight_in, weight_out))
    other_out = swapped(weight_out_sent, "ctx", 1)
    other_in = swapped(weight_in_sent, "ctx", 1)

    index = exp_index.reshape(1).astype(jnp.int32)
    owners = [0]
    for bit in bits:
        owners = owners + [owner ^ bit for owner in owners]
    turned_head = jax.ShapeDtypeStruct((block_rows, head_dim), jnp.bfloat16)
    table = jax.ShapeDtypeStruct((block_rows, head_dim), jnp.float32)
    rotated = small_kernel(
        rotation_kernel,
        (turned_head, turned_head, table, table),
        (index, positions[None, :], queries, kv_own),
        (True,) * 4,
        moved=20 << 20,
    )
    term = jax.ShapeDtypeStruct((token_rows, width), jnp.bfloat16)
    terms = small_kernel(
        functools.partial(attention_kernel, tuple(owners)),
        (term,) * exp_count,
        (index, positions[None, :], *rotated, before, kv_own, out_weight),
        (True,) * exp_count,
        (pltpu.VMEM((block_rows, head_dim), jnp.bfloat16),),
    )
    terms = [terms[0]] + [swapped(term, "exp", owner) for term, owner in zip(terms[1:], owners[1:])]
    lanes = -(-experts_total // 128) * 128
    attended, payload, router_kl = small_kernel(
        functools.partial(router_kernel, exp_count),
        (
            jax.ShapeDtypeStruct((token_rows, width), jnp.bfloat16),
            jax.ShapeDtypeStruct((token_rows, width + lanes), jnp.bfloat16),
            jax.ShapeDtypeStruct((1, token_rows), jnp.float32),
        ),
        (
            index,
            *terms,
            hidden,
            ffn_gain[None, :],
            router_weight.T,
            routes.T,
            rollout_logits.T,
        ),
        (False, True, False),
    )
    router_kl = router_kl[0]
    crossed, passed = {}, None
    for k in sorted(range(per_column), key=lambda k: (k.bit_count(), -k)):
        low = k & -k
        if k != low:
            crossed[k] = [swapped(part, "ctx", 2 * low) for part in crossed[k ^ low]]
            continue
        parts = [payload if k == 0 else swapped(payload, "ctx", 2 * k)]
        for bit in bits[:-1]:
            if k > 0:
                passed, *parts = lax.optimization_barrier((passed, *parts))
            parts = parts + [swapped(part, "exp", bit) for part in parts]
        passed = parts[-1]
        crossed[k] = parts
    crossed = [crossed[k] for k in range(per_column)]
    expert_index = (exp_index * per_column + ctx_index // 2).reshape(1).astype(jnp.int32)
    groups, pairs, tokens = 1, [], []
    for turn, parts in enumerate(crossed):
        stack = jnp.concatenate(parts, axis=0)
        if turn == per_column // 2:
            stack, other_in = lax.optimization_barrier((stack, other_in))
        tokens = tokens + [stack, swapped(stack, "exp", bits[-1])]
        if (turn + 1) % (per_column // groups) == 0:
            pairs.append(hidden_blocks(tokens, weight_in, other_in))
            tokens = []
    inner, spare = pairs[0]
    inner, other_out = lax.optimization_barrier((inner, other_out))
    partials = output_blocks(per_column, expert_index, inner, spare, weight_out, other_out)
    returned, arrived = {}, []
    for k in sorted(range(per_column), key=lambda k: -k):
        keep, send = partials[k]
        for bit in reversed(bits):
            if bit == bits[0] and k < 2 and per_column > 2:
                returned[per_column - 1], send = lax.optimization_barrier((returned[per_column - 1], send))
            received = swapped(send, "exp", bit)
            total = keep.astype(jnp.float32) + received.astype(jnp.float32)
            total = total.astype(jnp.bfloat16)
            middle = total.shape[0] // 2
            keep, send = total[:middle], total[middle:]
        returned[k] = total
    step = 1
    while step < per_column:
        for k in reversed(range(0, per_column, step)):
            if k & step:
                came = swapped(returned[k], "ctx", 2 * step).astype(jnp.float32)
                if k == step:
                    arrived.append(came)
                else:
                    returned[k ^ step] = (returned[k ^ step].astype(jnp.float32) + came).astype(jnp.bfloat16)
        step *= 2
    moe_out = returned[0].astype(jnp.float32) + sum(arrived)
    layer_out = (attended.astype(jnp.float32) + moe_out).astype(jnp.bfloat16)
    return (layer_out, router_kl)


def powers_of_two(*counts):
    return all(count & (count - 1) == 0 for count in counts)


def body(*arrays):
    experts_total = arrays[7].shape[1]
    exp_count, ctx_count = lax.axis_size("exp"), lax.axis_size("ctx")
    dense = experts_total <= 2 * arrays[8].shape[1] and powers_of_two(exp_count, ctx_count)
    return (dense_body if dense else sparse_body)(*arrays)


def solution(mesh):
    return jax.shard_map(
        body,
        mesh=mesh,
        in_specs=(
            P(("group", "ctx", "exp"), None),
            P(("group", "ctx"), "exp"),
            P(("group", "ctx"), None),
            P(("group", "ctx"), None),
            P(("group", "ctx")),
            P("exp", None),
            P(),
            P(),
            P(("group", "ctx", "exp"), None),
            P("ctx", "exp", None, None),
            P("ctx", "exp", None, None),
            P(("group", "ctx", "exp"), None),
        ),
        out_specs=(P(("group", "ctx", "exp"), None), P(("group", "ctx", "exp"))),
        check_vma=False,
    )
```

```python
import functools
import math

import jax
import jax.numpy as jnp
import numpy as np
from jax import lax
from jax.experimental import pallas as pl
from jax.experimental.pallas import tpu as pltpu
from jax.sharding import PartitionSpec as P

eps = 1e-06
theta = 1000000.0


def passed_along(value, axis, steps):
    count = lax.axis_size(axis)
    initial, last = (max(0, -steps), min(count, count - steps))
    return lax.ppermute(value, axis, [(source, source + steps) for source in range(initial, last)])


def frequencies(head_dim):
    return theta ** (-jnp.arange(head_dim // 2, dtype=jnp.float32) * 2.0 / head_dim)


def head_norm(values_in):
    widened = values_in.astype(jnp.float32)
    return widened / jnp.sqrt(jnp.mean(widened * widened, axis=-1, keepdims=True) + eps)


def rotate(vectors, angle):
    middle = vectors.shape[-1] // 2
    cosine = jnp.cos(angle)
    sine_part = jnp.sin(angle)
    leading = vectors[..., :middle]
    trailing = vectors[..., middle:]
    return jnp.concatenate(
        [leading * cosine - trailing * sine_part, trailing * cosine + leading * sine_part], axis=-1
    )


def activate(act):
    inner = act.shape[1] // 2
    return (jax.nn.silu(act[:, :inner]) * act[:, inner:]).astype(jnp.bfloat16)


def sparse_body(
    hidden,
    queries,
    keys,
    values,
    positions,
    out_weight,
    ffn_gain,
    router_weight,
    routes,
    expert_in,
    expert_out,
    rollout_logits,
):
    block_rows = queries.shape[0]
    head_dim = queries.shape[1]
    width = hidden.shape[1]
    token_rows = hidden.shape[0]
    top_count = routes.shape[1]
    experts_total = router_weight.shape[1]
    ctx_index = lax.axis_index("ctx")
    exp_index = lax.axis_index("exp")
    ctx_count = lax.axis_size("ctx")
    exp_count = lax.axis_size("exp")
    kv_heads = keys.shape[1] // head_dim
    kv_group = exp_index // (exp_count // kv_heads)
    angle = positions.astype(jnp.float32)[:, None] * frequencies(head_dim)[None, :]
    query_rot = rotate(head_norm(queries), angle).astype(jnp.bfloat16)
    key_own = rotate(
        head_norm(lax.dynamic_slice_in_dim(keys, kv_group * head_dim, head_dim, 1)), angle
    ).astype(jnp.bfloat16)
    value_own = lax.dynamic_slice_in_dim(values, kv_group * head_dim, head_dim, 1)
    key_before, value_before = passed_along((key_own, value_own), "ctx", 1)
    key_window = jnp.concatenate([key_before, key_own], axis=0)
    value_window = jnp.concatenate([value_before, value_own], axis=0)
    scores = lax.dot_general(
        query_rot, key_window, (((1,), (1,)), ((), ())), preferred_element_type=jnp.float32
    )
    scores = scores / jnp.sqrt(jnp.float32(head_dim))
    query_at = ctx_index * block_rows + jnp.arange(block_rows, dtype=jnp.int32)
    key_at = ctx_index * block_rows - block_rows + jnp.arange(2 * block_rows, dtype=jnp.int32)
    allowed = (key_at[None, :] <= query_at[:, None]) & (
        key_at[None, :] >= (query_at - positions)[:, None]
    )
    raw = jnp.where(allowed, jnp.exp(scores), 0.0)
    weights = (raw / jnp.sum(raw, axis=1, keepdims=True)).astype(jnp.bfloat16)
    head_out = jnp.dot(weights, value_window, preferred_element_type=jnp.float32).astype(
        jnp.bfloat16
    )
    term = jnp.dot(head_out, out_weight, preferred_element_type=jnp.float32).astype(jnp.bfloat16)
    summed = lax.psum_scatter(
        lax.optimization_barrier(term).astype(jnp.float32).astype(jnp.bfloat16),
        "exp",
        scatter_dimension=0,
        tiled=True,
    ).astype(jnp.float32)
    attended = (hidden.astype(jnp.float32) + summed).astype(jnp.bfloat16)
    widened = attended.astype(jnp.float32)
    moe_in = (
        widened
        / jnp.sqrt(jnp.mean(widened * widened, axis=1, keepdims=True) + eps)
        * ffn_gain[None, :]
    ).astype(jnp.bfloat16)
    router_logits = jnp.dot(moe_in, router_weight, preferred_element_type=jnp.float32)
    current_logprob = router_logits - jnp.log(
        jnp.sum(jnp.exp(router_logits), axis=1, keepdims=True)
    )
    rollout_logprob = rollout_logits - jnp.log(
        jnp.sum(jnp.exp(rollout_logits), axis=1, keepdims=True)
    )
    router_kl = jnp.sum(jnp.exp(rollout_logprob) * (rollout_logprob - current_logprob), axis=1)
    expert_ids = jnp.arange(experts_total, dtype=jnp.int32)
    picked = routes[:, :, None] == expert_ids[None, None, :]
    chosen_logits = jnp.sum(jnp.where(picked, router_logits[:, None, :], 0.0), axis=2)
    gate_raw = jnp.exp(chosen_logits)
    gates = (gate_raw / jnp.sum(gate_raw, axis=1, keepdims=True)).astype(jnp.bfloat16)
    capacity = min(token_rows, max(2, 3 * token_rows * top_count // (2 * experts_total)))
    per_column = experts_total // exp_count
    slots_total = experts_total * capacity
    flat_routes = routes.reshape(-1)
    member = (flat_routes[:, None] == expert_ids[None, :]).astype(jnp.int32)
    earlier = jnp.cumsum(member, axis=0) - member
    slot_rank = jnp.sum(earlier * member, axis=1)
    target = (
        flat_routes % per_column * exp_count + flat_routes // per_column
    ) * capacity + slot_rank
    target_grid = target.reshape(token_rows, top_count)
    slot_ids = jnp.arange(slots_total, dtype=jnp.int32)
    placing = jnp.any(target_grid[None, :, :] == slot_ids[:, None, None], axis=2).astype(
        jnp.bfloat16
    )
    gate_grid = jnp.where(
        target_grid[:, :, None] == slot_ids[None, None, :], gates[:, :, None], jnp.bfloat16(0)
    )
    combining = jnp.sum(gate_grid.astype(jnp.float32), axis=1).astype(jnp.bfloat16)
    weight_in = expert_in[0, 0]
    weight_out = expert_out[0, 0]
    packed = jnp.dot(placing, moe_in, preferred_element_type=jnp.float32).astype(jnp.bfloat16)
    packed = packed.reshape(per_column, 1, exp_count, capacity, width)
    doubled = jnp.broadcast_to(packed, (per_column, 2, exp_count, capacity, width)).reshape(
        ctx_count, exp_count, capacity, width
    )
    arrived = lax.all_to_all(
        lax.all_to_all(doubled, "ctx", split_axis=0, concat_axis=0, tiled=True),
        "exp",
        split_axis=1,
        concat_axis=1,
        tiled=True,
    )
    act = jnp.dot(arrived.reshape(-1, width), weight_in, preferred_element_type=jnp.float32)
    partial_value = jnp.dot(activate(act), weight_out, preferred_element_type=jnp.float32).astype(
        jnp.bfloat16
    )
    returned = lax.all_to_all(
        lax.all_to_all(
            partial_value.reshape(ctx_count, exp_count, capacity, width),
            "ctx",
            split_axis=0,
            concat_axis=0,
            tiled=True,
        ),
        "exp",
        split_axis=1,
        concat_axis=1,
        tiled=True,
    )
    paired = returned.reshape(per_column, 2, exp_count * capacity, width).astype(jnp.float32)
    expert_output = (paired[:, 0] + paired[:, 1]).astype(jnp.bfloat16).reshape(slots_total, width)
    moe_out = jnp.dot(combining, expert_output, preferred_element_type=jnp.float32)
    layer_out = (attended.astype(jnp.float32) + moe_out).astype(jnp.bfloat16)
    return (layer_out, router_kl)


def swapped(value, axis, mask):
    count = lax.axis_size(axis)
    return lax.ppermute(value, axis, [(source, source ^ mask) for source in range(count)])


def column_of(row):
    count = row.shape[1]
    along = lax.broadcasted_iota(jnp.int32, (count, count), 0)
    across = lax.broadcasted_iota(jnp.int32, (count, count), 1)
    return jnp.sum(jnp.where(along == across, row, 0.0), axis=1, keepdims=True)


def turned(vectors, cosine, sine):
    wide = vectors.astype(jnp.float32)
    wide = wide * lax.rsqrt(jnp.mean(wide * wide, axis=1, keepdims=True) + eps)
    return (wide * cosine + pltpu.roll(wide, wide.shape[1] // 2, 1) * sine).astype(jnp.bfloat16)


def rotation_kernel(share, index_ref, pos_ref, q_ref, own_ref, query_ref, key_ref, cos_ref, sin_ref):
    block, size = q_ref.shape
    group = pl.ds(pl.multiple_of(index_ref[0] // share * size, size), size)
    pos_row = pos_ref[...].astype(jnp.float32)
    pos_col = column_of(pos_row)
    first = lax.broadcasted_iota(jnp.int32, (1, block), 1) == 0
    opening = jnp.sum(jnp.where(first, pos_row, 0.0), axis=1, keepdims=True)
    earlier = opening - block + lax.broadcasted_iota(jnp.int32, (block, 1), 0).astype(jnp.float32)
    lane = lax.broadcasted_iota(jnp.int32, (1, size), 1)
    lower = lane < size // 2
    phase = jnp.where(lower, 0.0, math.pi / 2)
    turn_of = jnp.where(lower, lane, lane - size // 2).astype(jnp.float32)
    spectrum = jnp.exp(turn_of * (-2.0 * math.log(theta) / size))

    def table(at):
        turn = jnp.cos(at * spectrum - phase)
        swap = pltpu.roll(turn, size // 2, 1)
        return jnp.where(lower, turn, swap), jnp.where(lower, -swap, turn)

    cosine, sine = table(pos_col)
    query_ref[...] = turned(q_ref[...], cosine, sine)
    key_ref[...] = turned(own_ref[:, group], cosine, sine)
    cos_ref[...], sin_ref[...] = table(earlier)


def attention_kernel(share, order, weight_ready, index_ref, pos_ref, query_ref, key_ref, cos_ref, sin_ref, before_ref, own_ref, *refs):
    weight_ref, outputs, mixed = refs[0], refs[1:-1], refs[-1]
    block, size = query_ref.shape
    rows = block // len(order)
    pos_col = column_of(pos_ref[...].astype(jnp.float32))
    query_at = lax.broadcasted_iota(jnp.int32, (block, 2 * block), 0)
    key_at = lax.broadcasted_iota(jnp.int32, (block, 2 * block), 1) - block
    allowed = (key_at <= query_at) & (key_at >= query_at - pos_col.astype(jnp.int32))
    keys = jnp.concatenate(
        [turned(before_ref[:, :size], cos_ref[...], sin_ref[...]), key_ref[...]], axis=0
    )
    group = pl.ds(pl.multiple_of(index_ref[0] // share * size, size), size)
    values = jnp.concatenate([before_ref[:, size:], own_ref[:, group]], axis=0)
    scores = lax.dot_general(
        query_ref[...], keys, (((1,), (1,)), ((), ())), preferred_element_type=jnp.float32
    ) * (1.0 / math.sqrt(size))
    raw = jnp.where(allowed, jnp.exp(scores), 0.0)
    weights = (raw / jnp.sum(raw, axis=1, keepdims=True)).astype(jnp.bfloat16)
    mixed[...] = jnp.dot(weights, values, preferred_element_type=jnp.float32).astype(jnp.bfloat16)
    picked = [
        mixed[pl.ds(pl.multiple_of((index_ref[0] ^ owner) * rows, 16), rows), :] for owner in order
    ]
    weight_ready()
    term = jnp.dot(
        jnp.concatenate(picked, axis=0), weight_ref[...], preferred_element_type=jnp.float32
    ).astype(jnp.bfloat16)
    for i, output in enumerate(outputs):
        output[...] = term[i * rows : (i + 1) * rows]


def router_kernel(heads, index_ref, *refs):
    terms, refs = refs[:heads], refs[heads:]
    hidden_ref, gain_ref, router_ref, routes_ref, rollout_ref = refs[:5]
    attended_ref, payload_ref, kl_ref = refs[5:]
    width = hidden_ref.shape[1]
    experts, rows = rollout_ref.shape
    total = sum(term[...].astype(jnp.float32) for term in terms) + hidden_ref[...].astype(jnp.float32)
    attended = total.astype(jnp.bfloat16)
    attended_ref[...] = attended
    wide = attended.astype(jnp.float32)
    moe_in = (
        wide * lax.rsqrt(jnp.mean(wide * wide, axis=1, keepdims=True) + eps) * gain_ref[...]
    ).astype(jnp.bfloat16)
    payload_ref[:, :width] = moe_in
    logits = lax.dot_general(
        router_ref[...], moe_in, (((1,), (1,)), ((), ())), preferred_element_type=jnp.float32
    )
    raised = jnp.exp(logits)
    rollout = rollout_ref[...]
    current_log = logits - jnp.log(jnp.sum(raised, axis=0, keepdims=True))
    rollout_log = rollout - jnp.log(jnp.sum(jnp.exp(rollout), axis=0, keepdims=True))
    kl_ref[...] = jnp.sum(jnp.exp(rollout_log) * (rollout_log - current_log), axis=0, keepdims=True)
    ids = lax.broadcasted_iota(jnp.int32, (experts, rows), 0)
    picked = jnp.zeros((experts, rows), jnp.float32)
    for k in range(routes_ref.shape[0]):
        picked = picked + jnp.where(routes_ref[k : k + 1, :] == ids, 1.0, 0.0)
    chosen = jnp.where(picked > 0.0, raised, 0.0)
    gates = (chosen / jnp.sum(chosen, axis=0, keepdims=True)).astype(jnp.bfloat16)
    lanes = payload_ref.shape[1] - width
    spread = (
        lax.broadcasted_iota(jnp.int32, (experts, lanes), 0)
        == lax.broadcasted_iota(jnp.int32, (experts, lanes), 1)
    ).astype(jnp.float32).astype(jnp.bfloat16)
    payload_ref[:, width:] = lax.dot_general(
        gates, spread, (((0,), (0,)), ((), ())), preferred_element_type=jnp.float32
    ).astype(jnp.bfloat16)


VMEM = pl.BlockSpec(memory_space=pltpu.VMEM)
SMEM = pl.BlockSpec(memory_space=pltpu.SMEM)


HBM = pl.BlockSpec(memory_space=pltpu.HBM)
GRANT = 60 * 1024 * 1024
LEAN_GRANT = 24 * 1024 * 1024


def fetching(kernel, count, stored, late, index_ref, *refs):
    inputs, refs = refs[:count], refs[count:]
    outputs, refs = refs[: len(stored)], refs[len(stored) :]
    held, refs = refs[:count], refs[count:]
    sent, refs = refs[: sum(stored)], refs[sum(stored) :]
    arrived, left, scratch = refs[0], refs[1], refs[2:]
    copies = [
        pltpu.make_async_copy(source, target, arrived.at[i])
        for i, (source, target) in enumerate(zip(inputs, held))
    ]
    for copy in copies:
        copy.start()
    for copy in copies[: count - late]:
        copy.wait()
    awaited = [copy.wait for copy in copies[count - late :]]
    sent = iter(sent)
    built, copies = [], []
    for output, far in zip(outputs, stored):
        built.append(next(sent) if far else output)
        if far:
            copies.append(pltpu.make_async_copy(built[-1], output, left.at[len(copies)]))
    kernel(*awaited, index_ref, *held, *built, *scratch)
    for copy in copies:
        copy.start()
    for copy in copies:
        copy.wait()


def small_kernel(kernel, out_shape, inputs, stored, scratch=(), moved=0, late=0):
    held = [pltpu.VMEM(array.shape, array.dtype) for array in inputs[1:]]
    sent = [pltpu.VMEM(leaf.shape, leaf.dtype) for leaf, far in zip(out_shape, stored) if far]
    return pl.pallas_call(
        functools.partial(fetching, kernel, len(held), stored, late),
        out_shape=out_shape,
        in_specs=[SMEM] + [HBM] * len(held),
        out_specs=tuple(HBM if far else VMEM for far in stored),
        scratch_shapes=[
            *held,
            *sent,
            pltpu.SemaphoreType.DMA((len(held),)),
            pltpu.SemaphoreType.DMA((max(1, len(sent)),)),
            *scratch,
        ],
        compiler_params=pltpu.CompilerParams(vmem_limit_bytes=GRANT),
        cost_estimate=pl.CostEstimate(flops=0, bytes_accessed=moved, transcendentals=0),
    )(*inputs)


def fetched(sources, targets, arrived):
    copies = [
        pltpu.make_async_copy(source, target, arrived.at[i])
        for i, (source, target) in enumerate(zip(sources, targets))
    ]
    for copy in copies:
        copy.start()
    return copies


def hidden_kernel(width, *refs):
    parts = len(refs) - 8
    sources, refs = refs[: parts + 2], refs[parts + 2 :]
    inner_ref, spare_ref, own, other, tokens, arrived = refs
    rows = sources[2].shape[0]
    targets = [own, other] + [tokens.at[pl.ds(p * rows, rows), :] for p in range(parts)]
    copies = fetched(sources, targets, arrived)
    for copy in copies[:1] + copies[2:]:
        copy.wait()
    half = own.shape[1] // 2
    inner_ref[:, :half] = activate(
        jnp.dot(tokens[:, :width], own[...], preferred_element_type=jnp.float32)
    )
    spare_ref[...] = tokens[:, width:]
    copies[1].wait()
    inner_ref[:, half:] = activate(
        jnp.dot(tokens[:, :width], other[...], preferred_element_type=jnp.float32)
    )


def hidden_blocks(tokens, own_in, other_in):
    width, inner = own_in.shape
    rows, total = tokens[0].shape
    parts = len(tokens)
    return pl.pallas_call(
        functools.partial(hidden_kernel, width),
        out_shape=(
            jax.ShapeDtypeStruct((parts * rows, inner), jnp.bfloat16),
            jax.ShapeDtypeStruct((parts * rows, total - width), jnp.bfloat16),
        ),
        in_specs=[pl.BlockSpec(memory_space=pl.ANY)] * (parts + 2),
        out_specs=(VMEM, VMEM),
        scratch_shapes=[
            pltpu.VMEM(own_in.shape, own_in.dtype),
            pltpu.VMEM(own_in.shape, own_in.dtype),
            pltpu.VMEM((parts * rows, total), jnp.bfloat16),
            pltpu.SemaphoreType.DMA((parts + 2,)),
        ],
        compiler_params=pltpu.CompilerParams(vmem_limit_bytes=LEAN_GRANT),
        cost_estimate=pl.CostEstimate(flops=0, bytes_accessed=9 << 20, transcendentals=0),
    )(own_in, other_in, *tokens)


def output_kernel(index_ref, inner_ref, spare_ref, own_ref, other_ref, *refs):
    outputs, (inner, spare, weight, arrived) = refs[:-4], refs[-4:]
    depth = own_ref.shape[0]
    targets = [weight.at[pl.ds(0, depth), :], weight.at[pl.ds(depth, depth), :], inner, spare]
    for copy in fetched([own_ref, other_ref, inner_ref, spare_ref], targets, arrived):
        copy.wait()
    part = outputs[0].shape[0]
    step = 4 * part
    for start in reversed(range(0, inner.shape[0], step)):
        block = slice(start, start + step)
        chosen = spare[block, :].astype(jnp.float32)
        picked = lax.broadcasted_iota(jnp.int32, chosen.shape, 1) == index_ref[0]
        gate = jnp.sum(jnp.where(picked, chosen, 0.0), axis=1, keepdims=True)
        out = jnp.dot(inner[block, :], weight[...], preferred_element_type=jnp.float32)
        out = (out * gate).astype(jnp.bfloat16)
        for i in range(start // part, (start + step) // part):
            outputs[i][...] = out[i * part - start : (i + 1) * part - start]


def output_blocks(count, index, inner, spare, own_out, other_out):
    width = own_out.shape[1]
    rows = inner.shape[0]
    half = jax.ShapeDtypeStruct((rows // count // 2, width), jnp.bfloat16)
    flat = pl.pallas_call(
        output_kernel,
        out_shape=(half,) * (2 * count),
        in_specs=[SMEM] + [pl.BlockSpec(memory_space=pl.ANY)] * 4,
        out_specs=(VMEM,) * (2 * count),
        scratch_shapes=[
            pltpu.VMEM(inner.shape, inner.dtype),
            pltpu.VMEM(spare.shape, spare.dtype),
            pltpu.VMEM((inner.shape[1], width), jnp.bfloat16),
            pltpu.SemaphoreType.DMA((4,)),
        ],
        compiler_params=pltpu.CompilerParams(vmem_limit_bytes=LEAN_GRANT),
        cost_estimate=pl.CostEstimate(flops=0, bytes_accessed=0, transcendentals=0),
    )(index, inner, spare, own_out, other_out)
    return [flat[2 * k : 2 * k + 2] for k in range(count)]


def dense_body(
    hidden,
    queries,
    keys,
    values,
    positions,
    out_weight,
    ffn_gain,
    router_weight,
    routes,
    expert_in,
    expert_out,
    rollout_logits,
):
    block_rows = queries.shape[0]
    head_dim = queries.shape[1]
    width = hidden.shape[1]
    token_rows = hidden.shape[0]
    experts_total = router_weight.shape[1]
    ctx_index = lax.axis_index("ctx")
    exp_index = lax.axis_index("exp")
    exp_count = lax.axis_size("exp")
    kv_heads = keys.shape[1] // head_dim
    per_column = experts_total // exp_count
    share = exp_count // kv_heads
    bits = []
    step = exp_count // 2
    while step:
        bits.append(step)
        step //= 2

    weight_in = expert_in[0, 0]
    weight_out = expert_out[0, 0]
    kv_group = exp_index // share
    kv_own = jnp.concatenate(
        [lax.dynamic_slice_in_dim(array, kv_group * head_dim, head_dim, 1) for array in (keys, values)],
        axis=1,
    )
    before = passed_along(kv_own, "ctx", 1)
    before, weight_in_sent, weight_out_sent = lax.optimization_barrier((before, weight_in, weight_out))
    other_out = swapped(weight_out_sent, "ctx", 1)
    other_in = swapped(weight_in_sent, "ctx", 1)

    index = exp_index.reshape(1).astype(jnp.int32)
    owners = [0]
    for bit in bits:
        owners = owners + [owner ^ bit for owner in owners]
    turned_head = jax.ShapeDtypeStruct((block_rows, head_dim), jnp.bfloat16)
    table = jax.ShapeDtypeStruct((block_rows, head_dim), jnp.float32)
    rotated = small_kernel(
        functools.partial(rotation_kernel, share),
        (turned_head, turned_head, table, table),
        (index, positions[None, :], queries, keys),
        (True,) * 4,
        moved=20 << 20,
    )
    term = jax.ShapeDtypeStruct((token_rows, width), jnp.bfloat16)
    terms = small_kernel(
        functools.partial(attention_kernel, share, tuple(owners)),
        (term,) * exp_count,
        (index, positions[None, :], *rotated, before, values, out_weight),
        (True,) * exp_count,
        (pltpu.VMEM((block_rows, head_dim), jnp.bfloat16),),
        late=1,
    )
    terms = [terms[0]] + [swapped(term, "exp", owner) for term, owner in zip(terms[1:], owners[1:])]
    lanes = -(-experts_total // 128) * 128
    attended, payload, router_kl = small_kernel(
        functools.partial(router_kernel, exp_count),
        (
            jax.ShapeDtypeStruct((token_rows, width), jnp.bfloat16),
            jax.ShapeDtypeStruct((token_rows, width + lanes), jnp.bfloat16),
            jax.ShapeDtypeStruct((1, token_rows), jnp.float32),
        ),
        (
            index,
            *terms,
            hidden,
            ffn_gain[None, :],
            router_weight.T,
            routes.T,
            rollout_logits.T,
        ),
        (False, True, False),
    )
    router_kl = router_kl[0]
    crossed, passed = {}, None
    for k in sorted(range(per_column), key=lambda k: (k.bit_count(), -k)):
        low = k & -k
        if k != low:
            crossed[k] = [swapped(part, "ctx", 2 * low) for part in crossed[k ^ low]]
            continue
        parts = [payload if k == 0 else swapped(payload, "ctx", 2 * k)]
        for bit in bits[:-1]:
            if k > 0:
                passed, *parts = lax.optimization_barrier((passed, *parts))
            parts = parts + [swapped(part, "exp", bit) for part in parts]
        passed = parts[-1]
        crossed[k] = parts
    crossed = [crossed[k] for k in range(per_column)]
    expert_index = (exp_index * per_column + ctx_index // 2).reshape(1).astype(jnp.int32)
    groups, pairs, tokens = 1, [], []
    for turn, parts in enumerate(crossed):
        stack = jnp.concatenate(parts, axis=0)
        if turn == per_column // 2:
            stack, other_in = lax.optimization_barrier((stack, other_in))
        tokens = tokens + [stack, swapped(stack, "exp", bits[-1])]
        if (turn + 1) % (per_column // groups) == 0:
            pairs.append(hidden_blocks(tokens, weight_in, other_in))
            tokens = []
    inner, spare = pairs[0]
    inner, other_out = lax.optimization_barrier((inner, other_out))
    partials = output_blocks(per_column, expert_index, inner, spare, weight_out, other_out)
    returned, arrived = {}, []
    for k in sorted(range(per_column), key=lambda k: -k):
        keep, send = partials[k]
        for bit in reversed(bits):
            if bit == bits[0] and k < 2 and per_column > 2:
                returned[per_column - 1], send = lax.optimization_barrier((returned[per_column - 1], send))
            received = swapped(send, "exp", bit)
            total = keep.astype(jnp.float32) + received.astype(jnp.float32)
            total = total.astype(jnp.bfloat16)
            middle = total.shape[0] // 2
            keep, send = total[:middle], total[middle:]
        returned[k] = total
    step = 1
    while step < per_column:
        for k in reversed(range(0, per_column, step)):
            if k & step:
                came = swapped(returned[k], "ctx", 2 * step).astype(jnp.float32)
                if k == step:
                    arrived.append(came)
                else:
                    returned[k ^ step] = (returned[k ^ step].astype(jnp.float32) + came).astype(jnp.bfloat16)
        step *= 2
    moe_out = returned[0].astype(jnp.float32) + sum(arrived)
    layer_out = (attended.astype(jnp.float32) + moe_out).astype(jnp.bfloat16)
    return (layer_out, router_kl)


def powers_of_two(*counts):
    return all(count & (count - 1) == 0 for count in counts)


def body(*arrays):
    experts_total = arrays[7].shape[1]
    exp_count, ctx_count = lax.axis_size("exp"), lax.axis_size("ctx")
    dense = experts_total <= 2 * arrays[8].shape[1] and powers_of_two(exp_count, ctx_count)
    return (dense_body if dense else sparse_body)(*arrays)


def solution(mesh):
    return jax.shard_map(
        body,
        mesh=mesh,
        in_specs=(
            P(("group", "ctx", "exp"), None),
            P(("group", "ctx"), "exp"),
            P(("group", "ctx"), None),
            P(("group", "ctx"), None),
            P(("group", "ctx")),
            P("exp", None),
            P(),
            P(),
            P(("group", "ctx", "exp"), None),
            P("ctx", "exp", None, None),
            P("ctx", "exp", None, None),
            P(("group", "ctx", "exp"), None),
        ),
        out_specs=(P(("group", "ctx", "exp"), None), P(("group", "ctx", "exp"))),
        check_vma=False,
    )
```
